32 devices in a mesh: job: 2 (over x), tok: 16 (over z, y, core).
Axes of the slice: x: 2, y: 2, z: 4, core: 2. Of those that a mesh axis runs over, the one named last changes fastest.
Arguments:
- pair_states: bfloat16 [1024, 512, 128], P(('job', 'tok')), parts along dimension 0, may hold values from -6 to 6
- weight_in: bfloat16 [128, 1024], replicated, may hold values from -0.5 to 0.5
- weight_out: bfloat16 [512, 128], replicated, may hold values from -0.25 to 0.25
- weight_bias: bfloat16 [2, 128, 16], replicated, may hold values from -0.5 to 0.5
- key_mask: int32 [1024], P('job'), parts along dimension 0, may hold values 0 or 1
- noise_level: int32 [4], P('job'), parts along dimension 0, may hold values from 0 to 199
- query_states: bfloat16 [2, 16, 4, 48, 512], P(None, 'tok', 'job'), parts along dimension 2, may hold values from -16 to 16
- key_states: bfloat16 [2, 16, 4, 48, 512], P(None, 'tok', 'job'), parts along dimension 2, may hold values from -16 to 16
- value_states: bfloat16 [2, 16, 4, 48, 512], P(None, 'tok', 'job'), parts along dimension 2, may hold values from -6 to 6
- output_grad: bfloat16 [2, 16, 4, 48, 512], P(None, 'tok', 'job'), parts along dimension 2, may hold values from -6 to 6
Outputs:
- pair_grad: bfloat16 [1024, 512, 128], P(('job', 'tok')), parts along dimension 0
- query_grad: bfloat16 [2, 16, 4, 48, 512], P(None, 'tok', 'job'), parts along dimension 2
- key_grad: bfloat16 [2, 16, 4, 48, 512], P(None, 'tok', 'job'), parts along dimension 2
- value_grad: bfloat16 [2, 16, 4, 48, 512], P(None, 'tok', 'job'), parts along dimension 2
- weight_in_grad: float32 [256, 1024], P('job'), parts along dimension 0
- weight_out_grad: float32 [1024, 128], P('job'), parts along dimension 0
- weight_bias_grad: float32 [4, 128, 16], P('job'), parts along dimension 0
The draws below stay inside these ranges and needn't reach their ends.
There are 2 independent parts, one for each index of `job`. The reference program is written for one: setup_inputs(seed, part) draws one part's arguments, and reference() takes and returns one part's arrays. A program takes and returns all parts, laid end to end along the dimension named above; an argument that names none is the same for every part. Nothing has to cross between parts.
All inputs are finite; a program needn't handle non-finite values.
Results may differ from the reference program's by a relative error of at most 0.015.
Values may be sent and summed in bfloat16 or wider, within the bound.
No kernel may reach another device: no remote copies, remote signals or barrier semaphores. Data moves between devices by JAX's collectives and lax.ppermute only.
A program may use at most 192 MiB of HBM per device.

```python
import math
import jax
import jax.numpy as jnp
from jax import lax

CZ = 128
FF = 512
H = 16
DH = 48
N = 512
BLOCKS = 2
LEVELS = 200
S_DEV = 2
GH = 16
SAMPLES = 2


def query_key(key):
    base = jax.random.fold_in(key, 4099)
    seed_query, seed_key = jax.random.split(base, 2)
    shape = (BLOCKS, GH, S_DEV, DH, N)
    query_draw = jnp.clip(jax.random.normal(seed_query, shape, jnp.float32), -6.0, 6.0)
    key_draw = jnp.clip(jax.random.normal(seed_key, shape, jnp.float32), -6.0, 6.0)
    return (query_draw, key_draw)


def draw_query_states(key, part):
    return query_key(key)[0].astype(jnp.bfloat16)


def draw_key_states(key, part):
    return query_key(key)[1].astype(jnp.bfloat16)


def with_ends(values, stream_key, least, high):
    place = [jax.random.randint(jax.random.fold_in(stream_key, axis), (), 0, length) for axis, length in enumerate(values.shape)]
    main_axis = values.shape.index(max(values.shape))
    next_to = place[:main_axis] + [(place[main_axis] + 1) % values.shape[main_axis]] + place[main_axis + 1:]
    return values.at[tuple(place)].set(least).at[tuple(next_to)].set(high)


def steps_of(own_key, shape, cuts, least, largest):
    level = 1.0
    for dim, blocks in cuts:
        heights = jax.random.uniform(jax.random.fold_in(jax.random.fold_in(own_key, 6), dim), (blocks,), jnp.float32, least / len(cuts), largest / len(cuts))
        level = level * jnp.repeat(jnp.exp(heights), shape[dim] // blocks).reshape((-1,) + (1,) * (len(shape) - 1 - dim))
    return level


def gaussian(key, dims, deviation, bound, cuts=(), kind=jnp.bfloat16):
    drawn = jax.random.normal(key, dims, jnp.float32) * deviation
    if len(cuts) > 0:
        drawn = steps_of(key, dims, cuts, -0.22, 0.18) * drawn
    return jnp.clip(drawn, min=-bound, max=bound).astype(kind)


def setup_inputs(seed: int = 0, part: int = 0) -> dict:
    splits = jax.random.split(jax.random.key(seed), 11)
    part_keys = jax.random.split(jax.random.fold_in(splits[10], part), 11)
    return {
        "pair_states": gaussian(part_keys[0], (N, N, CZ), 1.0, 6.0, ((0, 16),)),
        "weight_in": gaussian(splits[1], (CZ, 2 * FF), CZ ** -0.5, 0.5),
        "weight_out": gaussian(splits[2], (FF, CZ), FF ** -0.5, 0.25),
        "weight_bias": gaussian(splits[3], (BLOCKS, CZ, H), CZ ** -0.5, 0.5),
        "key_mask": with_ends((jax.random.randint(part_keys[4], (N,), 0, 8) < 7).astype(jnp.int32), jax.random.fold_in(part_keys[4], 1), 0, 1),
        "noise_level": jax.random.randint(part_keys[5], (SAMPLES,), 0, LEVELS).astype(jnp.int32),
        "query_states": draw_query_states(jax.random.fold_in(jax.random.fold_in(splits[10], part), 71), part),
        "key_states": draw_key_states(jax.random.fold_in(jax.random.fold_in(splits[10], part), 71), part),
        "value_states": gaussian(part_keys[8], (BLOCKS, GH, S_DEV, DH, N), 1.0, 6.0, ((1, 16),)),
        "output_grad": gaussian(part_keys[9], (BLOCKS, GH, S_DEV, DH, N), 1.0, 6.0, ((1, 16),)),
    }


sigma_high = 160.0
sigma_low = 0.0004
sigma_data = 16.0
rho_power = 7.0
epsilon = 1e-05
masked_score = -1000000000.0

def sample_weight(levels):
    level = levels.astype(jnp.float32)
    top_root = sigma_high ** (1.0 / rho_power)
    low_root = sigma_low ** (1.0 / rho_power)
    sigma_level = (top_root + level / (LEVELS - 1) * (low_root - top_root)) ** rho_power
    return (sigma_level * sigma_level + sigma_data * sigma_data) / (sigma_level + sigma_data) ** 2

def normalize(inputs):
    row_mean = lax.optimization_barrier(jnp.mean(inputs, -1, keepdims=True))
    centered = inputs - row_mean
    variance = lax.optimization_barrier(jnp.mean(centered * centered, -1, keepdims=True))
    inv_std = lax.rsqrt(variance + epsilon)
    return (centered * inv_std, inv_std)

def norm_back(inputs, upstream):
    normed, inv_std = normalize(inputs)
    return inv_std * (upstream - lax.optimization_barrier(jnp.mean(upstream, -1, keepdims=True)) - normed * lax.optimization_barrier(jnp.mean(upstream * normed, -1, keepdims=True)))

def tile_forward(flattened, weight_in, weight_out):
    hidden_width = weight_out.shape[0]
    pair_float = flattened.astype(jnp.float32)
    normed_in = normalize(pair_float)[0].astype(jnp.bfloat16)
    projected = jnp.dot(normed_in, weight_in, preferred_element_type=jnp.float32)
    gate_in = projected[:, :hidden_width]
    up_in = projected[:, hidden_width:]
    hidden = (jax.nn.silu(gate_in) * up_in).astype(jnp.bfloat16)
    lifted = pair_float + jnp.dot(hidden, weight_out, preferred_element_type=jnp.float32)
    normed_out = normalize(lifted)[0].astype(jnp.bfloat16)
    return (pair_float, normed_in, gate_in, up_in, hidden, lifted, normed_out)

def tile_backward(stored, bias_half, weight_in, weight_out, weight_bias):
    pair_float, normed_in, gate_in, up_in, hidden, lifted, normed_out = stored
    bias_float = bias_half.astype(jnp.float32)
    d_normed = jnp.einsum('bhp,bch->pc', bias_float, weight_bias.astype(jnp.float32))
    grad_bias = jnp.einsum('pc,bhp->bch', normed_out.astype(jnp.float32), bias_float)
    d_lifted = norm_back(lifted, d_normed)
    lifted_half = d_lifted.astype(jnp.bfloat16)
    grad_out = jnp.einsum('pf,pc->fc', hidden.astype(jnp.float32), lifted_half.astype(jnp.float32))
    d_hidden = jnp.dot(lifted_half, weight_out.T, preferred_element_type=jnp.float32)
    gate_sigmoid = jax.nn.sigmoid(gate_in)
    d_gate = d_hidden * up_in * gate_sigmoid * (1.0 + gate_in * (1.0 - gate_sigmoid))
    d_up = d_hidden * gate_in * gate_sigmoid
    d_projected = jnp.concatenate([d_gate, d_up], -1).astype(jnp.bfloat16)
    grad_in = jnp.einsum('pc,pf->cf', normed_in.astype(jnp.float32), d_projected.astype(jnp.float32))
    d_normed_in = jnp.dot(d_projected, weight_in.T, preferred_element_type=jnp.float32)
    pair_grad = (d_lifted + norm_back(pair_float, d_normed_in)).astype(jnp.bfloat16)
    return (pair_grad, grad_in, grad_out, grad_bias)

def sample_back(query_vec, key_vec, value_vec, upstream, bias_float, key_valid, weight):
    scaling = 1.0 / math.sqrt(query_vec.shape[0])
    raw_scores = jnp.einsum('di,dj->ij', query_vec.astype(jnp.float32), key_vec.astype(jnp.float32)) * scaling + bias_float
    raw_scores = jnp.where(key_valid[None, :], raw_scores, masked_score)
    row_peak = lax.optimization_barrier(jnp.max(raw_scores, -1, keepdims=True))
    exp_scores = jnp.exp(raw_scores - row_peak)
    attention = exp_scores / lax.optimization_barrier(jnp.sum(exp_scores, -1, keepdims=True))
    attention_half = attention.astype(jnp.bfloat16)
    grad_half = (weight * upstream.astype(jnp.float32)).astype(jnp.bfloat16)
    d_attention = jnp.einsum('di,dj->ij', grad_half.astype(jnp.float32), value_vec.astype(jnp.float32))
    d_scores = attention * (d_attention - lax.optimization_barrier(jnp.sum(attention * d_attention, -1, keepdims=True)))
    scores_half = d_scores.astype(jnp.bfloat16)
    d_value = jnp.einsum('ij,di->dj', attention_half.astype(jnp.float32), grad_half.astype(jnp.float32)).astype(jnp.bfloat16)
    d_query = (jnp.einsum('ij,dj->di', scores_half.astype(jnp.float32), key_vec.astype(jnp.float32)) * scaling).astype(jnp.bfloat16)
    d_key = (jnp.einsum('ij,di->dj', scores_half.astype(jnp.float32), query_vec.astype(jnp.float32)) * scaling).astype(jnp.bfloat16)
    return (d_query, d_key, d_value, d_scores)

def attend_block(queries, keys_in, values_in, grads_in, bias_float, key_valid, weights):

    def advance(summed, items):
        query_vec, key_vec, value_vec, upstream, weight = items
        d_query, d_key, d_value, d_scores = sample_back(query_vec, key_vec, value_vec, upstream, bias_float, key_valid, weight)
        return (summed + d_scores, (d_query, d_key, d_value))
    start = jnp.zeros((queries.shape[2], queries.shape[2]), jnp.float32)
    return lax.scan(advance, start, (queries, keys_in, values_in, grads_in, weights))

def reference(pair_states, weight_in, weight_out, weight_bias, key_mask, noise_level, query_states, key_states, value_states, output_grad):
    row_block = N // 16
    rows_all = pair_states.reshape(16, row_block * N, CZ)

    def forward_rows(flattened):
        normed_out = tile_forward(flattened, weight_in, weight_out)[6]
        return jnp.einsum('pc,bch->bhp', normed_out.astype(jnp.float32), weight_bias.astype(jnp.float32)).astype(jnp.bfloat16)
    biases = lax.map(forward_rows, rows_all)
    biases = jnp.transpose(biases, (1, 2, 0, 3)).reshape(BLOCKS, H, N, N)
    key_valid = key_mask > 0
    weights_all = sample_weight(noise_level)
    slots = query_states.shape[1]

    def per_slot(flat_index):
        layer = flat_index // slots
        slot = flat_index % slots
        bias_float = biases[layer, slot % H].astype(jnp.float32)
        weights = lax.dynamic_slice_in_dim(weights_all, slot // H * S_DEV, S_DEV)
        return attend_block(query_states[layer, slot], key_states[layer, slot], value_states[layer, slot], output_grad[layer, slot], bias_float, key_valid, weights)
    summed, (d_query, d_key, d_value) = lax.map(per_slot, jnp.arange(BLOCKS * slots, dtype=jnp.int32))
    bias_grad = lax.optimization_barrier(jnp.sum(summed.reshape(BLOCKS, slots // H, H, N, N), 1))
    bias_half = bias_grad.astype(jnp.bfloat16)
    bias_rows = jnp.transpose(bias_half.reshape(BLOCKS, H, 16, row_block * N), (2, 0, 1, 3))

    def backward_rows(carry, items):
        flattened, bias_piece = items
        stored = tile_forward(flattened, weight_in, weight_out)
        pair_grad, grad_in, grad_out, grad_bias = tile_backward(stored, bias_piece, weight_in, weight_out, weight_bias)
        return ((carry[0] + grad_in, carry[1] + grad_out, carry[2] + grad_bias), pair_grad)
    start = (jnp.zeros((CZ, 2 * FF), jnp.float32), jnp.zeros((FF, CZ), jnp.float32), jnp.zeros((BLOCKS, CZ, H), jnp.float32))
    (grad_in, grad_out, grad_bias), pair_rows = lax.scan(backward_rows, start, (rows_all, bias_rows))
    pair_grad = pair_rows.reshape(N, N, CZ)
    shape = (BLOCKS, slots, S_DEV, DH, N)
    return (pair_grad, d_query.reshape(shape), d_key.reshape(shape), d_value.reshape(shape), grad_in, grad_out, grad_bias)
```

```python
import functools
import math

import jax
import jax.numpy as jnp
from jax import lax
from jax.experimental import pallas as pl
from jax.experimental.pallas import tpu as pltpu
from jax.sharding import PartitionSpec as P

LEVELS = 200
CHUNKS = 1


sigma_high = 160.0
sigma_low = 0.0004
sigma_data = 16.0
rho_power = 7.0
epsilon = 1e-05
masked_score = -1000000000.0

F32 = jnp.float32
BF16 = jnp.bfloat16


def sample_weight(levels):
    level = levels.astype(jnp.float32)
    top_root = sigma_high ** (1.0 / rho_power)
    low_root = sigma_low ** (1.0 / rho_power)
    sigma_level = (top_root + level / (LEVELS - 1) * (low_root - top_root)) ** rho_power
    return (sigma_level * sigma_level + sigma_data * sigma_data) / (sigma_level + sigma_data) ** 2


def mm(left, right, left_dim=1, right_dim=0):
    return lax.dot_general(
        left, right, (((left_dim,), (right_dim,)), ((), ())), preferred_element_type=F32
    )


def normalize(inputs):
    centered = inputs - jnp.mean(inputs, -1, keepdims=True)
    inv_std = lax.rsqrt(jnp.mean(centered * centered, -1, keepdims=True) + epsilon)
    return centered * inv_std, inv_std


def norm_back(normed, inv_std, upstream):
    return inv_std * (
        upstream
        - jnp.mean(upstream, -1, keepdims=True)
        - normed * jnp.mean(upstream * normed, -1, keepdims=True)
    )


def split_width(width):
    return 256 if width % 256 == 0 else width


def forward_kernel(pair_ref, w_in_ref, w_out_ref, w_bias_ref, bias_ref):
    width = w_out_ref.shape[0]
    piece = split_width(width)

    def one_row(row, carry):
        pair_float = pair_ref[row].astype(F32)
        normed_in = normalize(pair_float)[0].astype(BF16)
        lifted = pair_float
        for at in range(0, width, piece):
            half_gate = mm(normed_in, w_in_ref[:, at : at + piece])
            up_in = mm(normed_in, w_in_ref[:, width + at : width + at + piece])
            hidden = (half_gate * (1.0 + jnp.tanh(half_gate)) * up_in).astype(BF16)
            lifted = lifted + mm(hidden, w_out_ref[at : at + piece, :])
        normed_out = normalize(lifted)[0].astype(BF16)
        bias_ref[row] = mm(w_bias_ref[...], normed_out, 1, 1).astype(BF16)
        return carry

    lax.fori_loop(0, pair_ref.shape[0], one_row, 0)


def forward_rows(chunk, rows, pair, w_in_half, w_out, w_bias):
    crop, channels = pair.shape[1:]
    lanes = w_bias.shape[0]
    step = math.gcd(rows, 4)
    steps = rows // step
    positions = rows * crop
    width = w_out.shape[0]
    whole = lambda i: (0, 0)
    return pl.pallas_call(
        forward_kernel,
        grid=(steps,),
        in_specs=[
            pl.BlockSpec((step, crop, channels), lambda i: (chunk * steps + i, 0, 0)),
            pl.BlockSpec(w_in_half.shape, whole),
            pl.BlockSpec(w_out.shape, whole),
            pl.BlockSpec(w_bias.shape, whole),
        ],
        out_specs=pl.BlockSpec((step, lanes, crop), lambda i: (i, 0, 0)),
        out_shape=jax.ShapeDtypeStruct((rows, lanes, crop), BF16),
        compiler_params=pltpu.CompilerParams(vmem_limit_bytes=40 * 2**20),
        cost_estimate=pl.CostEstimate(
            flops=2 * positions * channels * (3 * width + lanes),
            bytes_accessed=positions * (channels + lanes) * 2,
            transcendentals=positions * width,
        ),
        name="pair_forward",
    )(pair, w_in_half, w_out, w_bias)


def backward_kernel(
    first,
    last,
    pair_ref,
    d_bias_ref,
    w_in_ref,
    w_out_ref,
    w_bias_ref,
    w_in_t_ref,
    w_out_t_ref,
    *refs,
):
    if first:
        pair_grad_ref, sums_ref, bias_sums_ref = refs[:3]
    else:
        before_ref, bias_before_ref, _, pair_grad_ref, sums_ref, bias_sums_ref = refs[:6]
    width = w_out_ref.shape[0]
    channels = w_out_ref.shape[1]
    piece = split_width(width)

    @pl.when(pl.program_id(0) == 0)
    def _():
        if first:
            sums_ref[...] = jnp.zeros_like(sums_ref)
            bias_sums_ref[...] = jnp.zeros_like(bias_sums_ref)
        else:
            sums_ref[...] = before_ref[...]
            bias_sums_ref[...] = bias_before_ref[...]

    def one_row(row, carry):
        pair_float = pair_ref[row].astype(F32)
        normed_float, inv_in = normalize(pair_float)
        normed_in = normed_float.astype(BF16)
        lifted = pair_float
        kept = []
        for at in range(0, width, piece):
            half_gate = mm(normed_in, w_in_ref[:, at : at + piece])
            up_in = mm(normed_in, w_in_ref[:, width + at : width + at + piece])
            one_plus = 1.0 + jnp.tanh(half_gate)
            silu = half_gate * one_plus
            hidden = (silu * up_in).astype(BF16)
            slope = one_plus * (1.0 + half_gate * (2.0 - one_plus)) * up_in
            kept.append((silu, slope, hidden))
            lifted = lifted + mm(hidden, w_out_ref[at : at + piece, :])
        out_float, inv_out = normalize(lifted)
        normed_out = out_float.astype(BF16)
        d_bias = d_bias_ref[row]
        bias_sums_ref[...] += mm(d_bias, normed_out)
        d_normed = mm(d_bias, w_bias_ref[...], 0, 0)
        d_lifted = norm_back(out_float, inv_out, d_normed)
        lifted_half = d_lifted.astype(BF16)
        lifted_t = lifted_half.T
        normed_t = normed_in.T
        d_normed_in = jnp.zeros_like(pair_float)
        for index, (silu, slope, hidden) in enumerate(kept):
            at = index * piece
            cols = slice(at, at + piece)
            up_cols = slice(width + at, width + at + piece)
            out_cols = slice(2 * width + at, 2 * width + at + piece)
            sums_ref[:, out_cols] += mm(lifted_t, hidden)
            d_hidden = mm(lifted_half, w_out_t_ref[:, cols])
            d_gate = (0.5 * d_hidden * slope).astype(BF16)
            d_up = (d_hidden * silu).astype(BF16)
            sums_ref[:, cols] += mm(normed_t, d_gate)
            sums_ref[:, up_cols] += mm(normed_t, d_up)
            d_normed_in = d_normed_in + mm(d_gate, w_in_t_ref[cols, :])
            d_normed_in = d_normed_in + mm(d_up, w_in_t_ref[up_cols, :])
        pair_grad_ref[row] = (
            d_lifted + norm_back(normed_float, inv_in, d_normed_in)
        ).astype(BF16)
        return carry

    lax.fori_loop(0, pair_ref.shape[0], one_row, 0)

    if last:
        packed_ref = refs[-1]

        @pl.when(pl.program_id(0) == pl.num_programs(0) - 1)
        def _():
            done = 3 * width
            lanes = bias_sums_ref.shape[0]
            packed_ref[:, :done] = sums_ref[...].astype(BF16)
            padded = jnp.concatenate(
                [bias_sums_ref[...], jnp.zeros((channels - lanes, channels), F32)], 0
            )
            packed_ref[:, done:] = padded.T.astype(BF16)


def backward_rows(chunk, chunks, rows, pair, d_bias, weights, state):
    w_in_half, w_out, w_bias, w_in_t, w_out_t = weights
    crop, channels = pair.shape[1:]
    lanes = w_bias.shape[0]
    width = w_out.shape[0]
    step = math.gcd(rows, 4)
    steps = rows // step
    positions = rows * crop
    first, last = chunk == 0, chunk == chunks - 1
    whole = lambda i: (0, 0)
    pair_spec = pl.BlockSpec((step, crop, channels), lambda i: (chunk * steps + i, 0, 0))
    in_specs = [pair_spec, pl.BlockSpec((step, lanes, crop), lambda i: (i, 0, 0))]
    in_specs += [pl.BlockSpec(w.shape, whole) for w in weights]
    operands = [pair, d_bias, *weights]
    aliases = {}
    if not first:
        pair_grad, sums, bias_sums = state
        operands += [sums, bias_sums, pair_grad]
        in_specs += [pl.BlockSpec(sums.shape, whole), pl.BlockSpec(bias_sums.shape, whole)]
        in_specs += [pl.BlockSpec(memory_space=pl.ANY)]
        aliases = {len(operands) - 1: 0}
    shapes = [
        jax.ShapeDtypeStruct(pair.shape, BF16),
        jax.ShapeDtypeStruct((channels, 3 * width), F32),
        jax.ShapeDtypeStruct((lanes, channels), F32),
    ]
    out_specs = [pair_spec, pl.BlockSpec(shapes[1].shape, whole), pl.BlockSpec(shapes[2].shape, whole)]
    if last:
        shapes.append(jax.ShapeDtypeStruct((channels, 3 * width + channels), BF16))
        out_specs.append(pl.BlockSpec(shapes[3].shape, whole))
    return pl.pallas_call(
        functools.partial(backward_kernel, first, last),
        grid=(steps,),
        in_specs=in_specs,
        out_specs=out_specs,
        out_shape=shapes,
        input_output_aliases=aliases,
        compiler_params=pltpu.CompilerParams(vmem_limit_bytes=48 * 2**20),
        cost_estimate=pl.CostEstimate(
            flops=2 * positions * channels * (9 * width + 2 * lanes),
            bytes_accessed=positions * (2 * channels + lanes) * 2,
            transcendentals=positions * width,
        ),
        name="pair_backward",
    )(*operands)


def attend_kernel(
    first, last, weight_ref, bias_ref, valid_ref, q_ref, k_ref, v_ref, g_ref, *refs
):
    if first:
        dq_ref, dk_ref, dv_ref, d_bias_ref = refs
    else:
        dk_before_ref, dv_before_ref, dq_ref, dk_ref, dv_ref, d_bias_ref = refs
    samples, depth = q_ref.shape[1:3]
    sources, _, rows, crop = bias_ref.shape
    scaling = 1.0 / math.sqrt(depth)
    bias = bias_ref[:, 0].astype(F32).reshape(sources * rows, crop)
    valid = valid_ref[...] > 0
    total = jnp.zeros_like(bias)
    for s in range(samples):
        query, key, value = q_ref[0, s], k_ref[0, s], v_ref[0, s]
        grad_half = (weight_ref[s] * g_ref[0, s].astype(F32)).astype(BF16)
        scores = mm(query, key, 0, 0) * scaling + bias
        scores = jnp.where(valid, scores, masked_score)
        exp_scores = jnp.exp(scores - jnp.max(scores, -1, keepdims=True))
        attention = exp_scores / jnp.sum(exp_scores, -1, keepdims=True)
        d_attention = mm(grad_half, value, 0, 0)
        d_scores = attention * (
            d_attention - jnp.sum(attention * d_attention, -1, keepdims=True)
        )
        total = total + d_scores
        scores_half = d_scores.astype(BF16)
        d_value = mm(grad_half, attention.astype(BF16))
        d_key = mm(query, scores_half)
        dq_ref[0, s] = (mm(key, scores_half, 1, 1) * scaling).astype(BF16)
        if not first:
            d_value = d_value + dv_before_ref[0, s]
            d_key = d_key + dk_before_ref[0, s]
        if last:
            d_key = d_key * scaling
        dv_ref[0, s] = d_value.astype(dv_ref.dtype)
        dk_ref[0, s] = d_key.astype(dk_ref.dtype)
    d_bias_ref[:, 0] = total.astype(BF16).reshape(sources, rows, crop)


def attend_rows(chunk, chunks, weights, bias, valid, query, key, value, grad, state):
    sources, layers, rows, crop = bias.shape
    samples, depth, row_count = query.shape[1:]
    first, last = chunk == 0, chunk == chunks - 1
    vec = lambda shape: pl.BlockSpec((1,) + shape[1:], lambda l: (l, 0, 0, 0))
    plane = pl.BlockSpec((sources, 1, rows, crop), lambda l: (0, l, 0, 0))
    in_specs = [
        pl.BlockSpec(memory_space=pltpu.SMEM),
        plane,
        pl.BlockSpec(valid.shape, lambda l: (0, 0)),
        vec(query.shape),
        vec(key.shape),
        vec(value.shape),
        vec(grad.shape),
    ]
    operands = [weights, bias, valid, query, key, value, grad]
    if not first:
        operands += list(state)
        in_specs += [vec(key.shape), vec(value.shape)]
    kind = BF16 if last else F32
    return pl.pallas_call(
        functools.partial(attend_kernel, first, last),
        grid=(layers,),
        in_specs=in_specs,
        out_specs=[vec(query.shape), vec(key.shape), vec(value.shape), plane],
        out_shape=[
            jax.ShapeDtypeStruct(query.shape, BF16),
            jax.ShapeDtypeStruct(key.shape, kind),
            jax.ShapeDtypeStruct(value.shape, kind),
            jax.ShapeDtypeStruct(bias.shape, BF16),
        ],
        compiler_params=pltpu.CompilerParams(vmem_limit_bytes=48 * 2**20),
        cost_estimate=pl.CostEstimate(
            flops=10 * layers * samples * depth * row_count * crop,
            bytes_accessed=layers * crop * (4 * row_count + 12 * samples * depth),
            transcendentals=layers * samples * row_count * crop,
        ),
        name="attention_backward",
    )(*operands)


def swap(array):
    return lax.all_to_all(array, "tok", split_axis=0, concat_axis=0, tiled=True)


def body(
    pair_states,
    weight_in,
    weight_out,
    weight_bias,
    key_mask,
    noise_level,
    query_states,
    key_states,
    value_states,
    output_grad,
):
    row_count, crop, channels = pair_states.shape
    layers, _, heads = weight_bias.shape
    width = weight_out.shape[0]
    devices = lax.axis_size("tok")
    groups = devices // heads
    samples, depth = query_states.shape[2:4]
    chunks = CHUNKS
    rows = row_count // chunks
    lanes = heads * layers

    halves = jnp.concatenate([jnp.full((width,), 0.5, BF16), jnp.ones((width,), BF16)])
    w_in_half = weight_in * halves[None, :]
    w_bias = jnp.transpose(weight_bias, (2, 0, 1)).reshape(lanes, channels)
    pair_weights = (w_in_half, weight_out, w_bias, weight_in.T, weight_out.T)

    group = lax.axis_index("tok") // heads
    weights = sample_weight(lax.dynamic_slice_in_dim(noise_level, group * samples, samples))
    valid = key_mask[None, :]

    def by_chunk(array):
        cut = array[:, 0].reshape(layers, samples, depth, devices, chunks, rows)
        cut = jnp.transpose(cut, (4, 0, 1, 2, 3, 5))
        return cut.reshape(chunks, layers, samples, depth, devices * rows)

    queries, grads = by_chunk(query_states), by_chunk(output_grad)

    arrived = []
    for chunk in range(chunks):
        bias = forward_rows(chunk, rows, pair_states, w_in_half, weight_out, w_bias)
        bias = jnp.transpose(bias, (1, 0, 2)).reshape(heads, layers, rows, crop)
        arrived.append(swap(jnp.tile(bias, (groups, 1, 1, 1))))

    returned = []
    d_queries = []
    state = None
    for chunk in range(chunks):
        bias = arrived[chunk]
        flat = rows % 16 != 0
        if flat:
            bias = jnp.transpose(bias, (1, 0, 2, 3)).reshape(1, layers, devices * rows, crop)
        d_query, d_key, d_value, d_bias = attend_rows(
            chunk,
            chunks,
            weights,
            bias,
            valid,
            queries[chunk],
            key_states[:, 0],
            value_states[:, 0],
            grads[chunk],
            state,
        )
        state = (d_key, d_value)
        d_queries.append(d_query)
        if flat:
            d_bias = jnp.transpose(d_bias.reshape(layers, devices, rows, crop), (1, 0, 2, 3))
        returned.append(swap(d_bias))

    pair_state = None
    for chunk in range(chunks):
        d_bias = returned[chunk]
        if groups > 1:
            d_bias = d_bias.reshape(groups, heads, layers, rows, crop).astype(F32)
            d_bias = jnp.sum(d_bias, 0).astype(BF16)
        d_bias = jnp.transpose(d_bias.reshape(lanes, rows, crop), (1, 0, 2))
        pair_state = backward_rows(
            chunk, chunks, rows, pair_states, d_bias, pair_weights, pair_state and pair_state[:3]
        )
    pair_grad, _, _, packed = pair_state

    share = channels // devices
    parts = swap(packed.reshape(devices, share, packed.shape[1]))
    summed = jnp.sum(parts.astype(F32), 0).astype(BF16)
    summed = lax.all_gather(summed, "tok", axis=0, tiled=True).astype(F32)
    grad_in = summed[:, : 2 * width]
    grad_out = summed[:, 2 * width : 3 * width].T
    grad_bias = summed[:, 3 * width : 3 * width + lanes].reshape(channels, heads, layers)
    grad_bias = jnp.transpose(grad_bias, (2, 0, 1))

    d_query = jnp.stack(d_queries, 0).reshape(chunks, layers, samples, depth, devices, rows)
    d_query = jnp.transpose(d_query, (1, 2, 3, 4, 0, 5)).reshape(query_states.shape)
    return (
        pair_grad,
        d_query,
        d_key[:, None],
        d_value[:, None],
        grad_in,
        grad_out,
        grad_bias,
    )


def solution(mesh):
    in_specs = (
        P(("job", "tok"), None, None),
        P(),
        P(),
        P(),
        P("job"),
        P("job"),
        P(None, "tok", "job", None, None),
        P(None, "tok", "job", None, None),
        P(None, "tok", "job", None, None),
        P(None, "tok", "job", None, None),
    )
    out_specs = (
        P(("job", "tok"), None, None),
        P(None, "tok", "job", None, None),
        P(None, "tok", "job", None, None),
        P(None, "tok", "job", None, None),
        P("job", None),
        P("job", None),
        P("job", None, None),
    )
    return jax.shard_map(body, mesh=mesh, in_specs=in_specs, out_specs=out_specs, check_vma=False)
```

```python
import functools
import math

import jax
import jax.numpy as jnp
from jax import lax
from jax.experimental import pallas as pl
from jax.experimental.pallas import tpu as pltpu
from jax.sharding import PartitionSpec as P

LEVELS = 200
CHUNKS = 2


sigma_high = 160.0
sigma_low = 0.0004
sigma_data = 16.0
rho_power = 7.0
epsilon = 1e-05
masked_score = -1000000000.0

F32 = jnp.float32
BF16 = jnp.bfloat16


def sample_weight(levels):
    level = levels.astype(jnp.float32)
    top_root = sigma_high ** (1.0 / rho_power)
    low_root = sigma_low ** (1.0 / rho_power)
    sigma_level = (top_root + level / (LEVELS - 1) * (low_root - top_root)) ** rho_power
    return (sigma_level * sigma_level + sigma_data * sigma_data) / (sigma_level + sigma_data) ** 2


def mm(left, right, left_dim=1, right_dim=0):
    return lax.dot_general(
        left, right, (((left_dim,), (right_dim,)), ((), ())), preferred_element_type=F32
    )


def normalize(inputs):
    centered = inputs - jnp.mean(inputs, 0, keepdims=True)
    inv_std = lax.rsqrt(jnp.mean(centered * centered, 0, keepdims=True) + epsilon)
    return centered * inv_std, inv_std


def norm_back(normed, inv_std, upstream):
    return inv_std * (
        upstream
        - jnp.mean(upstream, 0, keepdims=True)
        - normed * jnp.mean(upstream * normed, 0, keepdims=True)
    )


def split_width(width):
    return 256 if width % 256 == 0 else width


def interleave(make_stages, count, lag):
    rows = [make_stages(index) for index in range(count)]
    running = []
    clock = 0
    while rows or running:
        if rows and clock % lag == 0:
            running.append(rows.pop(0))
        running = [row for row in running if next(row, None) is not None]
        clock += 1


def for_rows(count, group, make_stages, lag):
    group = math.gcd(count, group)

    def step(at, carry):
        interleave(lambda index: make_stages(at * group + index), group, lag)
        return carry

    if count == group:
        step(0, 0)
    else:
        lax.fori_loop(0, count // group, step, 0)


def forward_kernel(pair_ref, w_in_t_ref, w_out_t_ref, w_bias_ref, bias_ref):
    width = w_out_t_ref.shape[1]
    piece = split_width(width)

    def stages(row):
        pair_float = pair_ref[row].T.astype(F32)
        normed_in = normalize(pair_float)[0].astype(BF16)
        yield True
        lifted = pair_float
        for at in range(0, width, piece):
            half_gate = mm(w_in_t_ref[at : at + piece, :], normed_in)
            up_in = mm(w_in_t_ref[width + at : width + at + piece, :], normed_in)
            yield True
            hidden = (half_gate * (1.0 + jnp.tanh(half_gate)) * up_in).astype(BF16)
            lifted = lifted + mm(w_out_t_ref[:, at : at + piece], hidden)
            yield True
        normed_out = normalize(lifted)[0].astype(BF16)
        yield True
        bias_ref[row] = mm(w_bias_ref[...], normed_out).astype(BF16)

    for_rows(pair_ref.shape[0], 4, stages, 2)


def forward_rows(chunk, rows, pair, w_in_half_t, w_out_t, w_bias):
    crop, channels = pair.shape[1:]
    lanes = w_bias.shape[0]
    step = math.gcd(rows, 8)
    steps = rows // step
    positions = rows * crop
    width = w_out_t.shape[1]
    whole = lambda i: (0, 0)
    return pl.pallas_call(
        forward_kernel,
        grid=(steps,),
        in_specs=[
            pl.BlockSpec((step, crop, channels), lambda i: (chunk * steps + i, 0, 0)),
            pl.BlockSpec(w_in_half_t.shape, whole),
            pl.BlockSpec(w_out_t.shape, whole),
            pl.BlockSpec(w_bias.shape, whole),
        ],
        out_specs=pl.BlockSpec((step, lanes, crop), lambda i: (i, 0, 0)),
        out_shape=jax.ShapeDtypeStruct((rows, lanes, crop), BF16),
        compiler_params=pltpu.CompilerParams(vmem_limit_bytes=48 * 2**20),
        cost_estimate=pl.CostEstimate(
            flops=2 * positions * channels * (3 * width + lanes),
            bytes_accessed=positions * (channels + lanes) * 2,
            transcendentals=positions * width,
        ),
        name="pair_forward",
    )(pair, w_in_half_t, w_out_t, w_bias)


def backward_kernel(
    first,
    last,
    pair_ref,
    d_bias_ref,
    w_in_t_ref,
    w_out_t_ref,
    w_bias_t_ref,
    w_in_ref,
    w_out_ref,
    *refs,
):
    if first:
        pair_grad_ref, sums_ref = refs[:2]
    else:
        before_ref, _, pair_grad_ref, sums_ref = refs[:4]
    width = w_out_ref.shape[0]
    piece = split_width(width)
    lanes = w_bias_t_ref.shape[1]

    @pl.when(pl.program_id(0) == 0)
    def _():
        if first:
            sums_ref[...] = jnp.zeros_like(sums_ref)
        else:
            sums_ref[...] = before_ref[...]

    def stages(row):
        pair_float = pair_ref[row].T.astype(F32)
        normed_float, inv_in = normalize(pair_float)
        normed_in = normed_float.astype(BF16)
        yield True
        lifted = pair_float
        kept = []
        for at in range(0, width, piece):
            half_gate = mm(w_in_t_ref[at : at + piece, :], normed_in)
            up_in = mm(w_in_t_ref[width + at : width + at + piece, :], normed_in)
            yield True
            one_plus = 1.0 + jnp.tanh(half_gate)
            silu = half_gate * one_plus
            hidden = (silu * up_in).astype(BF16)
            slope = one_plus * (1.0 + half_gate * (2.0 - one_plus)) * up_in
            kept.append((silu, slope, hidden))
            lifted = lifted + mm(w_out_t_ref[:, at : at + piece], hidden)
            yield True
        out_float, inv_out = normalize(lifted)
        normed_out = out_float.astype(BF16)
        yield True
        d_bias = d_bias_ref[row]
        d_normed = mm(w_bias_t_ref[...], d_bias)
        sums_ref[3 * width : 3 * width + lanes, :] += mm(d_bias, normed_out, 1, 1)
        d_lifted = norm_back(out_float, inv_out, d_normed)
        lifted_half = d_lifted.astype(BF16)
        yield True
        d_normed_in = jnp.zeros_like(pair_float)
        for index, (silu, slope, hidden) in enumerate(kept):
            at = index * piece
            cols = slice(at, at + piece)
            up_cols = slice(width + at, width + at + piece)
            out_cols = slice(2 * width + at, 2 * width + at + piece)
            d_hidden = mm(w_out_ref[cols, :], lifted_half)
            sums_ref[out_cols, :] += mm(hidden, lifted_half, 1, 1)
            yield True
            d_gate = (0.5 * d_hidden * slope).astype(BF16)
            d_up = (d_hidden * silu).astype(BF16)
            d_normed_in = d_normed_in + mm(w_in_ref[:, cols], d_gate)
            sums_ref[cols, :] += mm(d_gate, normed_in, 1, 1)
            d_normed_in = d_normed_in + mm(w_in_ref[:, up_cols], d_up)
            sums_ref[up_cols, :] += mm(d_up, normed_in, 1, 1)
            yield True
        pair_grad = d_lifted + norm_back(normed_float, inv_in, d_normed_in)
        pair_grad_ref[row] = pair_grad.astype(BF16).T

    for_rows(pair_ref.shape[0], 4, stages, 3)

    if last:
        packed_ref = refs[-1]

        @pl.when(pl.program_id(0) == pl.num_programs(0) - 1)
        def _():
            done = sums_ref.shape[0]
            packed_ref[:done, :] = sums_ref[...].astype(BF16)
            packed_ref[done:, :] = jnp.zeros((packed_ref.shape[0] - done, packed_ref.shape[1]), BF16)


def backward_rows(chunk, chunks, rows, packed_rows, pair, d_bias, weights, state):
    w_in_half_t, w_out_t, w_bias_t, w_in, w_out = weights
    crop, channels = pair.shape[1:]
    lanes = w_bias_t.shape[1]
    width = w_out.shape[0]
    step = math.gcd(rows, 8)
    steps = rows // step
    positions = rows * crop
    first, last = chunk == 0, chunk == chunks - 1
    whole = lambda i: (0, 0)
    pair_spec = pl.BlockSpec((step, crop, channels), lambda i: (chunk * steps + i, 0, 0))
    in_specs = [pair_spec, pl.BlockSpec((step, lanes, crop), lambda i: (i, 0, 0))]
    in_specs += [pl.BlockSpec(w.shape, whole) for w in weights]
    operands = [pair, d_bias, *weights]
    aliases = {}
    if not first:
        pair_grad, sums = state
        operands += [sums, pair_grad]
        in_specs += [pl.BlockSpec(sums.shape, whole), pl.BlockSpec(memory_space=pl.ANY)]
        aliases = {len(operands) - 1: 0}
    shapes = [
        jax.ShapeDtypeStruct(pair.shape, BF16),
        jax.ShapeDtypeStruct((3 * width + lanes, channels), F32),
    ]
    out_specs = [pair_spec, pl.BlockSpec(shapes[1].shape, whole)]
    if last:
        shapes.append(jax.ShapeDtypeStruct((packed_rows, channels), BF16))
        out_specs.append(pl.BlockSpec(shapes[2].shape, whole))
    return pl.pallas_call(
        functools.partial(backward_kernel, first, last),
        grid=(steps,),
        in_specs=in_specs,
        out_specs=out_specs,
        out_shape=shapes,
        input_output_aliases=aliases,
        compiler_params=pltpu.CompilerParams(vmem_limit_bytes=56 * 2**20),
        cost_estimate=pl.CostEstimate(
            flops=2 * positions * channels * (9 * width + 2 * lanes),
            bytes_accessed=positions * (2 * channels + lanes) * 2,
            transcendentals=positions * width,
        ),
        name="pair_backward",
    )(*operands)


def attend_kernel(
    first, last, weight_ref, bias_ref, valid_ref, q_ref, k_ref, v_ref, g_ref, *refs
):
    if first:
        dq_ref, dk_ref, dv_ref, d_bias_ref = refs
    else:
        dk_before_ref, dv_before_ref, dq_ref, dk_ref, dv_ref, d_bias_ref = refs
    samples, depth = q_ref.shape[1:3]
    sources, _, rows, crop = bias_ref.shape
    scaling = 1.0 / math.sqrt(depth)
    bias = bias_ref[:, 0].astype(F32).reshape(sources * rows, crop)
    valid = valid_ref[...] > 0
    total = jnp.zeros_like(bias)
    for s in range(samples):
        query, key, value = q_ref[0, s], k_ref[0, s], v_ref[0, s]
        grad_half = (weight_ref[s] * g_ref[0, s].astype(F32)).astype(BF16)
        scores = mm(query, key, 0, 0) * scaling + bias
        scores = jnp.where(valid, scores, masked_score)
        exp_scores = jnp.exp(scores - jnp.max(scores, -1, keepdims=True))
        attention = exp_scores / jnp.sum(exp_scores, -1, keepdims=True)
        d_attention = mm(grad_half, value, 0, 0)
        d_scores = attention * (
            d_attention - jnp.sum(attention * d_attention, -1, keepdims=True)
        )
        total = total + d_scores
        scores_half = d_scores.astype(BF16)
        d_value = mm(grad_half, attention.astype(BF16))
        d_key = mm(query, scores_half)
        dq_ref[0, s] = (mm(key, scores_half, 1, 1) * scaling).astype(BF16)
        if not first:
            d_value = d_value + dv_before_ref[0, s]
            d_key = d_key + dk_before_ref[0, s]
        if last:
            d_key = d_key * scaling
        dv_ref[0, s] = d_value.astype(dv_ref.dtype)
        dk_ref[0, s] = d_key.astype(dk_ref.dtype)
    d_bias_ref[:, 0] = total.astype(BF16).reshape(sources, rows, crop)


def attend_rows(chunk, chunks, weights, bias, valid, query, key, value, grad, state):
    sources, layers, rows, crop = bias.shape
    samples, depth, row_count = query.shape[1:]
    first, last = chunk == 0, chunk == chunks - 1
    vec = lambda shape: pl.BlockSpec((1,) + shape[1:], lambda l: (l, 0, 0, 0))
    plane = pl.BlockSpec((sources, 1, rows, crop), lambda l: (0, l, 0, 0))
    in_specs = [
        pl.BlockSpec(memory_space=pltpu.SMEM),
        plane,
        pl.BlockSpec(valid.shape, lambda l: (0, 0)),
        vec(query.shape),
        vec(key.shape),
        vec(value.shape),
        vec(grad.shape),
    ]
    operands = [weights, bias, valid, query, key, value, grad]
    if not first:
        operands += list(state)
        in_specs += [vec(key.shape), vec(value.shape)]
    kind = BF16 if last else F32
    return pl.pallas_call(
        functools.partial(attend_kernel, first, last),
        grid=(layers,),
        in_specs=in_specs,
        out_specs=[vec(query.shape), vec(key.shape), vec(value.shape), plane],
        out_shape=[
            jax.ShapeDtypeStruct(query.shape, BF16),
            jax.ShapeDtypeStruct(key.shape, kind),
            jax.ShapeDtypeStruct(value.shape, kind),
            jax.ShapeDtypeStruct(bias.shape, BF16),
        ],
        compiler_params=pltpu.CompilerParams(vmem_limit_bytes=48 * 2**20),
        cost_estimate=pl.CostEstimate(
            flops=10 * layers * samples * depth * row_count * crop,
            bytes_accessed=layers * crop * (4 * row_count + 12 * samples * depth),
            transcendentals=layers * samples * row_count * crop,
        ),
        name="attention_backward",
    )(*operands)


def swap(array):
    return lax.all_to_all(array, "tok", split_axis=0, concat_axis=0, tiled=True)


def body(
    pair_states,
    weight_in,
    weight_out,
    weight_bias,
    key_mask,
    noise_level,
    query_states,
    key_states,
    value_states,
    output_grad,
):
    row_count, crop, channels = pair_states.shape
    layers, _, heads = weight_bias.shape
    width = weight_out.shape[0]
    devices = lax.axis_size("tok")
    groups = devices // heads
    samples, depth = query_states.shape[2:4]
    chunks = CHUNKS
    rows = row_count // chunks
    lanes = heads * layers

    halves = jnp.concatenate([jnp.full((width,), 0.5, BF16), jnp.ones((width,), BF16)])
    w_in_half_t = (weight_in * halves[None, :]).T
    w_out_t = weight_out.T
    w_bias = jnp.transpose(weight_bias, (2, 0, 1)).reshape(lanes, channels)
    pair_weights = (w_in_half_t, w_out_t, w_bias.T, weight_in, weight_out)

    group = lax.axis_index("tok") // heads
    weights = sample_weight(lax.dynamic_slice_in_dim(noise_level, group * samples, samples))
    valid = key_mask[None, :]

    def by_chunk(array):
        cut = array[:, 0].reshape(layers, samples, depth, devices, chunks, rows)
        cut = jnp.transpose(cut, (4, 0, 1, 2, 3, 5))
        return cut.reshape(chunks, layers, samples, depth, devices * rows)

    queries, grads = by_chunk(query_states), by_chunk(output_grad)

    arrived = []
    for chunk in range(chunks):
        bias = forward_rows(chunk, rows, pair_states, w_in_half_t, w_out_t, w_bias)
        bias = jnp.transpose(bias, (1, 0, 2)).reshape(heads, layers, rows, crop)
        arrived.append(swap(jnp.tile(bias, (groups, 1, 1, 1))))

    returned = []
    d_queries = []
    state = None
    for chunk in range(chunks):
        bias = arrived[chunk]
        flat = rows % 16 != 0
        if flat:
            bias = jnp.transpose(bias, (1, 0, 2, 3)).reshape(1, layers, devices * rows, crop)
        d_query, d_key, d_value, d_bias = attend_rows(
            chunk,
            chunks,
            weights,
            bias,
            valid,
            queries[chunk],
            key_states[:, 0],
            value_states[:, 0],
            grads[chunk],
            state,
        )
        state = (d_key, d_value)
        d_queries.append(d_query)
        if flat:
            d_bias = jnp.transpose(d_bias.reshape(layers, devices, rows, crop), (1, 0, 2, 3))
        returned.append(swap(d_bias))

    sum_rows = 3 * width + lanes
    share = 16 * -(-sum_rows // (16 * devices))
    pair_state = None
    for chunk in range(chunks):
        d_bias = returned[chunk]
        if groups > 1:
            d_bias = d_bias.reshape(groups, heads, layers, rows, crop).astype(F32)
            d_bias = jnp.sum(d_bias, 0).astype(BF16)
        d_bias = jnp.transpose(d_bias.reshape(lanes, rows, crop), (1, 0, 2))
        pair_state = backward_rows(
            chunk,
            chunks,
            rows,
            share * devices,
            pair_states,
            d_bias,
            pair_weights,
            pair_state and pair_state[:2],
        )
    pair_grad, _, packed = pair_state

    parts = swap(packed.reshape(devices, share, channels))
    summed = jnp.sum(parts.astype(F32), 0).astype(BF16)
    summed = lax.all_gather(summed, "tok", axis=0, tiled=True).astype(F32)
    grad_in = summed[: 2 * width].T
    grad_out = summed[2 * width : 3 * width]
    grad_bias = summed[3 * width : sum_rows].reshape(heads, layers, channels)
    grad_bias = jnp.transpose(grad_bias, (1, 2, 0))

    d_query = jnp.stack(d_queries, 0).reshape(chunks, layers, samples, depth, devices, rows)
    d_query = jnp.transpose(d_query, (1, 2, 3, 4, 0, 5)).reshape(query_states.shape)
    return (
        pair_grad,
        d_query,
        d_key[:, None],
        d_value[:, None],
        grad_in,
        grad_out,
        grad_bias,
    )


def solution(mesh):
    in_specs = (
        P(("job", "tok"), None, None),
        P(),
        P(),
        P(),
        P("job"),
        P("job"),
        P(None, "tok", "job", None, None),
        P(None, "tok", "job", None, None),
        P(None, "tok", "job", None, None),
        P(None, "tok", "job", None, None),
    )
    out_specs = (
        P(("job", "tok"), None, None),
        P(None, "tok", "job", None, None),
        P(None, "tok", "job", None, None),
        P(None, "tok", "job", None, None),
        P("job", None),
        P("job", None),
        P("job", None, None),
    )
    return jax.shard_map(body, mesh=mesh, in_specs=in_specs, out_specs=out_specs, check_vma=False)
```

```python
import functools
import math

import jax
import jax.numpy as jnp
from jax import lax
from jax.experimental import pallas as pl
from jax.experimental.pallas import tpu as pltpu
from jax.sharding import PartitionSpec as P

LEVELS = 200
CHUNKS = 2


sigma_high = 160.0
sigma_low = 0.0004
sigma_data = 16.0
rho_power = 7.0
epsilon = 1e-05
masked_score = -1000000000.0

F32 = jnp.float32
BF16 = jnp.bfloat16


def sample_weight(levels):
    level = levels.astype(jnp.float32)
    top_root = sigma_high ** (1.0 / rho_power)
    low_root = sigma_low ** (1.0 / rho_power)
    sigma_level = (top_root + level / (LEVELS - 1) * (low_root - top_root)) ** rho_power
    return (sigma_level * sigma_level + sigma_data * sigma_data) / (sigma_level + sigma_data) ** 2


def mm(left, right, left_dim=1, right_dim=0):
    return lax.dot_general(
        left, right, (((left_dim,), (right_dim,)), ((), ())), preferred_element_type=F32
    )


def normalize(inputs):
    centered = inputs - jnp.mean(inputs, 0, keepdims=True)
    inv_std = lax.rsqrt(jnp.mean(centered * centered, 0, keepdims=True) + epsilon)
    return centered * inv_std, inv_std


def norm_back(normed, inv_std, upstream):
    return inv_std * (
        upstream
        - jnp.mean(upstream, 0, keepdims=True)
        - normed * jnp.mean(upstream * normed, 0, keepdims=True)
    )


def split_width(width):
    return 256 if width % 256 == 0 else width


def interleave(make_stages, count, lag):
    rows = [make_stages(index) for index in range(count)]
    running = []
    clock = 0
    while rows or running:
        if rows and clock % lag == 0:
            running.append(rows.pop(0))
        running = [row for row in running if next(row, None) is not None]
        clock += 1


def for_rows(count, group, make_stages, lag):
    group = math.gcd(count, group)

    def step(at, carry):
        interleave(lambda index: make_stages(at * group + index), group, lag)
        return carry

    if count == group:
        step(0, 0)
    else:
        lax.fori_loop(0, count // group, step, 0)


def forward_kernel(
    direct,
    pair_ref,
    w_in_ref,
    w_out_ref,
    w_bias_ref,
    bias_ref,
    kept_ref,
    normed_ref,
    inv_ref,
    w_in_t_ref,
    w_out_t_ref,
    w_lanes_ref,
    lines_ref,
):
    width = w_out_ref.shape[0]
    channels = w_out_ref.shape[1]
    layers, _, heads = w_bias_ref.shape
    piece = split_width(width)
    step = pair_ref.shape[0]
    first_row = pl.program_id(0) * step

    @pl.when(pl.program_id(0) == 0)
    def _():
        w_in_t = w_in_ref[...].T
        w_in_t_ref[:width, :] = w_in_t[:width] * 0.5
        w_in_t_ref[width:, :] = w_in_t[width:]
        w_out_t_ref[...] = w_out_ref[...].T
        for layer in range(layers):
            lanes = w_bias_ref[layer].astype(F32)
            w_lanes_ref[layer * heads : (layer + 1) * heads, :] = lanes.T.astype(BF16)

    def stages(row):
        pair_float = pair_ref[row].T.astype(F32)
        normed_float, inv_in = normalize(pair_float)
        normed_in = normed_float.astype(BF16)
        normed_ref[row, :channels, :] = normed_in
        yield True
        lifted = pair_float
        for at in range(0, width, piece):
            half_gate = mm(w_in_t_ref[at : at + piece, :], normed_in)
            up_in = mm(w_in_t_ref[width + at : width + at + piece, :], normed_in)
            yield True
            one_plus = 1.0 + jnp.tanh(half_gate)
            silu = half_gate * one_plus
            hidden = (silu * up_in).astype(BF16)
            slope = one_plus * (0.5 + half_gate * (1.0 - 0.5 * one_plus)) * up_in
            kept_ref[row, at : at + piece, :] = slope.astype(BF16)
            kept_ref[row, width + at : width + at + piece, :] = silu.astype(BF16)
            kept_ref[row, 2 * width + at : 2 * width + at + piece, :] = hidden
            lifted = lifted + mm(w_out_t_ref[:, at : at + piece], hidden)
            yield True
        out_float, inv_out = normalize(lifted)
        normed_out = out_float.astype(BF16)
        normed_ref[row, channels:, :] = normed_out
        inv_ref[row, 0:1, :] = inv_in
        inv_ref[row, 1:2, :] = inv_out
        yield True
        bias = mm(w_lanes_ref[...], normed_out)
        if direct:
            tiles, total, tile = lines_ref.shape
            rows = total // (layers * heads)
            for layer in range(layers):
                at = pl.ds(layer * rows + first_row + row, heads, stride=layers * rows)
                lines = bias[layer * heads : (layer + 1) * heads]
                for index in range(tiles):
                    lines_ref[index, at, :] = lines[:, index * tile : (index + 1) * tile]
        else:
            bias_ref[row] = bias.astype(BF16)

    for_rows(step, 4, stages, 2)

    if direct:

        @pl.when(pl.program_id(0) == pl.num_programs(0) - 1)
        def _():
            tiles, _, tile = lines_ref.shape
            for index in range(tiles):
                lines = lines_ref[index].reshape(bias_ref.shape[:2] + (tile,))
                bias_ref[:, :, index * tile : (index + 1) * tile] = lines.astype(BF16)


def forward_rows(chunk, rows, pair, w_in, w_out, w_bias):
    crop, channels = pair.shape[1:]
    layers, _, heads = w_bias.shape
    lanes = layers * heads
    step = math.gcd(rows, 4)
    steps = rows // step
    positions = rows * crop
    width = w_out.shape[0]
    direct = rows % 16 == 0 and crop % 128 == 0
    line_shape = (heads * layers, rows, crop) if direct else (rows, lanes, crop)
    line_spec = (
        pl.BlockSpec(line_shape, lambda i: (0, 0, 0))
        if direct
        else pl.BlockSpec((step, lanes, crop), lambda i: (i, 0, 0))
    )
    by_row = lambda height: pl.BlockSpec((step, height, crop), lambda i: (i, 0, 0))
    return pl.pallas_call(
        functools.partial(forward_kernel, direct),
        grid=(steps,),
        in_specs=[
            pl.BlockSpec((step, crop, channels), lambda i: (chunk * steps + i, 0, 0)),
            pl.BlockSpec(w_in.shape, lambda i: (0, 0)),
            pl.BlockSpec(w_out.shape, lambda i: (0, 0)),
            pl.BlockSpec(w_bias.shape, lambda i: (0, 0, 0)),
        ],
        out_specs=[line_spec, by_row(3 * width), by_row(2 * channels), by_row(2)],
        out_shape=[
            jax.ShapeDtypeStruct(line_shape, BF16),
            jax.ShapeDtypeStruct((rows, 3 * width, crop), BF16),
            jax.ShapeDtypeStruct((rows, 2 * channels, crop), BF16),
            jax.ShapeDtypeStruct((rows, 2, crop), F32),
        ],
        scratch_shapes=[
            pltpu.VMEM((2 * width, channels), BF16),
            pltpu.VMEM((channels, width), BF16),
            pltpu.VMEM((lanes, channels), BF16),
            pltpu.VMEM((crop // 128, lanes * rows, 128) if direct else (1, 8, 128), F32),
        ],
        compiler_params=pltpu.CompilerParams(vmem_limit_bytes=56 * 2**20),
        cost_estimate=pl.CostEstimate(
            flops=6 * positions * channels * (3 * width + lanes),
            bytes_accessed=positions * (3 * width + 3 * channels + lanes) * 2,
            transcendentals=positions * width,
        ),
        name="pair_forward",
    )(pair, w_in, w_out, w_bias)


def backward_kernel(
    first,
    last,
    direct,
    kept_ref,
    normed_ref,
    inv_ref,
    d_bias_ref,
    w_in_ref,
    w_out_ref,
    w_bias_ref,
    *refs,
):
    if first:
        pair_grad_ref, sums_ref = refs[:2]
    else:
        before_ref, _, pair_grad_ref, sums_ref = refs[:4]
    w_lanes_ref, lines_ref = refs[-2:]
    width, channels = w_out_ref.shape
    layers, _, heads = w_bias_ref.shape
    lanes = layers * heads
    step = kept_ref.shape[0]
    first_row = pl.program_id(0) * step

    @pl.when(pl.program_id(0) == 0)
    def _():
        if first:
            sums_ref[...] = jnp.zeros_like(sums_ref)
        else:
            sums_ref[...] = before_ref[...]
        for layer in range(layers):
            line = w_bias_ref[layer].astype(F32)
            w_lanes_ref[layer * heads : (layer + 1) * heads, :] = line.T.astype(BF16)
        if direct:
            tiles, total, tile = lines_ref.shape
            for index in range(tiles):
                lines = d_bias_ref[:, :, index * tile : (index + 1) * tile].astype(F32)
                lines_ref[index] = lines.reshape(total, tile)

    def stages(row):
        if direct:
            tiles, total, _ = lines_ref.shape
            rows = total // lanes
            lines = []
            for layer in range(layers):
                at = pl.ds(layer * rows + first_row + row, heads, stride=layers * rows)
                lines.append(
                    jnp.concatenate([lines_ref[index, at, :] for index in range(tiles)], 1)
                )
            d_bias = jnp.concatenate(lines, 0).astype(BF16)
        else:
            d_bias = d_bias_ref[row]
        normed_in = normed_ref[row, :channels, :]
        normed_out = normed_ref[row, channels:, :]
        inv_in, inv_out = inv_ref[row, 0:1, :], inv_ref[row, 1:2, :]
        d_normed = mm(w_lanes_ref[...], d_bias, 0, 0)
        sums_ref[3 * width :, :] += mm(d_bias, normed_out, 1, 1)
        yield True
        d_lifted = norm_back(normed_out.astype(F32), inv_out, d_normed)
        lifted_half = d_lifted.astype(BF16)
        yield True
        sums_ref[2 * width : 3 * width, :] += mm(kept_ref[row, 2 * width :, :], lifted_half, 1, 1)
        d_hidden = mm(w_out_ref[...], lifted_half)
        yield True
        d_gate = (d_hidden * kept_ref[row, :width, :].astype(F32)).astype(BF16)
        d_up = (d_hidden * kept_ref[row, width : 2 * width, :].astype(F32)).astype(BF16)
        d_projected = jnp.concatenate([d_gate, d_up], 0)
        yield True
        d_normed_in = mm(w_in_ref[...], d_projected)
        sums_ref[: 2 * width, :] += mm(d_projected, normed_in, 1, 1)
        yield True
        pair_grad = d_lifted + norm_back(normed_in.astype(F32), inv_in, d_normed_in)
        pair_grad_ref[row] = pair_grad.astype(BF16).T

    for_rows(step, 4, stages, 2)

    if last:
        packed_ref = refs[-3]

        @pl.when(pl.program_id(0) == pl.num_programs(0) - 1)
        def _():
            done = sums_ref.shape[0]
            packed_ref[:done, :] = sums_ref[...].astype(BF16)
            packed_ref[done:, :] = jnp.zeros((packed_ref.shape[0] - done, packed_ref.shape[1]), BF16)


def backward_rows(chunk, chunks, rows, packed_rows, shape, stored, d_bias, weights, state):
    w_in, w_out, w_bias = weights
    crop, channels = shape[1:]
    layers, _, heads = w_bias.shape
    lanes = layers * heads
    width = w_out.shape[0]
    step = math.gcd(rows, 4)
    steps = rows // step
    positions = rows * crop
    first, last = chunk == 0, chunk == chunks - 1
    direct = rows % 16 == 0 and crop % 128 == 0
    whole = lambda i: (0, 0)
    by_row = lambda height: pl.BlockSpec((step, height, crop), lambda i: (i, 0, 0))
    in_specs = [by_row(array.shape[1]) for array in stored]
    if direct:
        in_specs.append(pl.BlockSpec(d_bias.shape, lambda i: (0, 0, 0)))
    else:
        in_specs.append(by_row(lanes))
    in_specs += [
        pl.BlockSpec(w_in.shape, whole),
        pl.BlockSpec(w_out.shape, whole),
        pl.BlockSpec(w_bias.shape, lambda i: (0, 0, 0)),
    ]
    operands = [*stored, d_bias, *weights]
    aliases = {}
    if not first:
        pair_grad, sums = state
        operands += [sums, pair_grad]
        in_specs += [pl.BlockSpec(sums.shape, whole), pl.BlockSpec(memory_space=pl.ANY)]
        aliases = {len(operands) - 1: 0}
    shapes = [
        jax.ShapeDtypeStruct(shape, BF16),
        jax.ShapeDtypeStruct((3 * width + lanes, channels), F32),
    ]
    out_specs = [
        pl.BlockSpec((step, crop, channels), lambda i: (chunk * steps + i, 0, 0)),
        pl.BlockSpec(shapes[1].shape, whole),
    ]
    if last:
        shapes.append(jax.ShapeDtypeStruct((packed_rows, channels), BF16))
        out_specs.append(pl.BlockSpec(shapes[2].shape, whole))
    return pl.pallas_call(
        functools.partial(backward_kernel, first, last, direct),
        grid=(steps,),
        in_specs=in_specs,
        out_specs=out_specs,
        out_shape=shapes,
        input_output_aliases=aliases,
        scratch_shapes=[
            pltpu.VMEM((lanes, channels), BF16),
            pltpu.VMEM((crop // 128, lanes * rows, 128) if direct else (1, 8, 128), F32),
        ],
        compiler_params=pltpu.CompilerParams(vmem_limit_bytes=56 * 2**20),
        cost_estimate=pl.CostEstimate(
            flops=6 * positions * channels * (6 * width + 2 * lanes),
            bytes_accessed=positions * (3 * width + 3 * channels + lanes) * 2,
            transcendentals=0,
        ),
        name="pair_backward",
    )(*operands)


def attend_kernel(
    first, last, weight_ref, bias_ref, valid_ref, q_ref, k_ref, v_ref, g_ref, *refs
):
    if first:
        dq_ref, dk_ref, dv_ref, d_bias_ref = refs
    else:
        dk_before_ref, dv_before_ref, dq_ref, dk_ref, dv_ref, d_bias_ref = refs
    samples, depth = q_ref.shape[1:3]
    sources, _, rows, crop = bias_ref.shape
    scaling = 1.0 / math.sqrt(depth)
    bias = bias_ref[:, 0].astype(F32).reshape(sources * rows, crop)
    valid = valid_ref[...] > 0
    total = jnp.zeros_like(bias)
    for s in range(samples):
        query, key, value = q_ref[0, s], k_ref[0, s], v_ref[0, s]
        grad_half = (weight_ref[s] * g_ref[0, s].astype(F32)).astype(BF16)
        scores = mm(query, key, 0, 0) * scaling + bias
        scores = jnp.where(valid, scores, masked_score)
        exp_scores = jnp.exp(scores - jnp.max(scores, -1, keepdims=True))
        attention = exp_scores / jnp.sum(exp_scores, -1, keepdims=True)
        d_attention = mm(grad_half, value, 0, 0)
        d_scores = attention * (
            d_attention - jnp.sum(attention * d_attention, -1, keepdims=True)
        )
        total = total + d_scores
        scores_half = d_scores.astype(BF16)
        d_value = mm(grad_half, attention.astype(BF16))
        d_key = mm(query, scores_half)
        dq_ref[0, s] = (mm(key, scores_half, 1, 1) * scaling).astype(BF16)
        if not first:
            d_value = d_value + dv_before_ref[0, s]
            d_key = d_key + dk_before_ref[0, s]
        if last:
            d_key = d_key * scaling
        dv_ref[0, s] = d_value.astype(dv_ref.dtype)
        dk_ref[0, s] = d_key.astype(dk_ref.dtype)
    d_bias_ref[:, 0] = total.astype(BF16).reshape(sources, rows, crop)


def attend_rows(chunk, chunks, weights, bias, valid, query, key, value, grad, state):
    sources, layers, rows, crop = bias.shape
    samples, depth, row_count = query.shape[1:]
    first, last = chunk == 0, chunk == chunks - 1
    vec = lambda shape: pl.BlockSpec((1,) + shape[1:], lambda l: (l, 0, 0, 0))
    plane = pl.BlockSpec((sources, 1, rows, crop), lambda l: (0, l, 0, 0))
    in_specs = [
        pl.BlockSpec(memory_space=pltpu.SMEM),
        plane,
        pl.BlockSpec(valid.shape, lambda l: (0, 0)),
        vec(query.shape),
        vec(key.shape),
        vec(value.shape),
        vec(grad.shape),
    ]
    operands = [weights, bias, valid, query, key, value, grad]
    if not first:
        operands += list(state)
        in_specs += [vec(key.shape), vec(value.shape)]
    kind = BF16 if last else F32
    return pl.pallas_call(
        functools.partial(attend_kernel, first, last),
        grid=(layers,),
        in_specs=in_specs,
        out_specs=[vec(query.shape), vec(key.shape), vec(value.shape), plane],
        out_shape=[
            jax.ShapeDtypeStruct(query.shape, BF16),
            jax.ShapeDtypeStruct(key.shape, kind),
            jax.ShapeDtypeStruct(value.shape, kind),
            jax.ShapeDtypeStruct(bias.shape, BF16),
        ],
        compiler_params=pltpu.CompilerParams(vmem_limit_bytes=48 * 2**20),
        cost_estimate=pl.CostEstimate(
            flops=200 * layers * samples * depth * row_count * crop,
            bytes_accessed=layers * crop * (4 * row_count + 12 * samples * depth),
            transcendentals=layers * samples * row_count * crop,
        ),
        name="attention_backward",
    )(*operands)


def swap(array):
    return lax.all_to_all(array, "tok", split_axis=0, concat_axis=0, tiled=True)


def body(
    pair_states,
    weight_in,
    weight_out,
    weight_bias,
    key_mask,
    noise_level,
    query_states,
    key_states,
    value_states,
    output_grad,
):
    row_count, crop, channels = pair_states.shape
    layers, _, heads = weight_bias.shape
    width = weight_out.shape[0]
    devices = lax.axis_size("tok")
    groups = devices // heads
    samples, depth = query_states.shape[2:4]
    chunks = CHUNKS
    rows = row_count // chunks
    lanes = heads * layers

    pair_weights = (weight_in, weight_out, weight_bias)

    group = lax.axis_index("tok") // heads
    weights = sample_weight(lax.dynamic_slice_in_dim(noise_level, group * samples, samples))
    valid = key_mask[None, :]

    def by_chunk(array):
        cut = array[:, 0].reshape(layers, samples, depth, devices, chunks, rows)
        cut = jnp.transpose(cut, (4, 0, 1, 2, 3, 5))
        return cut.reshape(chunks, layers, samples, depth, devices * rows)

    queries, grads = by_chunk(query_states), by_chunk(output_grad)

    direct = rows % 16 == 0 and crop % 128 == 0
    arrived = []
    stored = []
    for chunk in range(chunks):
        bias, *kept = forward_rows(chunk, rows, pair_states, *pair_weights)
        stored.append(kept)
        if direct:
            bias = bias.reshape(heads, layers, rows, crop)
        else:
            bias = jnp.transpose(bias.reshape(rows, layers, heads, crop), (2, 1, 0, 3))
        if groups > 1:
            bias = jnp.tile(bias, (groups, 1, 1, 1))
        arrived.append(swap(bias))

    returned = []
    d_queries = []
    state = None
    for chunk in range(chunks):
        bias = arrived[chunk]
        if not direct:
            bias = jnp.transpose(bias, (1, 0, 2, 3)).reshape(1, layers, devices * rows, crop)
        d_query, d_key, d_value, d_bias = attend_rows(
            chunk,
            chunks,
            weights,
            bias,
            valid,
            queries[chunk],
            key_states[:, 0],
            value_states[:, 0],
            grads[chunk],
            state,
        )
        state = (d_key, d_value)
        d_queries.append(d_query)
        if not direct:
            d_bias = jnp.transpose(d_bias.reshape(layers, devices, rows, crop), (1, 0, 2, 3))
        returned.append(swap(d_bias))

    sum_rows = 3 * width + lanes
    share = 16 * -(-sum_rows // (16 * devices))
    pair_state = None
    for chunk in range(chunks):
        d_bias = returned[chunk]
        if groups > 1:
            d_bias = d_bias.reshape(groups, heads, layers, rows, crop).astype(F32)
            d_bias = jnp.sum(d_bias, 0).astype(BF16)
        if direct:
            d_bias = d_bias.reshape(lanes, rows, crop)
        else:
            d_bias = jnp.transpose(d_bias, (2, 1, 0, 3)).reshape(rows, lanes, crop)
        pair_state = backward_rows(
            chunk,
            chunks,
            rows,
            share * devices,
            pair_states.shape,
            stored[chunk],
            d_bias,
            pair_weights,
            pair_state and pair_state[:2],
        )
    pair_grad, _, packed = pair_state

    parts = swap(packed.reshape(devices, share, channels))
    summed = jnp.sum(parts.astype(F32), 0).astype(BF16)
    copies = jnp.broadcast_to(summed[None], (devices, share, channels))
    summed = swap(copies).reshape(devices * share, channels).astype(F32)
    grad_in = summed[: 2 * width].T
    grad_out = summed[2 * width : 3 * width]
    grad_bias = summed[3 * width : sum_rows].reshape(layers, heads, channels)
    grad_bias = jnp.transpose(grad_bias, (0, 2, 1))

    d_query = jnp.stack(d_queries, 0).reshape(chunks, layers, samples, depth, devices, rows)
    d_query = jnp.transpose(d_query, (1, 2, 3, 4, 0, 5)).reshape(query_states.shape)
    return (
        pair_grad,
        d_query,
        d_key[:, None],
        d_value[:, None],
        grad_in,
        grad_out,
        grad_bias,
    )


def solution(mesh):
    in_specs = (
        P(("job", "tok"), None, None),
        P(),
        P(),
        P(),
        P("job"),
        P("job"),
        P(None, "tok", "job", None, None),
        P(None, "tok", "job", None, None),
        P(None, "tok", "job", None, None),
        P(None, "tok", "job", None, None),
    )
    out_specs = (
        P(("job", "tok"), None, None),
        P(None, "tok", "job", None, None),
        P(None, "tok", "job", None, None),
        P(None, "tok", "job", None, None),
        P("job", None),
        P("job", None),
        P("job", None, None),
    )
    return jax.shard_map(body, mesh=mesh, in_specs=in_specs, out_specs=out_specs, check_vma=False)
```

```python
import functools
import math

import jax
import jax.numpy as jnp
from jax import lax
from jax.experimental import pallas as pl
from jax.experimental.pallas import tpu as pltpu
from jax.sharding import PartitionSpec as P

LEVELS = 200
CHUNKS = 2


sigma_high = 160.0
sigma_low = 0.0004
sigma_data = 16.0
rho_power = 7.0
epsilon = 1e-05
masked_score = -1000000000.0

F32 = jnp.float32
BF16 = jnp.bfloat16


def sample_weight(levels):
    level = levels.astype(jnp.float32)
    top_root = sigma_high ** (1.0 / rho_power)
    low_root = sigma_low ** (1.0 / rho_power)
    sigma_level = (top_root + level / (LEVELS - 1) * (low_root - top_root)) ** rho_power
    return (sigma_level * sigma_level + sigma_data * sigma_data) / (sigma_level + sigma_data) ** 2


def mm(left, right, left_dim=1, right_dim=0):
    return lax.dot_general(
        left, right, (((left_dim,), (right_dim,)), ((), ())), preferred_element_type=F32
    )


def normalize(inputs):
    centered = inputs - jnp.mean(inputs, 0, keepdims=True)
    inv_std = lax.rsqrt(jnp.mean(centered * centered, 0, keepdims=True) + epsilon)
    return centered * inv_std, inv_std


def norm_back(normed, inv_std, upstream):
    return inv_std * (
        upstream
        - jnp.mean(upstream, 0, keepdims=True)
        - normed * jnp.mean(upstream * normed, 0, keepdims=True)
    )


UNIT = 128
LANES = 256


def unit_of(size, wanted):
    return wanted if size % wanted == 0 else size


def interleave(make_stages, count, lag):
    rows = [make_stages(index) for index in range(count)]
    running = []
    clock = 0
    while rows or running:
        if rows and clock % lag == 0:
            running.append(rows.pop(0))
        running = [row for row in running if next(row, None) is not None]
        clock += 1


def for_rows(count, group, make_stages, lag):
    group = math.gcd(count, group)

    def step(at, carry):
        interleave(lambda index: make_stages(at * group + index, index), group, lag)
        return carry

    if count == group:
        step(0, 0)
    else:
        lax.fori_loop(0, count // group, step, 0)


def mix_weights(w_in_ref, w_out_ref, w_mix_ref, w_out_t_ref):
    width = w_out_ref.shape[0]
    unit = unit_of(width, UNIT)
    w_in_t = w_in_ref[...].T
    for at in range(0, width, unit):
        w_mix_ref[2 * at : 2 * at + unit, :] = w_in_t[at : at + unit] * 0.5
        w_mix_ref[2 * at + unit : 2 * at + 2 * unit, :] = w_in_t[width + at : width + at + unit]
    w_out_t_ref[...] = w_out_ref[...].T


def pipelined(products, finish):
    waiting = None
    for make in products:
        fresh = make()
        if waiting is not None:
            finish(*waiting)
        waiting = fresh
        yield True
    finish(*waiting)


def forward_kernel(
    direct,
    pair_ref,
    w_in_ref,
    w_out_ref,
    w_bias_ref,
    bias_ref,
    w_mix_ref,
    w_out_t_ref,
    lines_ref,
    hidden_ref,
):
    width = w_out_ref.shape[0]
    layers, heads, channels = w_bias_ref.shape
    unit = unit_of(width, UNIT)
    step, crop, _ = pair_ref.shape
    span = unit_of(crop, LANES)
    first_row = pl.program_id(0) * step

    @pl.when(pl.program_id(0) == 0)
    def _():
        mix_weights(w_in_ref, w_out_ref, w_mix_ref, w_out_t_ref)

    def stages(row, slot):
        for left in range(0, crop, span):
            cols = slice(left, left + span)
            pair_float = pair_ref[row, cols, :].T.astype(F32)
            normed_in = normalize(pair_float)[0].astype(BF16)
            yield True

            def product(at):
                both = mm(w_mix_ref[2 * at : 2 * at + 2 * unit, :], normed_in)
                return at, both[:unit], both[unit:]

            def finish(at, half_gate, up_in):
                silu = half_gate + half_gate * jnp.tanh(half_gate)
                hidden_ref[slot, at : at + unit, cols] = (silu * up_in).astype(BF16)

            yield from pipelined(
                [functools.partial(product, at) for at in range(0, width, unit)], finish
            )
            lifted = pair_float + mm(w_out_t_ref[...], hidden_ref[slot, :, cols])
            yield True
            normed_out = normalize(lifted)[0].astype(BF16)
            bias = mm(w_bias_ref[...].reshape(layers * heads, channels), normed_out)
            if direct:
                tiles, total, tile = lines_ref.shape
                rows = total // (layers * heads)
                for layer in range(layers):
                    at = pl.ds(layer * rows + first_row + row, heads, stride=layers * rows)
                    lines = bias[layer * heads : (layer + 1) * heads]
                    for index in range(span // tile):
                        lines_ref[left // tile + index, at, :] = lines[
                            :, index * tile : (index + 1) * tile
                        ]
            else:
                bias_ref[row, :, cols] = bias.astype(BF16)
            yield True

    for_rows(step, 4, stages, 7)

    if direct:

        @pl.when(pl.program_id(0) == pl.num_programs(0) - 1)
        def _():
            tiles, _, tile = lines_ref.shape
            for index in range(tiles):
                lines = lines_ref[index].reshape(bias_ref.shape[:2] + (tile,))
                bias_ref[:, :, index * tile : (index + 1) * tile] = lines.astype(BF16)


def forward_rows(chunk, rows, pair, w_in, w_out, w_bias):
    crop, channels = pair.shape[1:]
    layers, heads, _ = w_bias.shape
    lanes = layers * heads
    step = math.gcd(rows, 8)
    steps = rows // step
    positions = rows * crop
    width = w_out.shape[0]
    direct = rows % 16 == 0 and crop % 128 == 0
    line_shape = (heads * layers, rows, crop) if direct else (rows, lanes, crop)
    line_spec = (
        pl.BlockSpec(line_shape, lambda i: (0, 0, 0))
        if direct
        else pl.BlockSpec((step, lanes, crop), lambda i: (i, 0, 0))
    )
    return pl.pallas_call(
        functools.partial(forward_kernel, direct),
        grid=(steps,),
        in_specs=[
            pl.BlockSpec((step, crop, channels), lambda i: (chunk * steps + i, 0, 0)),
            pl.BlockSpec(w_in.shape, lambda i: (0, 0)),
            pl.BlockSpec(w_out.shape, lambda i: (0, 0)),
            pl.BlockSpec(w_bias.shape, lambda i: (0, 0, 0)),
        ],
        out_specs=line_spec,
        out_shape=jax.ShapeDtypeStruct(line_shape, BF16),
        scratch_shapes=[
            pltpu.VMEM((2 * width, channels), BF16),
            pltpu.VMEM((channels, width), BF16),
            pltpu.VMEM((crop // 128, lanes * rows, 128) if direct else (1, 8, 128), F32),
            pltpu.VMEM((4, width, crop), BF16),
        ],
        compiler_params=pltpu.CompilerParams(vmem_limit_bytes=56 * 2**20),
        cost_estimate=pl.CostEstimate(
            flops=6 * positions * channels * (3 * width + lanes),
            bytes_accessed=positions * (channels + lanes) * 2,
            transcendentals=positions * width,
        ),
        name="pair_forward",
    )(pair, w_in, w_out, w_bias)


def backward_kernel(
    first,
    last,
    direct,
    pair_ref,
    d_bias_ref,
    w_in_ref,
    w_out_ref,
    w_bias_ref,
    *refs,
):
    if first:
        pair_grad_ref, sums_ref = refs[:2]
    else:
        before_ref, _, pair_grad_ref, sums_ref = refs[:4]
    w_mix_ref, w_out_t_ref, lines_ref = refs[-8:-5]
    hidden_ref, slope_ref, silu_ref, d_projected_ref, flipped_ref = refs[-5:]
    width = w_out_ref.shape[0]
    layers, heads, channels = w_bias_ref.shape
    lanes = layers * heads
    unit = unit_of(width, UNIT)
    step, crop, _ = pair_ref.shape
    span = unit_of(crop, LANES)
    first_row = pl.program_id(0) * step

    @pl.when(pl.program_id(0) == 0)
    def _():
        mix_weights(w_in_ref, w_out_ref, w_mix_ref, w_out_t_ref)
        if first:
            sums_ref[...] = jnp.zeros_like(sums_ref)
        else:
            sums_ref[...] = before_ref[...]
        if direct:
            tiles, total, tile = lines_ref.shape
            for index in range(tiles):
                lines = d_bias_ref[:, :, index * tile : (index + 1) * tile].astype(F32)
                lines_ref[index] = lines.reshape(total, tile)

    def read_lines(row, left):
        if not direct:
            return d_bias_ref[row, :, left : left + span]
        tiles, total, tile = lines_ref.shape
        rows = total // lanes
        found = []
        for layer in range(layers):
            at = pl.ds(layer * rows + first_row + row, heads, stride=layers * rows)
            held = [lines_ref[left // tile + index, at, :] for index in range(span // tile)]
            found.append(jnp.concatenate(held, 1))
        return jnp.concatenate(found, 0).astype(BF16)

    def stages(row, slot):
        bias_sum = jnp.zeros((lanes, channels), F32)
        for left in range(0, crop, span):
            cols = slice(left, left + span)
            pair_float = pair_ref[row, cols, :].T.astype(F32)
            normed_float, inv_in = normalize(pair_float)
            normed_in = normed_float.astype(BF16)
            flipped_ref[slot, 0, cols, :] = normed_in.T
            yield True

            def product(at):
                both = mm(w_mix_ref[2 * at : 2 * at + 2 * unit, :], normed_in)
                return at, both[:unit], both[unit:]

            def finish(at, half_gate, up_in):
                one_plus = 1.0 + jnp.tanh(half_gate)
                silu = half_gate * one_plus
                slope = one_plus * (0.5 + half_gate * (1.0 - 0.5 * one_plus)) * up_in
                hidden_ref[slot, at : at + unit, cols] = (silu * up_in).astype(BF16)
                silu_ref[slot, at : at + unit, :] = silu
                slope_ref[slot, at : at + unit, :] = slope

            yield from pipelined(
                [functools.partial(product, at) for at in range(0, width, unit)], finish
            )
            lifted = pair_float + mm(w_out_t_ref[...], hidden_ref[slot, :, cols])
            d_bias = read_lines(row, left)
            d_normed = mm(w_bias_ref[...].reshape(lanes, channels), d_bias, 0, 0)
            yield True
            out_float, inv_out = normalize(lifted)
            bias_sum = bias_sum + mm(d_bias, out_float.astype(BF16), 1, 1)
            d_lifted = norm_back(out_float, inv_out, d_normed)
            lifted_half = d_lifted.astype(BF16)
            flipped_ref[slot, 1, cols, :] = lifted_half.T
            yield True

            def product_back(at):
                return at, mm(w_out_ref[at : at + unit, :], lifted_half)

            def finish_back(at, d_hidden):
                d_gate = d_hidden * slope_ref[slot, at : at + unit, :]
                d_up = d_hidden * silu_ref[slot, at : at + unit, :]
                d_projected_ref[slot, at : at + unit, cols] = d_gate.astype(BF16)
                d_projected_ref[slot, width + at : width + at + unit, cols] = d_up.astype(BF16)

            yield from pipelined(
                [functools.partial(product_back, at) for at in range(0, width, unit)], finish_back
            )
            d_normed_in = mm(w_in_ref[...], d_projected_ref[slot, :, cols])
            yield True
            pair_grad = d_lifted + norm_back(normed_float, inv_in, d_normed_in)
            pair_grad_ref[row, cols, :] = pair_grad.astype(BF16).T
            yield True
        sums_ref[3 * width :, :] += bias_sum
        for at in range(0, 2 * width, width):
            sums_ref[at : at + width, :] += mm(
                d_projected_ref[slot, at : at + width, :], flipped_ref[slot, 0]
            )
            yield True
        sums_ref[2 * width : 3 * width, :] += mm(hidden_ref[slot], flipped_ref[slot, 1])
        yield True

    for_rows(step, 4, stages, 14)

    if last:
        packed_ref = refs[-9]

        @pl.when(pl.program_id(0) == pl.num_programs(0) - 1)
        def _():
            done = sums_ref.shape[0]
            packed_ref[:done, :] = sums_ref[...].astype(BF16)
            packed_ref[done:, :] = jnp.zeros((packed_ref.shape[0] - done, packed_ref.shape[1]), BF16)


def backward_rows(chunk, chunks, rows, packed_rows, pair, d_bias, weights, state):
    w_in, w_out, w_bias = weights
    crop, channels = pair.shape[1:]
    layers, heads, _ = w_bias.shape
    lanes = layers * heads
    width = w_out.shape[0]
    step = math.gcd(rows, 8)
    steps = rows // step
    positions = rows * crop
    first, last = chunk == 0, chunk == chunks - 1
    direct = rows % 16 == 0 and crop % 128 == 0
    whole = lambda i: (0, 0)
    pair_spec = pl.BlockSpec((step, crop, channels), lambda i: (chunk * steps + i, 0, 0))
    in_specs = [pair_spec]
    if direct:
        in_specs.append(pl.BlockSpec(d_bias.shape, lambda i: (0, 0, 0)))
    else:
        in_specs.append(pl.BlockSpec((step, lanes, crop), lambda i: (i, 0, 0)))
    in_specs += [
        pl.BlockSpec(w_in.shape, whole),
        pl.BlockSpec(w_out.shape, whole),
        pl.BlockSpec(w_bias.shape, lambda i: (0, 0, 0)),
    ]
    operands = [pair, d_bias, *weights]
    aliases = {}
    if not first:
        pair_grad, sums = state
        operands += [sums, pair_grad]
        in_specs += [pl.BlockSpec(sums.shape, whole), pl.BlockSpec(memory_space=pl.ANY)]
        aliases = {len(operands) - 1: 0}
    shapes = [
        jax.ShapeDtypeStruct(pair.shape, BF16),
        jax.ShapeDtypeStruct((3 * width + lanes, channels), F32),
    ]
    out_specs = [pair_spec, pl.BlockSpec(shapes[1].shape, whole)]
    if last:
        shapes.append(jax.ShapeDtypeStruct((packed_rows, channels), BF16))
        out_specs.append(pl.BlockSpec(shapes[2].shape, whole))
    slots = 4
    span = unit_of(crop, LANES)
    return pl.pallas_call(
        functools.partial(backward_kernel, first, last, direct),
        grid=(steps,),
        in_specs=in_specs,
        out_specs=out_specs,
        out_shape=shapes,
        input_output_aliases=aliases,
        scratch_shapes=[
            pltpu.VMEM((2 * width, channels), BF16),
            pltpu.VMEM((channels, width), BF16),
            pltpu.VMEM((crop // 128, lanes * rows, 128) if direct else (1, 8, 128), F32),
            pltpu.VMEM((slots, width, crop), BF16),
            pltpu.VMEM((slots, width, span), F32),
            pltpu.VMEM((slots, width, span), F32),
            pltpu.VMEM((slots, 2 * width, crop), BF16),
            pltpu.VMEM((slots, 2, crop, channels), BF16),
        ],
        compiler_params=pltpu.CompilerParams(vmem_limit_bytes=56 * 2**20),
        cost_estimate=pl.CostEstimate(
            flops=6 * positions * channels * (9 * width + 2 * lanes),
            bytes_accessed=positions * (2 * channels + lanes) * 2,
            transcendentals=positions * width,
        ),
        name="pair_backward",
    )(*operands)


def attend_kernel(
    first, last, weight_ref, bias_ref, valid_ref, q_ref, k_ref, v_ref, g_ref, *refs
):
    if first:
        dq_ref, dk_ref, dv_ref, d_bias_ref = refs
    else:
        dk_before_ref, dv_before_ref, dq_ref, dk_ref, dv_ref, d_bias_ref = refs
    samples, depth = q_ref.shape[1:3]
    sources, _, rows, crop = bias_ref.shape
    scaling = 1.0 / math.sqrt(depth)
    bias = bias_ref[:, 0].astype(F32).reshape(sources * rows, crop)
    valid = valid_ref[...] > 0
    total = jnp.zeros_like(bias)
    for s in range(samples):
        query, key, value = q_ref[0, s], k_ref[0, s], v_ref[0, s]
        grad_half = (weight_ref[s] * g_ref[0, s].astype(F32)).astype(BF16)
        scores = mm(query, key, 0, 0) * scaling + bias
        scores = jnp.where(valid, scores, masked_score)
        exp_scores = jnp.exp(scores - jnp.max(scores, -1, keepdims=True))
        attention = exp_scores / jnp.sum(exp_scores, -1, keepdims=True)
        d_attention = mm(grad_half, value, 0, 0)
        d_scores = attention * (
            d_attention - jnp.sum(attention * d_attention, -1, keepdims=True)
        )
        total = total + d_scores
        scores_half = d_scores.astype(BF16)
        d_value = mm(grad_half, attention.astype(BF16))
        d_key = mm(query, scores_half)
        dq_ref[0, s] = (mm(key, scores_half, 1, 1) * scaling).astype(BF16)
        if not first:
            d_value = d_value + dv_before_ref[0, s]
            d_key = d_key + dk_before_ref[0, s]
        if last:
            d_key = d_key * scaling
        dv_ref[0, s] = d_value.astype(dv_ref.dtype)
        dk_ref[0, s] = d_key.astype(dk_ref.dtype)
    d_bias_ref[:, 0] = total.astype(BF16).reshape(sources, rows, crop)


def attend_rows(chunk, chunks, weights, bias, valid, query, key, value, grad, state):
    sources, layers, rows, crop = bias.shape
    samples, depth, row_count = query.shape[1:]
    first, last = chunk == 0, chunk == chunks - 1
    vec = lambda shape: pl.BlockSpec((1,) + shape[1:], lambda l: (l, 0, 0, 0))
    plane = pl.BlockSpec((sources, 1, rows, crop), lambda l: (0, l, 0, 0))
    in_specs = [
        pl.BlockSpec(memory_space=pltpu.SMEM),
        plane,
        pl.BlockSpec(valid.shape, lambda l: (0, 0)),
        vec(query.shape),
        vec(key.shape),
        vec(value.shape),
        vec(grad.shape),
    ]
    operands = [weights, bias, valid, query, key, value, grad]
    if not first:
        operands += list(state)
        in_specs += [vec(key.shape), vec(value.shape)]
    kind = BF16 if last else F32
    return pl.pallas_call(
        functools.partial(attend_kernel, first, last),
        grid=(layers,),
        in_specs=in_specs,
        out_specs=[vec(query.shape), vec(key.shape), vec(value.shape), plane],
        out_shape=[
            jax.ShapeDtypeStruct(query.shape, BF16),
            jax.ShapeDtypeStruct(key.shape, kind),
            jax.ShapeDtypeStruct(value.shape, kind),
            jax.ShapeDtypeStruct(bias.shape, BF16),
        ],
        compiler_params=pltpu.CompilerParams(vmem_limit_bytes=48 * 2**20),
        cost_estimate=pl.CostEstimate(
            flops=200 * layers * samples * depth * row_count * crop,
            bytes_accessed=layers * crop * (4 * row_count + 12 * samples * depth),
            transcendentals=layers * samples * row_count * crop,
        ),
        name="attention_backward",
    )(*operands)


def swap(array, teams=None):
    return lax.all_to_all(
        array, "tok", split_axis=0, concat_axis=0, tiled=True, axis_index_groups=teams
    )


def body(
    pair_states,
    weight_in,
    weight_out,
    weight_bias,
    key_mask,
    noise_level,
    query_states,
    key_states,
    value_states,
    output_grad,
):
    row_count, crop, channels = pair_states.shape
    layers, _, heads = weight_bias.shape
    width = weight_out.shape[0]
    devices = lax.axis_size("tok")
    groups = devices // heads
    samples, depth = query_states.shape[2:4]
    chunks = CHUNKS
    rows = row_count // chunks
    lanes = heads * layers

    pair_weights = (weight_in, weight_out, jnp.transpose(weight_bias, (0, 2, 1)))

    group = lax.axis_index("tok") // heads
    weights = sample_weight(lax.dynamic_slice_in_dim(noise_level, group * samples, samples))
    valid = key_mask[None, :]

    def by_chunk(array):
        cut = array[:, 0].reshape(layers, samples, depth, devices, chunks, rows)
        cut = jnp.transpose(cut, (4, 0, 1, 2, 3, 5))
        return cut.reshape(chunks, layers, samples, depth, devices * rows)

    queries, grads = by_chunk(query_states), by_chunk(output_grad)

    direct = rows % 16 == 0 and crop % 128 == 0
    arrived = []
    for chunk in range(chunks):
        bias = forward_rows(chunk, rows, pair_states, *pair_weights)
        if direct:
            bias = bias.reshape(heads, layers, rows, crop)
        else:
            bias = jnp.transpose(bias.reshape(rows, layers, heads, crop), (2, 1, 0, 3))
        if groups > 1:
            bias = jnp.tile(bias, (groups, 1, 1, 1))
        arrived.append(swap(bias))

    returned = []
    d_queries = []
    state = None
    for chunk in range(chunks):
        bias = arrived[chunk]
        if not direct:
            bias = jnp.transpose(bias, (1, 0, 2, 3)).reshape(1, layers, devices * rows, crop)
        d_query, d_key, d_value, d_bias = attend_rows(
            chunk,
            chunks,
            weights,
            bias,
            valid,
            queries[chunk],
            key_states[:, 0],
            value_states[:, 0],
            grads[chunk],
            state,
        )
        state = (d_key, d_value)
        d_queries.append(d_query)
        if not direct:
            d_bias = jnp.transpose(d_bias.reshape(layers, devices, rows, crop), (1, 0, 2, 3))
        returned.append(swap(d_bias))

    sum_rows = 3 * width + lanes
    share = 16 * -(-sum_rows // (16 * devices))
    pair_state = None
    for chunk in range(chunks):
        d_bias = returned[chunk]
        if groups > 1:
            d_bias = d_bias.reshape(groups, heads, layers, rows, crop).astype(F32)
            d_bias = jnp.sum(d_bias, 0).astype(BF16)
        if direct:
            d_bias = d_bias.reshape(lanes, rows, crop)
        else:
            d_bias = jnp.transpose(d_bias, (2, 1, 0, 3)).reshape(rows, lanes, crop)
        pair_state = backward_rows(
            chunk,
            chunks,
            rows,
            share * devices,
            pair_states,
            d_bias,
            pair_weights,
            pair_state and pair_state[:2],
        )
    pair_grad, _, packed = pair_state

    parity = lax.axis_index("tok") % 2
    across = [(index, index ^ 1) for index in range(devices)]
    teams = [list(range(odd, devices, 2)) for odd in range(2)]
    halves = packed.reshape(2, devices // 2 * share, channels)
    theirs = lax.ppermute(lax.dynamic_index_in_dim(halves, 1 - parity, 0, False), "tok", across)
    mine = lax.dynamic_index_in_dim(halves, parity, 0, False)
    mine = (mine.astype(F32) + theirs.astype(F32)).astype(BF16)
    parts = swap(mine.reshape(devices // 2, share, channels), teams)
    summed = jnp.sum(parts.astype(F32), 0).astype(BF16)
    copies = jnp.broadcast_to(summed[None], (devices // 2, share, channels))
    mine = swap(copies, teams).reshape(devices // 2 * share, channels)
    theirs = lax.ppermute(mine, "tok", across)
    even = parity == 0
    summed = jnp.concatenate([jnp.where(even, mine, theirs), jnp.where(even, theirs, mine)], 0)
    summed = summed.astype(F32)
    grad_in = summed[: 2 * width].T
    grad_out = summed[2 * width : 3 * width]
    grad_bias = summed[3 * width : sum_rows].reshape(layers, heads, channels)
    grad_bias = jnp.transpose(grad_bias, (0, 2, 1))

    d_query = jnp.stack(d_queries, 0).reshape(chunks, layers, samples, depth, devices, rows)
    d_query = jnp.transpose(d_query, (1, 2, 3, 4, 0, 5)).reshape(query_states.shape)
    return (
        pair_grad,
        d_query,
        d_key[:, None],
        d_value[:, None],
        grad_in,
        grad_out,
        grad_bias,
    )


def solution(mesh):
    in_specs = (
        P(("job", "tok"), None, None),
        P(),
        P(),
        P(),
        P("job"),
        P("job"),
        P(None, "tok", "job", None, None),
        P(None, "tok", "job", None, None),
        P(None, "tok", "job", None, None),
        P(None, "tok", "job", None, None),
    )
    out_specs = (
        P(("job", "tok"), None, None),
        P(None, "tok", "job", None, None),
        P(None, "tok", "job", None, None),
        P(None, "tok", "job", None, None),
        P("job", None),
        P("job", None),
        P("job", None, None),
    )
    return jax.shard_map(body, mesh=mesh, in_specs=in_specs, out_specs=out_specs, check_vma=False)
```

```python
import functools
import math

import jax
import jax.numpy as jnp
from jax import lax
from jax.experimental import pallas as pl
from jax.experimental.pallas import tpu as pltpu
from jax.sharding import PartitionSpec as P

LEVELS = 200
CHUNKS = 2


sigma_high = 160.0
sigma_low = 0.0004
sigma_data = 16.0
rho_power = 7.0
epsilon = 1e-05
masked_score = -1000000000.0

F32 = jnp.float32
BF16 = jnp.bfloat16


def sample_weight(levels):
    level = levels.astype(jnp.float32)
    top_root = sigma_high ** (1.0 / rho_power)
    low_root = sigma_low ** (1.0 / rho_power)
    sigma_level = (top_root + level / (LEVELS - 1) * (low_root - top_root)) ** rho_power
    return (sigma_level * sigma_level + sigma_data * sigma_data) / (sigma_level + sigma_data) ** 2


def mm(left, right, left_dim=1, right_dim=0):
    return lax.dot_general(
        left, right, (((left_dim,), (right_dim,)), ((), ())), preferred_element_type=F32
    )


def normalize(inputs):
    centered = inputs - jnp.mean(inputs, 0, keepdims=True)
    inv_std = lax.rsqrt(jnp.mean(centered * centered, 0, keepdims=True) + epsilon)
    return centered * inv_std, inv_std


def norm_back(normed, inv_std, upstream):
    return inv_std * (
        upstream
        - jnp.mean(upstream, 0, keepdims=True)
        - normed * jnp.mean(upstream * normed, 0, keepdims=True)
    )


def split_width(width):
    return 256 if width % 256 == 0 else width


def interleave(make_stages, count, lag):
    rows = [make_stages(index) for index in range(count)]
    running = []
    clock = 0
    while rows or running:
        if rows and clock % lag == 0:
            running.append(rows.pop(0))
        running = [row for row in running if next(row, None) is not None]
        clock += 1


def for_groups(count, group, one_group):
    group = math.gcd(count, group)

    def step(at, carry):
        one_group(at * group, group)
        return carry

    if count == group:
        step(0, 0)
    else:
        lax.fori_loop(0, count // group, step, 0)


def forward_kernel(
    direct,
    pair_ref,
    w_in_ref,
    w_out_ref,
    w_bias_ref,
    bias_ref,
    w_in_t_ref,
    w_out_t_ref,
    lines_ref,
):
    width = w_out_ref.shape[0]
    layers, heads, channels = w_bias_ref.shape
    piece = split_width(width)
    step = pair_ref.shape[0]
    first_row = pl.program_id(0) * step

    @pl.when(pl.program_id(0) == 0)
    def _():
        w_in_t = w_in_ref[...].T
        w_in_t_ref[:width, :] = w_in_t[:width] * 0.5
        w_in_t_ref[width:, :] = w_in_t[width:]
        w_out_t_ref[...] = w_out_ref[...].T

    def stages(row):
        pair_float = pair_ref[row].T.astype(F32)
        normed_in = normalize(pair_float)[0].astype(BF16)
        yield True
        hiddens = []
        for at in range(0, width, piece):
            half_gate = mm(w_in_t_ref[at : at + piece, :], normed_in)
            up_in = mm(w_in_t_ref[width + at : width + at + piece, :], normed_in)
            yield True
            hidden = half_gate * (1.0 + jnp.tanh(half_gate)) * up_in
            hiddens.append(hidden.astype(BF16))
            yield True
        lifted = pair_float + mm(w_out_t_ref[...], jnp.concatenate(hiddens, 0))
        normed_out = normalize(lifted)[0].astype(BF16)
        yield True
        bias = mm(w_bias_ref[...].reshape(layers * heads, channels), normed_out)
        if direct:
            tiles, total, tile = lines_ref.shape
            rows = total // (layers * heads)
            for layer in range(layers):
                at = pl.ds(layer * rows + first_row + row, heads, stride=layers * rows)
                lines = bias[layer * heads : (layer + 1) * heads]
                for index in range(tiles):
                    lines_ref[index, at, :] = lines[:, index * tile : (index + 1) * tile]
        else:
            bias_ref[row] = bias.astype(BF16)

    for_groups(step, 4, lambda at, count: interleave(lambda i: stages(at + i), count, 2))

    if direct:

        @pl.when(pl.program_id(0) == pl.num_programs(0) - 1)
        def _():
            tiles, _, tile = lines_ref.shape
            for index in range(tiles):
                lines = lines_ref[index].reshape(bias_ref.shape[:2] + (tile,))
                bias_ref[:, :, index * tile : (index + 1) * tile] = lines.astype(BF16)


def forward_rows(chunk, rows, pair, w_in, w_out, w_bias):
    crop, channels = pair.shape[1:]
    layers, heads, _ = w_bias.shape
    lanes = layers * heads
    step = math.gcd(rows, 8)
    steps = rows // step
    positions = rows * crop
    width = w_out.shape[0]
    direct = rows % 16 == 0 and crop % 128 == 0
    line_shape = (heads * layers, rows, crop) if direct else (rows, lanes, crop)
    line_spec = (
        pl.BlockSpec(line_shape, lambda i: (0, 0, 0))
        if direct
        else pl.BlockSpec((step, lanes, crop), lambda i: (i, 0, 0))
    )
    return pl.pallas_call(
        functools.partial(forward_kernel, direct),
        grid=(steps,),
        in_specs=[
            pl.BlockSpec((step, crop, channels), lambda i: (chunk * steps + i, 0, 0)),
            pl.BlockSpec(w_in.shape, lambda i: (0, 0)),
            pl.BlockSpec(w_out.shape, lambda i: (0, 0)),
            pl.BlockSpec(w_bias.shape, lambda i: (0, 0, 0)),
        ],
        out_specs=line_spec,
        out_shape=jax.ShapeDtypeStruct(line_shape, BF16),
        scratch_shapes=[
            pltpu.VMEM((2 * width, channels), BF16),
            pltpu.VMEM((channels, width), BF16),
            pltpu.VMEM((crop // 128, lanes * rows, 128) if direct else (1, 8, 128), F32),
        ],
        compiler_params=pltpu.CompilerParams(vmem_limit_bytes=56 * 2**20),
        cost_estimate=pl.CostEstimate(
            flops=6 * positions * channels * (3 * width + lanes),
            bytes_accessed=positions * (channels + lanes) * 2,
            transcendentals=positions * width,
        ),
        name="pair_forward",
    )(pair, w_in, w_out, w_bias)


def backward_kernel(
    first,
    last,
    direct,
    pair_ref,
    d_bias_ref,
    w_in_ref,
    w_out_ref,
    w_bias_ref,
    *refs,
):
    if first:
        pair_grad_ref, sums_ref = refs[:2]
    else:
        before_ref, _, pair_grad_ref, sums_ref = refs[:4]
    w_in_t_ref, w_out_t_ref, w_back_ref, w_half_ref, lines_ref = refs[-5:]
    width = w_out_ref.shape[0]
    layers, heads, channels = w_bias_ref.shape
    lanes = layers * heads
    piece = split_width(width)
    step = pair_ref.shape[0]
    first_row = pl.program_id(0) * step

    @pl.when(pl.program_id(0) == 0)
    def _():
        w_in_t = w_in_ref[...].T
        w_in_t_ref[:width, :] = w_in_t[:width] * 0.5
        w_in_t_ref[width:, :] = w_in_t[width:]
        w_out_t_ref[...] = w_out_ref[...].T
        w_back_ref[:, :width] = w_in_ref[:, :width]
        w_back_ref[:, width:] = w_in_ref[:, width:] * 2.0
        w_half_ref[...] = w_out_ref[...] * 0.5
        if first:
            sums_ref[...] = jnp.zeros_like(sums_ref)
        else:
            sums_ref[...] = before_ref[...]
        if direct:
            tiles, total, tile = lines_ref.shape
            for index in range(tiles):
                lines = d_bias_ref[:, :, index * tile : (index + 1) * tile].astype(F32)
                lines_ref[index] = lines.reshape(total, tile)

    def read_lines(row):
        if not direct:
            return d_bias_ref[row]
        tiles, total, _ = lines_ref.shape
        rows = total // lanes
        found = []
        for layer in range(layers):
            at = pl.ds(layer * rows + first_row + row, heads, stride=layers * rows)
            found.append(jnp.concatenate([lines_ref[index, at, :] for index in range(tiles)], 1))
        return jnp.concatenate(found, 0).astype(BF16)

    def stages(row, kept):
        pair_float = pair_ref[row].T.astype(F32)
        normed_float, inv_in = normalize(pair_float)
        normed_in = normed_float.astype(BF16)
        yield True
        pieces = []
        for at in range(0, width, piece):
            half_gate = mm(w_in_t_ref[at : at + piece, :], normed_in)
            up_in = mm(w_in_t_ref[width + at : width + at + piece, :], normed_in)
            yield True
            one_plus = 1.0 + jnp.tanh(half_gate)
            silu = half_gate * one_plus
            hidden = (silu * up_in).astype(BF16)
            slope = one_plus * (1.0 + half_gate * (2.0 - one_plus)) * up_in
            pieces.append((silu, slope, hidden))
            yield True
        hidden = jnp.concatenate([hidden for _, _, hidden in pieces], 0)
        lifted = pair_float + mm(w_out_t_ref[...], hidden)
        d_bias = read_lines(row)
        d_normed = mm(w_bias_ref[...].reshape(lanes, channels), d_bias, 0, 0)
        yield True
        out_float, inv_out = normalize(lifted)
        normed_out = out_float.astype(BF16)
        d_lifted = norm_back(out_float, inv_out, d_normed)
        lifted_half = d_lifted.astype(BF16)
        yield True
        d_gates, d_ups = [], []
        for index, (silu, slope, _) in enumerate(pieces):
            at = index * piece
            d_hidden = mm(w_half_ref[at : at + piece, :], lifted_half)
            yield True
            d_gates.append((d_hidden * slope).astype(BF16))
            d_ups.append((d_hidden * silu).astype(BF16))
            yield True
        d_projected = jnp.concatenate(d_gates + d_ups, 0)
        kept.append((d_projected, normed_in, hidden, lifted_half, d_bias, normed_out))
        d_normed_in = mm(w_back_ref[...], d_projected)
        yield True
        pair_grad = d_lifted + norm_back(normed_float, inv_in, d_normed_in)
        pair_grad_ref[row] = pair_grad.astype(BF16).T

    def one_group(at, count):
        kept = []
        interleave(lambda index: stages(at + index, kept), count, 3)
        d_projected, normed_in, hidden, lifted_half, d_bias, normed_out = (
            jnp.concatenate(parts, 1) for parts in zip(*kept)
        )
        sums_ref[: 2 * width, :] += mm(d_projected, normed_in, 1, 1)
        sums_ref[2 * width : 3 * width, :] += mm(hidden, lifted_half, 1, 1)
        sums_ref[3 * width :, :] += mm(d_bias, normed_out, 1, 1)

    for_groups(step, 4, one_group)

    if last:
        packed_ref = refs[-6]

        @pl.when(pl.program_id(0) == pl.num_programs(0) - 1)
        def _():
            done = sums_ref.shape[0]
            packed_ref[:done, :] = sums_ref[...].astype(BF16)
            packed_ref[width : 2 * width, :] = (2.0 * sums_ref[width : 2 * width, :]).astype(BF16)
            packed_ref[done:, :] = jnp.zeros((packed_ref.shape[0] - done, packed_ref.shape[1]), BF16)


def backward_rows(chunk, chunks, rows, packed_rows, pair, d_bias, weights, state):
    w_in, w_out, w_bias = weights
    crop, channels = pair.shape[1:]
    layers, heads, _ = w_bias.shape
    lanes = layers * heads
    width = w_out.shape[0]
    step = math.gcd(rows, 8)
    steps = rows // step
    positions = rows * crop
    first, last = chunk == 0, chunk == chunks - 1
    direct = rows % 16 == 0 and crop % 128 == 0
    whole = lambda i: (0, 0)
    pair_spec = pl.BlockSpec((step, crop, channels), lambda i: (chunk * steps + i, 0, 0))
    in_specs = [pair_spec]
    if direct:
        in_specs.append(pl.BlockSpec(d_bias.shape, lambda i: (0, 0, 0)))
    else:
        in_specs.append(pl.BlockSpec((step, lanes, crop), lambda i: (i, 0, 0)))
    in_specs += [
        pl.BlockSpec(w_in.shape, whole),
        pl.BlockSpec(w_out.shape, whole),
        pl.BlockSpec(w_bias.shape, lambda i: (0, 0, 0)),
    ]
    operands = [pair, d_bias, *weights]
    aliases = {}
    if not first:
        pair_grad, sums = state
        operands += [sums, pair_grad]
        in_specs += [pl.BlockSpec(sums.shape, whole), pl.BlockSpec(memory_space=pl.ANY)]
        aliases = {len(operands) - 1: 0}
    shapes = [
        jax.ShapeDtypeStruct(pair.shape, BF16),
        jax.ShapeDtypeStruct((3 * width + lanes, channels), F32),
    ]
    out_specs = [pair_spec, pl.BlockSpec(shapes[1].shape, whole)]
    if last:
        shapes.append(jax.ShapeDtypeStruct((packed_rows, channels), BF16))
        out_specs.append(pl.BlockSpec(shapes[2].shape, whole))
    return pl.pallas_call(
        functools.partial(backward_kernel, first, last, direct),
        grid=(steps,),
        in_specs=in_specs,
        out_specs=out_specs,
        out_shape=shapes,
        input_output_aliases=aliases,
        scratch_shapes=[
            pltpu.VMEM((2 * width, channels), BF16),
            pltpu.VMEM((channels, width), BF16),
            pltpu.VMEM((channels, 2 * width), BF16),
            pltpu.VMEM((width, channels), BF16),
            pltpu.VMEM((crop // 128, lanes * rows, 128) if direct else (1, 8, 128), F32),
        ],
        compiler_params=pltpu.CompilerParams(vmem_limit_bytes=56 * 2**20),
        cost_estimate=pl.CostEstimate(
            flops=6 * positions * channels * (9 * width + 2 * lanes),
            bytes_accessed=positions * (2 * channels + lanes) * 2,
            transcendentals=positions * width,
        ),
        name="pair_backward",
    )(*operands)


def attend_kernel(
    first, last, weight_ref, bias_ref, valid_ref, q_ref, k_ref, v_ref, g_ref, *refs
):
    if first:
        dq_ref, dk_ref, dv_ref, d_bias_ref = refs
    else:
        dk_before_ref, dv_before_ref, dq_ref, dk_ref, dv_ref, d_bias_ref = refs
    samples, depth = q_ref.shape[1:3]
    sources, _, rows, crop = bias_ref.shape
    scaling = 1.0 / math.sqrt(depth)
    bias = bias_ref[:, 0].astype(F32).reshape(sources * rows, crop)
    valid = valid_ref[...] > 0
    total = jnp.zeros_like(bias)
    for s in range(samples):
        query, key, value = q_ref[0, s], k_ref[0, s], v_ref[0, s]
        grad_half = (weight_ref[s] * g_ref[0, s].astype(F32)).astype(BF16)
        scores = mm(query, key, 0, 0) * scaling + bias
        scores = jnp.where(valid, scores, masked_score)
        exp_scores = jnp.exp(scores - jnp.max(scores, -1, keepdims=True))
        attention = exp_scores / jnp.sum(exp_scores, -1, keepdims=True)
        d_attention = mm(grad_half, value, 0, 0)
        d_scores = attention * (
            d_attention - jnp.sum(attention * d_attention, -1, keepdims=True)
        )
        total = total + d_scores
        scores_half = d_scores.astype(BF16)
        d_value = mm(grad_half, attention.astype(BF16))
        d_key = mm(query, scores_half)
        dq_ref[0, s] = (mm(key, scores_half, 1, 1) * scaling).astype(BF16)
        if not first:
            d_value = d_value + dv_before_ref[0, s]
            d_key = d_key + dk_before_ref[0, s]
        if last:
            d_key = d_key * scaling
        dv_ref[0, s] = d_value.astype(dv_ref.dtype)
        dk_ref[0, s] = d_key.astype(dk_ref.dtype)
    d_bias_ref[:, 0] = total.astype(BF16).reshape(sources, rows, crop)


def attend_rows(chunk, chunks, weights, bias, valid, query, key, value, grad, state):
    sources, layers, rows, crop = bias.shape
    samples, depth, row_count = query.shape[1:]
    first, last = chunk == 0, chunk == chunks - 1
    vec = lambda shape: pl.BlockSpec((1,) + shape[1:], lambda l: (l, 0, 0, 0))
    plane = pl.BlockSpec((sources, 1, rows, crop), lambda l: (0, l, 0, 0))
    in_specs = [
        pl.BlockSpec(memory_space=pltpu.SMEM),
        plane,
        pl.BlockSpec(valid.shape, lambda l: (0, 0)),
        vec(query.shape),
        vec(key.shape),
        vec(value.shape),
        vec(grad.shape),
    ]
    operands = [weights, bias, valid, query, key, value, grad]
    if not first:
        operands += list(state)
        in_specs += [vec(key.shape), vec(value.shape)]
    kind = BF16 if last else F32
    return pl.pallas_call(
        functools.partial(attend_kernel, first, last),
        grid=(layers,),
        in_specs=in_specs,
        out_specs=[vec(query.shape), vec(key.shape), vec(value.shape), plane],
        out_shape=[
            jax.ShapeDtypeStruct(query.shape, BF16),
            jax.ShapeDtypeStruct(key.shape, kind),
            jax.ShapeDtypeStruct(value.shape, kind),
            jax.ShapeDtypeStruct(bias.shape, BF16),
        ],
        compiler_params=pltpu.CompilerParams(vmem_limit_bytes=48 * 2**20),
        cost_estimate=pl.CostEstimate(
            flops=200 * layers * samples * depth * row_count * crop,
            bytes_accessed=layers * crop * (4 * row_count + 12 * samples * depth),
            transcendentals=layers * samples * row_count * crop,
        ),
        name="attention_backward",
    )(*operands)


def swap(array):
    return lax.all_to_all(array, "tok", split_axis=0, concat_axis=0, tiled=True)


def bit_groups(devices):
    bits = list(range(devices.bit_length() - 1))
    groups = [[bit] for bit in bits[:2]]
    return groups + [bits[at : at + 2] for at in range(2, len(bits), 2)]


def partner_list(devices, bits, step):
    mask = sum(((step >> place) & 1) << bit for place, bit in enumerate(bits))
    return [(index, index ^ mask) for index in range(devices)]


def digit_of(index, bits):
    return sum(((index >> bit) & 1) << place for place, bit in enumerate(bits))


def pick(blocks, index):
    return lax.dynamic_index_in_dim(blocks, index, 0, False)


def sum_over_devices(array):
    devices = lax.axis_size("tok")
    index = lax.axis_index("tok")
    groups = bit_groups(devices)
    held = array
    for bits in groups:
        count = 1 << len(bits)
        digit = digit_of(index, bits)
        blocks = held.reshape(count, held.shape[0] // count, held.shape[1])
        total = pick(blocks, digit).astype(F32)
        received = [
            lax.ppermute(pick(blocks, digit ^ step), "tok", partner_list(devices, bits, step))
            for step in range(1, count)
        ]
        for block in received:
            total = total + block.astype(F32)
        held = total.astype(BF16)
    for bits in reversed(groups):
        count = 1 << len(bits)
        digit = digit_of(index, bits)
        received = [held] + [
            lax.ppermute(held, "tok", partner_list(devices, bits, step)) for step in range(1, count)
        ]
        if count == 2:
            even = digit == 0
            ordered = [jnp.where(even, *received), jnp.where(even, *received[::-1])]
        else:
            stacked = jnp.stack(received, 0)
            ordered = [pick(stacked, digit ^ place) for place in range(count)]
        held = jnp.concatenate(ordered, 0)
    return held.astype(F32)


def body(
    pair_states,
    weight_in,
    weight_out,
    weight_bias,
    key_mask,
    noise_level,
    query_states,
    key_states,
    value_states,
    output_grad,
):
    row_count, crop, channels = pair_states.shape
    layers, _, heads = weight_bias.shape
    width = weight_out.shape[0]
    devices = lax.axis_size("tok")
    groups = devices // heads
    samples, depth = query_states.shape[2:4]
    chunks = CHUNKS
    rows = row_count // chunks
    lanes = heads * layers

    pair_weights = (weight_in, weight_out, jnp.transpose(weight_bias, (0, 2, 1)))

    group = lax.axis_index("tok") // heads
    weights = sample_weight(lax.dynamic_slice_in_dim(noise_level, group * samples, samples))
    valid = key_mask[None, :]

    def by_chunk(array):
        cut = array[:, 0].reshape(layers, samples, depth, devices, chunks, rows)
        cut = jnp.transpose(cut, (4, 0, 1, 2, 3, 5))
        return cut.reshape(chunks, layers, samples, depth, devices * rows)

    queries, grads = by_chunk(query_states), by_chunk(output_grad)

    direct = rows % 16 == 0 and crop % 128 == 0
    arrived = []
    for chunk in range(chunks):
        bias = forward_rows(chunk, rows, pair_states, *pair_weights)
        if direct:
            bias = bias.reshape(heads, layers, rows, crop)
        else:
            bias = jnp.transpose(bias.reshape(rows, layers, heads, crop), (2, 1, 0, 3))
        if groups > 1:
            bias = jnp.tile(bias, (groups, 1, 1, 1))
        arrived.append(swap(bias))

    returned = []
    d_queries = []
    state = None
    for chunk in range(chunks):
        bias = arrived[chunk]
        if not direct:
            bias = jnp.transpose(bias, (1, 0, 2, 3)).reshape(1, layers, devices * rows, crop)
        d_query, d_key, d_value, d_bias = attend_rows(
            chunk,
            chunks,
            weights,
            bias,
            valid,
            queries[chunk],
            key_states[:, 0],
            value_states[:, 0],
            grads[chunk],
            state,
        )
        state = (d_key, d_value)
        d_queries.append(d_query)
        if not direct:
            d_bias = jnp.transpose(d_bias.reshape(layers, devices, rows, crop), (1, 0, 2, 3))
        returned.append(swap(d_bias))

    sum_rows = 3 * width + lanes
    share = 16 * -(-sum_rows // (16 * devices))
    pair_state = None
    for chunk in range(chunks):
        d_bias = returned[chunk]
        if groups > 1:
            d_bias = d_bias.reshape(groups, heads, layers, rows, crop).astype(F32)
            d_bias = jnp.sum(d_bias, 0).astype(BF16)
        if direct:
            d_bias = d_bias.reshape(lanes, rows, crop)
        else:
            d_bias = jnp.transpose(d_bias, (2, 1, 0, 3)).reshape(rows, lanes, crop)
        pair_state = backward_rows(
            chunk,
            chunks,
            rows,
            share * devices,
            pair_states,
            d_bias,
            pair_weights,
            pair_state and pair_state[:2],
        )
    pair_grad, _, packed = pair_state

    summed = sum_over_devices(packed)
    grad_in = summed[: 2 * width].T
    grad_out = summed[2 * width : 3 * width]
    grad_bias = summed[3 * width : sum_rows].reshape(layers, heads, channels)
    grad_bias = jnp.transpose(grad_bias, (0, 2, 1))

    d_query = jnp.stack(d_queries, 0).reshape(chunks, layers, samples, depth, devices, rows)
    d_query = jnp.transpose(d_query, (1, 2, 3, 4, 0, 5)).reshape(query_states.shape)
    return (
        pair_grad,
        d_query,
        d_key[:, None],
        d_value[:, None],
        grad_in,
        grad_out,
        grad_bias,
    )


def solution(mesh):
    in_specs = (
        P(("job", "tok"), None, None),
        P(),
        P(),
        P(),
        P("job"),
        P("job"),
        P(None, "tok", "job", None, None),
        P(None, "tok", "job", None, None),
        P(None, "tok", "job", None, None),
        P(None, "tok", "job", None, None),
    )
    out_specs = (
        P(("job", "tok"), None, None),
        P(None, "tok", "job", None, None),
        P(None, "tok", "job", None, None),
        P(None, "tok", "job", None, None),
        P("job", None),
        P("job", None),
        P("job", None, None),
    )
    return jax.shard_map(body, mesh=mesh, in_specs=in_specs, out_specs=out_specs, check_vma=False)
```

```python
import functools
import math

import jax
import jax.numpy as jnp
from jax import lax
from jax.experimental import pallas as pl
from jax.experimental.pallas import tpu as pltpu
from jax.sharding import PartitionSpec as P

LEVELS = 200


sigma_high = 160.0
sigma_low = 0.0004
sigma_data = 16.0
rho_power = 7.0
epsilon = 1e-05
masked_score = -1000000000.0

F32 = jnp.float32
BF16 = jnp.bfloat16


def sample_weight(levels):
    level = levels.astype(jnp.float32)
    top_root = sigma_high ** (1.0 / rho_power)
    low_root = sigma_low ** (1.0 / rho_power)
    sigma_level = (top_root + level / (LEVELS - 1) * (low_root - top_root)) ** rho_power
    return (sigma_level * sigma_level + sigma_data * sigma_data) / (sigma_level + sigma_data) ** 2


def mm(left, right, left_dim=1, right_dim=0):
    return lax.dot_general(
        left, right, (((left_dim,), (right_dim,)), ((), ())), preferred_element_type=F32
    )


def normalize(inputs):
    centered = inputs - jnp.mean(inputs, 0, keepdims=True)
    inv_std = lax.rsqrt(jnp.mean(centered * centered, 0, keepdims=True) + epsilon)
    return centered * inv_std, inv_std


def norm_back(normed, inv_std, upstream):
    return inv_std * (
        upstream
        - jnp.mean(upstream, 0, keepdims=True)
        - normed * jnp.mean(upstream * normed, 0, keepdims=True)
    )


def split_width(width):
    return 256 if width % 256 == 0 else width


def interleave(make_stages, count, lag):
    rows = [make_stages(index) for index in range(count)]
    running = []
    clock = 0
    while rows or running:
        if rows and clock % lag == 0:
            running.append(rows.pop(0))
        running = [row for row in running if next(row, None) is not None]
        clock += 1


def for_groups(count, group, one_group):
    group = math.gcd(count, group)

    def step(at, carry):
        one_group(at * group, group)
        return carry

    if count == group:
        step(0, 0)
    else:
        lax.fori_loop(0, count // group, step, 0)


def row_step(rows):
    return math.gcd(rows, 8 if rows > 8 else 4)


def is_direct(rows, crop):
    return rows % 8 == 0 and crop % 128 == 0


def forward_kernel(direct, first, pair_ref, w_bias_ref, *refs):
    if first:
        w_in_ref, w_out_ref, bias_ref, w_in_t_ref, w_out_t_ref, w_back_ref, w_half_ref = refs[:-1]
    else:
        w_in_t_ref, w_out_t_ref, bias_ref = refs[:-1]
    lines_ref = refs[-1]
    width = w_out_t_ref.shape[1]
    layers, heads, channels = w_bias_ref.shape
    piece = split_width(width)
    step = pair_ref.shape[0]
    first_row = pl.program_id(0) * step

    if first:

        @pl.when(pl.program_id(0) == 0)
        def _():
            w_in_t = w_in_ref[...].T
            w_in_t_ref[:width, :] = w_in_t[:width] * 0.5
            w_in_t_ref[width:, :] = w_in_t[width:]
            w_out_t_ref[...] = w_out_ref[...].T
            w_back_ref[:, :width] = w_in_ref[:, :width]
            w_back_ref[:, width:] = w_in_ref[:, width:] * 2.0
            w_half_ref[...] = w_out_ref[...] * 0.5

    def stages(row):
        pair_float = pair_ref[row].T.astype(F32)
        normed_in = normalize(pair_float)[0].astype(BF16)
        yield True
        lifted = pair_float
        for at in range(0, width, piece):
            half_gate = mm(w_in_t_ref[at : at + piece, :], normed_in)
            up_in = mm(w_in_t_ref[width + at : width + at + piece, :], normed_in)
            yield True
            hidden = (half_gate * (1.0 + jnp.tanh(half_gate)) * up_in).astype(BF16)
            lifted = lifted + mm(w_out_t_ref[:, at : at + piece], hidden)
            yield True
        normed_out = normalize(lifted)[0].astype(BF16)
        yield True
        bias = mm(w_bias_ref[...].reshape(layers * heads, channels), normed_out)
        if direct:
            tiles, total, tile = lines_ref.shape
            rows = total // (layers * heads)
            for layer in range(layers):
                at = pl.ds(layer * rows + first_row + row, heads, stride=layers * rows)
                lines = bias[layer * heads : (layer + 1) * heads]
                for index in range(tiles):
                    lines_ref[index, at, :] = lines[:, index * tile : (index + 1) * tile]
        else:
            bias_ref[row] = bias.astype(BF16)

    for_groups(step, 4, lambda at, count: interleave(lambda i: stages(at + i), count, 2))

    if direct:

        @pl.when(pl.program_id(0) == pl.num_programs(0) - 1)
        def _():
            tiles, _, tile = lines_ref.shape
            for index in range(tiles):
                lines = lines_ref[index].reshape(bias_ref.shape[:2] + (tile,))
                bias_ref[:, :, index * tile : (index + 1) * tile] = lines.astype(BF16)


def whole_spec(array):
    return pl.BlockSpec(array.shape, lambda i: (0,) * len(array.shape))


def forward_rows(start, rows, pair, w_in, w_out, w_bias, prepared):
    crop, channels = pair.shape[1:]
    layers, heads, _ = w_bias.shape
    lanes = layers * heads
    step = row_step(rows)
    first_step = start // step
    positions = rows * crop
    width = w_out.shape[0]
    direct = is_direct(rows, crop)
    first = prepared is None
    line_shape = (heads * layers, rows, crop) if direct else (rows, lanes, crop)
    shapes = [jax.ShapeDtypeStruct(line_shape, BF16)]
    out_specs = [
        whole_spec(shapes[0])
        if direct
        else pl.BlockSpec((step, lanes, crop), lambda i: (i, 0, 0))
    ]
    if first:
        operands = [pair, w_bias, w_in, w_out]
        for shape in (w_in.shape[::-1], w_out.shape[::-1], w_in.shape, w_out.shape):
            shapes.append(jax.ShapeDtypeStruct(shape, BF16))
            out_specs.append(whole_spec(shapes[-1]))
    else:
        operands = [pair, w_bias, *prepared[:2]]
    return pl.pallas_call(
        functools.partial(forward_kernel, direct, first),
        grid=(rows // step,),
        in_specs=[pl.BlockSpec((step, crop, channels), lambda i: (first_step + i, 0, 0))]
        + [whole_spec(array) for array in operands[1:]],
        out_specs=out_specs,
        out_shape=shapes,
        scratch_shapes=[
            pltpu.VMEM((crop // 128, lanes * rows, 128) if direct else (1, 8, 128), F32),
        ],
        compiler_params=pltpu.CompilerParams(vmem_limit_bytes=56 * 2**20),
        cost_estimate=pl.CostEstimate(
            flops=6 * positions * channels * (3 * width + lanes),
            bytes_accessed=positions * (channels + lanes) * 2,
            transcendentals=positions * width,
        ),
        name="pair_forward",
    )(*operands)


def backward_kernel(
    first,
    last,
    direct,
    pair_ref,
    d_bias_ref,
    w_bias_ref,
    w_in_t_ref,
    w_out_t_ref,
    w_back_ref,
    w_half_ref,
    *refs,
):
    if first:
        pair_grad_ref, sums_ref = refs[:2]
    else:
        before_ref, _, pair_grad_ref, sums_ref = refs[:4]
    lines_ref = refs[-1]
    width = w_half_ref.shape[0]
    layers, heads, channels = w_bias_ref.shape
    lanes = layers * heads
    piece = split_width(width)
    step = pair_ref.shape[0]
    first_row = pl.program_id(0) * step

    @pl.when(pl.program_id(0) == 0)
    def _():
        if first:
            sums_ref[...] = jnp.zeros_like(sums_ref)
        else:
            sums_ref[...] = before_ref[...]
        if direct:
            tiles, total, tile = lines_ref.shape
            for index in range(tiles):
                lines = d_bias_ref[:, :, index * tile : (index + 1) * tile].astype(F32)
                lines_ref[index] = lines.reshape(total, tile)

    def read_lines(row):
        if not direct:
            return d_bias_ref[row]
        tiles, total, _ = lines_ref.shape
        rows = total // lanes
        found = []
        for layer in range(layers):
            at = pl.ds(layer * rows + first_row + row, heads, stride=layers * rows)
            found.append(jnp.concatenate([lines_ref[index, at, :] for index in range(tiles)], 1))
        return jnp.concatenate(found, 0).astype(BF16)

    def stages(row):
        pair_float = pair_ref[row].T.astype(F32)
        normed_float, inv_in = normalize(pair_float)
        normed_in = normed_float.astype(BF16)
        yield True
        lifted = pair_float
        kept = []
        for at in range(0, width, piece):
            half_gate = mm(w_in_t_ref[at : at + piece, :], normed_in)
            up_in = mm(w_in_t_ref[width + at : width + at + piece, :], normed_in)
            yield True
            one_plus = 1.0 + jnp.tanh(half_gate)
            silu = half_gate * one_plus
            hidden = (silu * up_in).astype(BF16)
            slope = one_plus * (1.0 + half_gate * (2.0 - one_plus)) * up_in
            kept.append((silu, slope, hidden))
            lifted = lifted + mm(w_out_t_ref[:, at : at + piece], hidden)
            yield True
        out_float, inv_out = normalize(lifted)
        normed_out = out_float.astype(BF16)
        yield True
        d_bias = read_lines(row)
        d_normed = mm(w_bias_ref[...].reshape(lanes, channels), d_bias, 0, 0)
        sums_ref[3 * width :, :] += mm(d_bias, normed_out, 1, 1)
        d_lifted = norm_back(out_float, inv_out, d_normed)
        lifted_half = d_lifted.astype(BF16)
        yield True
        d_normed_in = None
        for index, (silu, slope, hidden) in enumerate(kept):
            at = index * piece
            cols = slice(at, at + piece)
            up_cols = slice(width + at, width + at + piece)
            d_hidden = mm(w_half_ref[cols, :], lifted_half)
            sums_ref[2 * width + at : 2 * width + at + piece, :] += mm(hidden, lifted_half, 1, 1)
            yield True
            d_gate = (d_hidden * slope).astype(BF16)
            d_up = (d_hidden * silu).astype(BF16)
            part = mm(w_back_ref[:, cols], d_gate)
            sums_ref[cols, :] += mm(d_gate, normed_in, 1, 1)
            part = part + mm(w_back_ref[:, up_cols], d_up)
            sums_ref[up_cols, :] += mm(d_up, normed_in, 1, 1)
            d_normed_in = part if d_normed_in is None else d_normed_in + part
            yield True
        pair_grad = d_lifted + norm_back(normed_float, inv_in, d_normed_in)
        pair_grad_ref[row] = pair_grad.astype(BF16).T

    for_groups(step, 4, lambda at, count: interleave(lambda i: stages(at + i), count, 3))

    if last:
        packed_ref = refs[-2]

        @pl.when(pl.program_id(0) == pl.num_programs(0) - 1)
        def _():
            done = sums_ref.shape[0]
            packed_ref[:done, :] = sums_ref[...].astype(BF16)
            packed_ref[width : 2 * width, :] = (2.0 * sums_ref[width : 2 * width, :]).astype(BF16)
            packed_ref[done:, :] = jnp.zeros((packed_ref.shape[0] - done, packed_ref.shape[1]), BF16)


def backward_rows(start, rows, packed_rows, pair, d_bias, w_bias, prepared, state):
    crop, channels = pair.shape[1:]
    layers, heads, _ = w_bias.shape
    lanes = layers * heads
    width = prepared[3].shape[0]
    step = row_step(rows)
    first_step = start // step
    positions = rows * crop
    first, last = start == 0, start + rows == pair.shape[0]
    direct = is_direct(rows, crop)
    pair_spec = pl.BlockSpec((step, crop, channels), lambda i: (first_step + i, 0, 0))
    line_spec = whole_spec(d_bias) if direct else pl.BlockSpec((step, lanes, crop), lambda i: (i, 0, 0))
    operands = [pair, d_bias, w_bias, *prepared]
    in_specs = [pair_spec, line_spec] + [whole_spec(array) for array in operands[2:]]
    aliases = {}
    if not first:
        pair_grad, sums = state
        operands += [sums, pair_grad]
        in_specs += [whole_spec(sums), pl.BlockSpec(memory_space=pl.ANY)]
        aliases = {len(operands) - 1: 0}
    shapes = [
        jax.ShapeDtypeStruct(pair.shape, BF16),
        jax.ShapeDtypeStruct((3 * width + lanes, channels), F32),
    ]
    out_specs = [pair_spec, whole_spec(shapes[1])]
    if last:
        shapes.append(jax.ShapeDtypeStruct((packed_rows, channels), BF16))
        out_specs.append(whole_spec(shapes[2]))
    return pl.pallas_call(
        functools.partial(backward_kernel, first, last, direct),
        grid=(rows // step,),
        in_specs=in_specs,
        out_specs=out_specs,
        out_shape=shapes,
        input_output_aliases=aliases,
        scratch_shapes=[
            pltpu.VMEM((crop // 128, lanes * rows, 128) if direct else (1, 8, 128), F32),
        ],
        compiler_params=pltpu.CompilerParams(vmem_limit_bytes=56 * 2**20),
        cost_estimate=pl.CostEstimate(
            flops=6 * positions * channels * (9 * width + 2 * lanes),
            bytes_accessed=positions * (2 * channels + lanes) * 2,
            transcendentals=positions * width,
        ),
        name="pair_backward",
    )(*operands)


def attend_kernel(
    first, last, weight_ref, bias_ref, valid_ref, q_ref, k_ref, v_ref, g_ref, *refs
):
    if first:
        dq_ref, dk_ref, dv_ref, d_bias_ref = refs
    else:
        dk_before_ref, dv_before_ref, dq_ref, dk_ref, dv_ref, d_bias_ref = refs
    samples, depth = q_ref.shape[1:3]
    sources, _, rows, crop = bias_ref.shape
    scaling = 1.0 / math.sqrt(depth)
    bias = bias_ref[:, 0].astype(F32).reshape(sources * rows, crop)
    valid = valid_ref[...] > 0
    total = jnp.zeros_like(bias)
    for s in range(samples):
        query, key, value = q_ref[0, s], k_ref[0, s], v_ref[0, s]
        grad_half = (weight_ref[s] * g_ref[0, s].astype(F32)).astype(BF16)
        scores = mm(query, key, 0, 0) * scaling + bias
        scores = jnp.where(valid, scores, masked_score)
        exp_scores = jnp.exp(scores - jnp.max(scores, -1, keepdims=True))
        attention = exp_scores / jnp.sum(exp_scores, -1, keepdims=True)
        d_attention = mm(grad_half, value, 0, 0)
        d_scores = attention * (
            d_attention - jnp.sum(attention * d_attention, -1, keepdims=True)
        )
        total = total + d_scores
        scores_half = d_scores.astype(BF16)
        d_value = mm(grad_half, attention.astype(BF16))
        d_key = mm(query, scores_half)
        dq_ref[0, s] = (mm(key, scores_half, 1, 1) * scaling).astype(BF16)
        if not first:
            d_value = d_value + dv_before_ref[0, s]
            d_key = d_key + dk_before_ref[0, s]
        if last:
            d_key = d_key * scaling
        dv_ref[0, s] = d_value.astype(dv_ref.dtype)
        dk_ref[0, s] = d_key.astype(dk_ref.dtype)
    d_bias_ref[:, 0] = total.astype(BF16).reshape(sources, rows, crop)


def attend_rows(first, last, weights, bias, valid, query, key, value, grad, state):
    sources, layers, rows, crop = bias.shape
    samples, depth, row_count = query.shape[1:]
    vec = lambda shape: pl.BlockSpec((1,) + shape[1:], lambda l: (l, 0, 0, 0))
    plane = pl.BlockSpec((sources, 1, rows, crop), lambda l: (0, l, 0, 0))
    in_specs = [
        pl.BlockSpec(memory_space=pltpu.SMEM),
        plane,
        pl.BlockSpec(valid.shape, lambda l: (0, 0)),
        vec(query.shape),
        vec(key.shape),
        vec(value.shape),
        vec(grad.shape),
    ]
    operands = [weights, bias, valid, query, key, value, grad]
    if not first:
        operands += list(state)
        in_specs += [vec(key.shape), vec(value.shape)]
    kind = BF16 if last else F32
    return pl.pallas_call(
        functools.partial(attend_kernel, first, last),
        grid=(layers,),
        in_specs=in_specs,
        out_specs=[vec(query.shape), vec(key.shape), vec(value.shape), plane],
        out_shape=[
            jax.ShapeDtypeStruct(query.shape, BF16),
            jax.ShapeDtypeStruct(key.shape, kind),
            jax.ShapeDtypeStruct(value.shape, kind),
            jax.ShapeDtypeStruct(bias.shape, BF16),
        ],
        compiler_params=pltpu.CompilerParams(vmem_limit_bytes=48 * 2**20),
        cost_estimate=pl.CostEstimate(
            flops=200 * layers * samples * depth * row_count * crop,
            bytes_accessed=layers * crop * (4 * row_count + 12 * samples * depth),
            transcendentals=layers * samples * row_count * crop,
        ),
        name="attention_backward",
    )(*operands)


def swap(array, teams=None):
    return lax.all_to_all(
        array, "tok", split_axis=0, concat_axis=0, tiled=True, axis_index_groups=teams
    )


def sum_over_devices(array):
    devices = lax.axis_size("tok")
    parity = lax.axis_index("tok") % 2
    across = [(index, index ^ 1) for index in range(devices)]
    teams = [list(range(odd, devices, 2)) for odd in range(2)]
    total, channels = array.shape
    share = total // devices
    halves = array.reshape(2, total // 2, channels)
    theirs = lax.ppermute(lax.dynamic_index_in_dim(halves, 1 - parity, 0, False), "tok", across)
    mine = lax.dynamic_index_in_dim(halves, parity, 0, False)
    mine = (mine.astype(F32) + theirs.astype(F32)).astype(BF16)
    parts = swap(mine.reshape(devices // 2, share, channels), teams)
    summed = jnp.sum(parts.astype(F32), 0).astype(BF16)
    copies = jnp.broadcast_to(summed[None], (devices // 2, share, channels))
    mine = swap(copies, teams).reshape(total // 2, channels)
    theirs = lax.ppermute(mine, "tok", across)
    even = parity == 0
    summed = jnp.concatenate([jnp.where(even, mine, theirs), jnp.where(even, theirs, mine)], 0)
    return summed.astype(F32)


def body(
    pair_states,
    weight_in,
    weight_out,
    weight_bias,
    key_mask,
    noise_level,
    query_states,
    key_states,
    value_states,
    output_grad,
):
    row_count, crop, channels = pair_states.shape
    layers, _, heads = weight_bias.shape
    width = weight_out.shape[0]
    devices = lax.axis_size("tok")
    groups = devices // heads
    samples, depth = query_states.shape[2:4]
    lanes = heads * layers
    sizes = [row_count]
    if row_count % 32 == 0:
        sizes = [row_count // 4, row_count - row_count // 4]
    starts = [sum(sizes[:index]) for index in range(len(sizes))]
    w_bias = jnp.transpose(weight_bias, (0, 2, 1))

    group = lax.axis_index("tok") // heads
    weights = sample_weight(lax.dynamic_slice_in_dim(noise_level, group * samples, samples))
    valid = key_mask[None, :]

    def take_rows(array, start, rows):
        cut = array[:, 0].reshape(layers, samples, depth, devices, row_count)
        cut = cut[..., start : start + rows]
        return cut.reshape(layers, samples, depth, devices * rows)

    arrived = []
    prepared = None
    for start, rows in zip(starts, sizes):
        bias, *made = forward_rows(
            start, rows, pair_states, weight_in, weight_out, w_bias, prepared
        )
        prepared = prepared or made
        if is_direct(rows, crop):
            bias = bias.reshape(heads, layers, rows, crop)
        else:
            bias = jnp.transpose(bias.reshape(rows, layers, heads, crop), (2, 1, 0, 3))
        if groups > 1:
            bias = jnp.tile(bias, (groups, 1, 1, 1))
        arrived.append(swap(bias))

    returned = []
    d_queries = []
    state = None
    for start, rows, bias in zip(starts, sizes, arrived):
        direct = is_direct(rows, crop)
        if not direct:
            bias = jnp.transpose(bias, (1, 0, 2, 3)).reshape(1, layers, devices * rows, crop)
        d_query, d_key, d_value, d_bias = attend_rows(
            start == 0,
            start + rows == row_count,
            weights,
            bias,
            valid,
            take_rows(query_states, start, rows),
            key_states[:, 0],
            value_states[:, 0],
            take_rows(output_grad, start, rows),
            state,
        )
        state = (d_key, d_value)
        d_queries.append(d_query.reshape(layers, samples, depth, devices, rows))
        if not direct:
            d_bias = jnp.transpose(d_bias.reshape(layers, devices, rows, crop), (1, 0, 2, 3))
        returned.append(swap(d_bias))

    sum_rows = 3 * width + lanes
    packed_rows = 8 * devices * -(-sum_rows // (8 * devices))
    pair_state = None
    for start, rows, d_bias in zip(starts, sizes, returned):
        if groups > 1:
            d_bias = d_bias.reshape(groups, heads, layers, rows, crop).astype(F32)
            d_bias = jnp.sum(d_bias, 0).astype(BF16)
        if is_direct(rows, crop):
            d_bias = d_bias.reshape(lanes, rows, crop)
        else:
            d_bias = jnp.transpose(d_bias, (2, 1, 0, 3)).reshape(rows, lanes, crop)
        pair_state = backward_rows(
            start,
            rows,
            packed_rows,
            pair_states,
            d_bias,
            w_bias,
            prepared,
            pair_state and pair_state[:2],
        )
    pair_grad, _, packed = pair_state

    summed = sum_over_devices(packed)
    grad_in = summed[: 2 * width].T
    grad_out = summed[2 * width : 3 * width]
    grad_bias = summed[3 * width : sum_rows].reshape(layers, heads, channels)
    grad_bias = jnp.transpose(grad_bias, (0, 2, 1))

    d_query = jnp.concatenate(d_queries, -1).reshape(query_states.shape)
    return (
        pair_grad,
        d_query,
        d_key[:, None],
        d_value[:, None],
        grad_in,
        grad_out,
        grad_bias,
    )


def solution(mesh):
    in_specs = (
        P(("job", "tok"), None, None),
        P(),
        P(),
        P(),
        P("job"),
        P("job"),
        P(None, "tok", "job", None, None),
        P(None, "tok", "job", None, None),
        P(None, "tok", "job", None, None),
        P(None, "tok", "job", None, None),
    )
    out_specs = (
        P(("job", "tok"), None, None),
        P(None, "tok", "job", None, None),
        P(None, "tok", "job", None, None),
        P(None, "tok", "job", None, None),
        P("job", None),
        P("job", None),
        P("job", None, None),
    )
    return jax.shard_map(body, mesh=mesh, in_specs=in_specs, out_specs=out_specs, check_vma=False)
```

```python
import functools
import math

import jax
import jax.numpy as jnp
from jax import lax
from jax.experimental import pallas as pl
from jax.experimental.pallas import tpu as pltpu
from jax.sharding import PartitionSpec as P

LEVELS = 200


sigma_high = 160.0
sigma_low = 0.0004
sigma_data = 16.0
rho_power = 7.0
epsilon = 1e-05
masked_score = -1000000000.0

F32 = jnp.float32
BF16 = jnp.bfloat16


def sample_weight(levels):
    level = levels.astype(jnp.float32)
    top_root = sigma_high ** (1.0 / rho_power)
    low_root = sigma_low ** (1.0 / rho_power)
    sigma_level = (top_root + level / (LEVELS - 1) * (low_root - top_root)) ** rho_power
    return (sigma_level * sigma_level + sigma_data * sigma_data) / (sigma_level + sigma_data) ** 2


def mm(left, right, left_dim=1, right_dim=0):
    return lax.dot_general(
        left, right, (((left_dim,), (right_dim,)), ((), ())), preferred_element_type=F32
    )


def normalize(inputs):
    centered = inputs - jnp.mean(inputs, 0, keepdims=True)
    inv_std = lax.rsqrt(jnp.mean(centered * centered, 0, keepdims=True) + epsilon)
    return centered * inv_std, inv_std


def norm_back(normed, inv_std, upstream):
    return inv_std * (
        upstream
        - jnp.mean(upstream, 0, keepdims=True)
        - normed * jnp.mean(upstream * normed, 0, keepdims=True)
    )


def split_width(width):
    return 256 if width % 256 == 0 else width


def interleave(make_stages, count, lag):
    rows = [make_stages(index) for index in range(count)]
    running = []
    clock = 0
    while rows or running:
        if rows and clock % lag == 0:
            running.append(rows.pop(0))
        running = [row for row in running if next(row, None) is not None]
        clock += 1


def for_groups(count, group, one_group):
    group = math.gcd(count, group)

    def step(at, carry):
        one_group(at * group, group)
        return carry

    if count == group:
        step(0, 0)
    else:
        lax.fori_loop(0, count // group, step, 0)


def row_step(rows):
    return math.gcd(rows, 8 if rows > 8 else 4)


def is_direct(rows, crop):
    return rows % 8 == 0 and crop % 128 == 0


def forward_kernel(direct, first, pair_ref, w_bias_ref, *refs):
    if first:
        w_in_ref, w_out_ref, bias_ref, w_in_t_ref, w_out_t_ref = refs[:-1]
    else:
        w_in_t_ref, w_out_t_ref, bias_ref = refs[:-1]
    lines_ref = refs[-1]
    width = w_out_t_ref.shape[1]
    layers, heads, channels = w_bias_ref.shape
    piece = split_width(width)
    step = pair_ref.shape[0]
    first_row = pl.program_id(0) * step

    if first:

        @pl.when(pl.program_id(0) == 0)
        def _():
            w_in_t = w_in_ref[...].T
            w_in_t_ref[:width, :] = w_in_t[:width] * 0.5
            w_in_t_ref[width:, :] = w_in_t[width:]
            w_out_t_ref[...] = w_out_ref[...].T

    def stages(row):
        pair_float = pair_ref[row].T.astype(F32)
        normed_in = normalize(pair_float)[0].astype(BF16)
        yield True
        lifted = pair_float
        for at in range(0, width, piece):
            half_gate = mm(w_in_t_ref[at : at + piece, :], normed_in)
            up_in = mm(w_in_t_ref[width + at : width + at + piece, :], normed_in)
            yield True
            hidden = (half_gate * (1.0 + jnp.tanh(half_gate)) * up_in).astype(BF16)
            lifted = lifted + mm(w_out_t_ref[:, at : at + piece], hidden)
            yield True
        normed_out = normalize(lifted)[0].astype(BF16)
        yield True
        bias = mm(w_bias_ref[...].reshape(layers * heads, channels), normed_out)
        if direct:
            tiles, total, tile = lines_ref.shape
            rows = total // (layers * heads)
            for layer in range(layers):
                at = pl.ds(layer * rows + first_row + row, heads, stride=layers * rows)
                lines = bias[layer * heads : (layer + 1) * heads]
                for index in range(tiles):
                    lines_ref[index, at, :] = lines[:, index * tile : (index + 1) * tile]
        else:
            bias_ref[row] = bias.astype(BF16)

    for_groups(step, 4, lambda at, count: interleave(lambda i: stages(at + i), count, 3))

    if direct:

        @pl.when(pl.program_id(0) == pl.num_programs(0) - 1)
        def _():
            tiles, _, tile = lines_ref.shape
            for index in range(tiles):
                lines = lines_ref[index].reshape(bias_ref.shape[:2] + (tile,))
                bias_ref[:, :, index * tile : (index + 1) * tile] = lines.astype(BF16)


def whole_spec(array):
    return pl.BlockSpec(array.shape, lambda i: (0,) * len(array.shape))


def forward_rows(start, rows, pair, w_in, w_out, w_bias, prepared):
    crop, channels = pair.shape[1:]
    layers, heads, _ = w_bias.shape
    lanes = layers * heads
    step = row_step(rows)
    first_step = start // step
    positions = rows * crop
    width = w_out.shape[0]
    direct = is_direct(rows, crop)
    first = prepared is None
    line_shape = (heads * layers, rows, crop) if direct else (rows, lanes, crop)
    shapes = [jax.ShapeDtypeStruct(line_shape, BF16)]
    out_specs = [
        whole_spec(shapes[0])
        if direct
        else pl.BlockSpec((step, lanes, crop), lambda i: (i, 0, 0))
    ]
    if first:
        operands = [pair, w_bias, w_in, w_out]
        for shape in (w_in.shape[::-1], w_out.shape[::-1]):
            shapes.append(jax.ShapeDtypeStruct(shape, BF16))
            out_specs.append(whole_spec(shapes[-1]))
    else:
        operands = [pair, w_bias, *prepared]
    return pl.pallas_call(
        functools.partial(forward_kernel, direct, first),
        grid=(rows // step,),
        in_specs=[pl.BlockSpec((step, crop, channels), lambda i: (first_step + i, 0, 0))]
        + [whole_spec(array) for array in operands[1:]],
        out_specs=out_specs,
        out_shape=shapes,
        scratch_shapes=[
            pltpu.VMEM((crop // 128, lanes * rows, 128) if direct else (1, 8, 128), F32),
        ],
        compiler_params=pltpu.CompilerParams(vmem_limit_bytes=56 * 2**20),
        cost_estimate=pl.CostEstimate(
            flops=6 * positions * channels * (3 * width + lanes),
            bytes_accessed=positions * (channels + lanes) * 2,
            transcendentals=positions * width,
        ),
        name="pair_forward",
    )(*operands)


def backward_kernel(
    first,
    last,
    sums,
    grads,
    direct,
    base,
    pair_ref,
    d_bias_ref,
    w_bias_ref,
    w_in_t_ref,
    w_out_t_ref,
    w_back_ref,
    w_half_ref,
    *refs,
):
    outs = list(refs[:-1])
    if sums and not first:
        before_ref = outs.pop(0)
    if not first:
        outs.pop(0)
    if not sums:
        outs.pop(0)
    pair_grad_ref = outs.pop(0)
    sums_ref = outs.pop(0) if sums else None
    lines_ref = refs[-1]
    width = w_half_ref.shape[0]
    layers, heads, channels = w_bias_ref.shape
    lanes = layers * heads
    piece = split_width(width)
    step = pair_ref.shape[0]
    first_row = base + pl.program_id(0) * step

    @pl.when(pl.program_id(0) == 0)
    def _():
        if sums and first:
            sums_ref[...] = jnp.zeros_like(sums_ref)
        elif sums:
            sums_ref[...] = before_ref[...]
        if direct:
            tiles, total, tile = lines_ref.shape
            for index in range(tiles):
                lines = d_bias_ref[:, :, index * tile : (index + 1) * tile].astype(F32)
                lines_ref[index] = lines.reshape(total, tile)

    def read_lines(row):
        if not direct:
            return d_bias_ref[row]
        tiles, total, _ = lines_ref.shape
        rows = total // lanes
        found = []
        for layer in range(layers):
            at = pl.ds(layer * rows + first_row + row, heads, stride=layers * rows)
            found.append(jnp.concatenate([lines_ref[index, at, :] for index in range(tiles)], 1))
        return jnp.concatenate(found, 0).astype(BF16)

    def stages(row):
        pair_float = pair_ref[row].T.astype(F32)
        normed_float, inv_in = normalize(pair_float)
        normed_in = normed_float.astype(BF16)
        yield True
        lifted = pair_float
        kept = []
        for at in range(0, width, piece):
            half_gate = mm(w_in_t_ref[at : at + piece, :], normed_in)
            up_in = mm(w_in_t_ref[width + at : width + at + piece, :], normed_in)
            yield True
            one_plus = 1.0 + jnp.tanh(half_gate)
            silu = half_gate * one_plus
            hidden = (silu * up_in).astype(BF16)
            slope = one_plus * (1.0 + half_gate * (2.0 - one_plus)) * up_in
            kept.append((silu, slope, hidden))
            lifted = lifted + mm(w_out_t_ref[:, at : at + piece], hidden)
            yield True
        out_float, inv_out = normalize(lifted)
        normed_out = out_float.astype(BF16)
        yield True
        d_bias = read_lines(row)
        d_normed = mm(w_bias_ref[...].reshape(lanes, channels), d_bias, 0, 0)
        if sums:
            sums_ref[3 * width :, :] += mm(d_bias, normed_out, 1, 1)
        d_lifted = norm_back(out_float, inv_out, d_normed)
        lifted_half = d_lifted.astype(BF16)
        yield True
        d_normed_in = None
        for index, (silu, slope, hidden) in enumerate(kept):
            at = index * piece
            cols = slice(at, at + piece)
            up_cols = slice(width + at, width + at + piece)
            d_hidden = mm(w_half_ref[cols, :], lifted_half)
            if sums:
                out_cols = slice(2 * width + at, 2 * width + at + piece)
                sums_ref[out_cols, :] += mm(hidden, lifted_half, 1, 1)
            yield True
            d_gate = (d_hidden * slope).astype(BF16)
            d_up = (d_hidden * silu).astype(BF16)
            if sums:
                sums_ref[cols, :] += mm(d_gate, normed_in, 1, 1)
                sums_ref[up_cols, :] += mm(d_up, normed_in, 1, 1)
            if grads:
                part = mm(w_back_ref[:, cols], d_gate) + mm(w_back_ref[:, up_cols], d_up)
                d_normed_in = part if d_normed_in is None else d_normed_in + part
            yield True
        if grads:
            pair_grad = d_lifted + norm_back(normed_float, inv_in, d_normed_in)
            pair_grad_ref[row] = pair_grad.astype(BF16).T

    for_groups(step, 4, lambda at, count: interleave(lambda i: stages(at + i), count, 5))

    if last:
        packed_ref = outs.pop(0)

        @pl.when(pl.program_id(0) == pl.num_programs(0) - 1)
        def _():
            done = sums_ref.shape[0]
            packed_ref[:done, :] = sums_ref[...].astype(BF16)
            packed_ref[width : 2 * width, :] = (2.0 * sums_ref[width : 2 * width, :]).astype(BF16)
            packed_ref[done:, :] = jnp.zeros((packed_ref.shape[0] - done, packed_ref.shape[1]), BF16)


def backward_rows(
    start,
    rows,
    base,
    direct,
    packed_rows,
    pair,
    d_bias,
    w_bias,
    prepared,
    state,
    grads=True,
    after=None,
):
    crop, channels = pair.shape[1:]
    layers, heads, _ = w_bias.shape
    lanes = layers * heads
    width = prepared[3].shape[0]
    step = row_step(rows)
    first_step = start // step
    positions = rows * crop
    sums = after is None
    first = start == 0
    last = sums and start + rows == pair.shape[0]
    pair_spec = pl.BlockSpec((step, crop, channels), lambda i: (first_step + i, 0, 0))
    line_spec = whole_spec(d_bias) if direct else pl.BlockSpec((step, lanes, crop), lambda i: (i, 0, 0))
    held_spec = pl.BlockSpec(memory_space=pl.ANY)
    operands = [pair, d_bias, w_bias, *prepared]
    in_specs = [pair_spec, line_spec] + [whole_spec(array) for array in operands[2:]]
    aliases = {}
    if sums and not first:
        operands.append(state[1])
        in_specs.append(whole_spec(state[1]))
    if not first:
        aliases = {len(operands): 0}
        operands.append(state[0])
        in_specs.append(held_spec)
    if not sums:
        operands.append(after)
        in_specs.append(held_spec)
    shapes = [jax.ShapeDtypeStruct(pair.shape, BF16)]
    out_specs = [pair_spec if grads else held_spec]
    if sums:
        shapes.append(jax.ShapeDtypeStruct((3 * width + lanes, channels), F32))
        out_specs.append(whole_spec(shapes[-1]))
    if last:
        shapes.append(jax.ShapeDtypeStruct((packed_rows, channels), BF16))
        out_specs.append(whole_spec(shapes[-1]))
    return pl.pallas_call(
        functools.partial(backward_kernel, first, last, sums, grads, direct, base),
        grid=(rows // step,),
        in_specs=in_specs,
        out_specs=out_specs,
        out_shape=shapes,
        input_output_aliases=aliases,
        scratch_shapes=[
            pltpu.VMEM((crop // 128, lanes * d_bias.shape[1], 128) if direct else (1, 8, 128), F32),
        ],
        compiler_params=pltpu.CompilerParams(vmem_limit_bytes=56 * 2**20),
        cost_estimate=pl.CostEstimate(
            flops=6 * positions * channels * (9 * width + 2 * lanes),
            bytes_accessed=positions * (2 * channels + lanes) * 2,
            transcendentals=positions * width,
        ),
        name="pair_backward" if sums else "pair_grad_rows",
    )(*operands)


def attend_kernel(
    first, last, weight_ref, bias_ref, valid_ref, q_ref, k_ref, v_ref, g_ref, *refs
):
    if first:
        dq_ref, dk_ref, dv_ref, d_bias_ref = refs
    else:
        dk_before_ref, dv_before_ref, dq_ref, dk_ref, dv_ref, d_bias_ref = refs
    samples, depth = q_ref.shape[1:3]
    sources, _, rows, crop = bias_ref.shape
    scaling = 1.0 / math.sqrt(depth)
    bias = bias_ref[:, 0].astype(F32).reshape(sources * rows, crop)
    valid = valid_ref[...] > 0
    total = jnp.zeros_like(bias)
    for s in range(samples):
        query, key, value = q_ref[0, s], k_ref[0, s], v_ref[0, s]
        grad_half = (weight_ref[s] * g_ref[0, s].astype(F32)).astype(BF16)
        scores = mm(query, key, 0, 0) * scaling + bias
        scores = jnp.where(valid, scores, masked_score)
        exp_scores = jnp.exp(scores - jnp.max(scores, -1, keepdims=True))
        attention = exp_scores / jnp.sum(exp_scores, -1, keepdims=True)
        d_attention = mm(grad_half, value, 0, 0)
        d_scores = attention * (
            d_attention - jnp.sum(attention * d_attention, -1, keepdims=True)
        )
        total = total + d_scores
        scores_half = d_scores.astype(BF16)
        d_value = mm(grad_half, attention.astype(BF16))
        d_key = mm(query, scores_half)
        dq_ref[0, s] = (mm(key, scores_half, 1, 1) * scaling).astype(BF16)
        if not first:
            d_value = d_value + dv_before_ref[0, s]
            d_key = d_key + dk_before_ref[0, s]
        if last:
            d_key = d_key * scaling
        dv_ref[0, s] = d_value.astype(dv_ref.dtype)
        dk_ref[0, s] = d_key.astype(dk_ref.dtype)
    d_bias_ref[:, 0] = total.astype(BF16).reshape(sources, rows, crop)


def attend_rows(first, last, weights, bias, valid, query, key, value, grad, state):
    sources, layers, rows, crop = bias.shape
    samples, depth, row_count = query.shape[1:]
    vec = lambda shape: pl.BlockSpec((1,) + shape[1:], lambda l: (l, 0, 0, 0))
    plane = pl.BlockSpec((sources, 1, rows, crop), lambda l: (0, l, 0, 0))
    in_specs = [
        pl.BlockSpec(memory_space=pltpu.SMEM),
        plane,
        pl.BlockSpec(valid.shape, lambda l: (0, 0)),
        vec(query.shape),
        vec(key.shape),
        vec(value.shape),
        vec(grad.shape),
    ]
    operands = [weights, bias, valid, query, key, value, grad]
    if not first:
        operands += list(state)
        in_specs += [vec(key.shape), vec(value.shape)]
    kind = BF16 if last else F32
    return pl.pallas_call(
        functools.partial(attend_kernel, first, last),
        grid=(layers,),
        in_specs=in_specs,
        out_specs=[vec(query.shape), vec(key.shape), vec(value.shape), plane],
        out_shape=[
            jax.ShapeDtypeStruct(query.shape, BF16),
            jax.ShapeDtypeStruct(key.shape, kind),
            jax.ShapeDtypeStruct(value.shape, kind),
            jax.ShapeDtypeStruct(bias.shape, BF16),
        ],
        compiler_params=pltpu.CompilerParams(vmem_limit_bytes=48 * 2**20),
        cost_estimate=pl.CostEstimate(
            flops=200 * layers * samples * depth * row_count * crop,
            bytes_accessed=layers * crop * (4 * row_count + 12 * samples * depth),
            transcendentals=layers * samples * row_count * crop,
        ),
        name="attention_backward",
    )(*operands)


def swap(array, teams=None):
    return lax.all_to_all(
        array, "tok", split_axis=0, concat_axis=0, tiled=True, axis_index_groups=teams
    )


def sum_pairs(array):
    devices = lax.axis_size("tok")
    parity = lax.axis_index("tok") % 2
    across = [(index, index ^ 1) for index in range(devices)]
    halves = array.reshape(2, array.shape[0] // 2, array.shape[1])
    theirs = lax.ppermute(lax.dynamic_index_in_dim(halves, 1 - parity, 0, False), "tok", across)
    mine = lax.dynamic_index_in_dim(halves, parity, 0, False)
    return (mine.astype(F32) + theirs.astype(F32)).astype(BF16)


def sum_team(array):
    devices = lax.axis_size("tok")
    teams = [list(range(odd, devices, 2)) for odd in range(2)]
    members = devices // 2
    parts = swap(array.reshape(members, array.shape[0] // members, array.shape[1]), teams)
    return jnp.sum(parts.astype(F32), 0).astype(BF16)


def gather_shares(share):
    devices = lax.axis_size("tok")
    parts = swap(jnp.broadcast_to(share[None], (devices,) + share.shape))
    parts = parts.reshape(devices // 2, 2, *share.shape)
    parts = jnp.transpose(parts, (1, 0, 2, 3)).reshape(devices * share.shape[0], share.shape[1])
    return parts.astype(F32)


def body(
    pair_states,
    weight_in,
    weight_out,
    weight_bias,
    key_mask,
    noise_level,
    query_states,
    key_states,
    value_states,
    output_grad,
):
    row_count, crop, channels = pair_states.shape
    layers, _, heads = weight_bias.shape
    width = weight_out.shape[0]
    devices = lax.axis_size("tok")
    groups = devices // heads
    samples, depth = query_states.shape[2:4]
    lanes = heads * layers
    sizes = [row_count]
    if row_count % 16 == 0:
        sizes = [row_count // 2] * 2
    starts = [sum(sizes[:index]) for index in range(len(sizes))]
    w_bias = jnp.transpose(weight_bias, (0, 2, 1))

    group = lax.axis_index("tok") // heads
    weights = sample_weight(lax.dynamic_slice_in_dim(noise_level, group * samples, samples))
    valid = key_mask[None, :]

    def take_rows(array, start, rows):
        cut = array[:, 0].reshape(layers, samples, depth, devices, row_count)
        cut = cut[..., start : start + rows]
        return cut.reshape(layers, samples, depth, devices * rows)

    arrived = []
    prepared = None
    for start, rows in zip(starts, sizes):
        bias, *made = forward_rows(
            start, rows, pair_states, weight_in, weight_out, w_bias, prepared
        )
        prepared = prepared or made
        if is_direct(rows, crop):
            bias = bias.reshape(heads, layers, rows, crop)
        else:
            bias = jnp.transpose(bias.reshape(rows, layers, heads, crop), (2, 1, 0, 3))
        if groups > 1:
            bias = jnp.tile(bias, (groups, 1, 1, 1))
        arrived.append(swap(bias))

    returned = []
    d_queries = []
    state = None
    for start, rows, bias in zip(starts, sizes, arrived):
        direct = is_direct(rows, crop)
        if not direct:
            bias = jnp.transpose(bias, (1, 0, 2, 3)).reshape(1, layers, devices * rows, crop)
        d_query, d_key, d_value, d_bias = attend_rows(
            start == 0,
            start + rows == row_count,
            weights,
            bias,
            valid,
            take_rows(query_states, start, rows),
            key_states[:, 0],
            value_states[:, 0],
            take_rows(output_grad, start, rows),
            state,
        )
        state = (d_key, d_value)
        d_queries.append(d_query.reshape(layers, samples, depth, devices, rows))
        if not direct:
            d_bias = jnp.transpose(d_bias.reshape(layers, devices, rows, crop), (1, 0, 2, 3))
        returned.append(swap(d_bias))

    sum_rows = 3 * width + lanes
    packed_rows = 8 * devices * -(-sum_rows // (8 * devices))
    doubled = jnp.concatenate([jnp.ones((width,), BF16), jnp.full((width,), 2.0, BF16)])
    prepared = (*prepared, weight_in * doubled[None, :], weight_out * jnp.asarray(0.5, BF16))
    pair_state = None
    for start, rows, d_bias in zip(starts, sizes, returned):
        if groups > 1:
            d_bias = d_bias.reshape(groups, heads, layers, rows, crop).astype(F32)
            d_bias = jnp.sum(d_bias, 0).astype(BF16)
        if is_direct(rows, crop):
            d_bias = d_bias.reshape(lanes, rows, crop)
        else:
            d_bias = jnp.transpose(d_bias, (2, 1, 0, 3)).reshape(rows, lanes, crop)
        later = start > 0 and is_direct(rows, crop)
        make = functools.partial(
            backward_rows,
            direct=is_direct(rows, crop),
            packed_rows=packed_rows,
            pair=pair_states,
            d_bias=d_bias,
            w_bias=w_bias,
            prepared=prepared,
        )
        pair_state = make(start, rows, 0, state=pair_state, grads=not later)
    pair_grad, _, packed = pair_state

    half = rows // 2
    packed = sum_pairs(packed)
    if later:
        (pair_grad,) = make(start, half, 0, state=(pair_grad,), after=packed)
    share = sum_team(packed)
    if later:
        (pair_grad,) = make(start + half, half, half, state=(pair_grad,), after=share)
    summed = gather_shares(share)
    grad_in = summed[: 2 * width].T
    grad_out = summed[2 * width : 3 * width]
    grad_bias = summed[3 * width : sum_rows].reshape(layers, heads, channels)
    grad_bias = jnp.transpose(grad_bias, (0, 2, 1))

    d_query = jnp.concatenate(d_queries, -1).reshape(query_states.shape)
    return (
        pair_grad,
        d_query,
        d_key[:, None],
        d_value[:, None],
        grad_in,
        grad_out,
        grad_bias,
    )


def solution(mesh):
    in_specs = (
        P(("job", "tok"), None, None),
        P(),
        P(),
        P(),
        P("job"),
        P("job"),
        P(None, "tok", "job", None, None),
        P(None, "tok", "job", None, None),
        P(None, "tok", "job", None, None),
        P(None, "tok", "job", None, None),
    )
    out_specs = (
        P(("job", "tok"), None, None),
        P(None, "tok", "job", None, None),
        P(None, "tok", "job", None, None),
        P(None, "tok", "job", None, None),
        P("job", None),
        P("job", None),
        P("job", None, None),
    )
    return jax.shard_map(body, mesh=mesh, in_specs=in_specs, out_specs=out_specs, check_vma=False)
```

```python
import functools
import math

import jax
import jax.numpy as jnp
from jax import lax
from jax.experimental import pallas as pl
from jax.experimental.pallas import tpu as pltpu
from jax.sharding import PartitionSpec as P

LEVELS = 200


sigma_high = 160.0
sigma_low = 0.0004
sigma_data = 16.0
rho_power = 7.0
epsilon = 1e-05
masked_score = -1000000000.0

F32 = jnp.float32
BF16 = jnp.bfloat16


def sample_weight(levels):
    level = levels.astype(jnp.float32)
    top_root = sigma_high ** (1.0 / rho_power)
    low_root = sigma_low ** (1.0 / rho_power)
    sigma_level = (top_root + level / (LEVELS - 1) * (low_root - top_root)) ** rho_power
    return (sigma_level * sigma_level + sigma_data * sigma_data) / (sigma_level + sigma_data) ** 2


def mm(left, right, left_dim=1, right_dim=0):
    return lax.dot_general(
        left, right, (((left_dim,), (right_dim,)), ((), ())), preferred_element_type=F32
    )


def normalize(inputs):
    centered = inputs - jnp.mean(inputs, 0, keepdims=True)
    inv_std = lax.rsqrt(jnp.mean(centered * centered, 0, keepdims=True) + epsilon)
    return centered * inv_std, inv_std


def norm_back(normed, inv_std, upstream):
    return inv_std * (
        upstream
        - jnp.mean(upstream, 0, keepdims=True)
        - normed * jnp.mean(upstream * normed, 0, keepdims=True)
    )


def split_width(width):
    return 256 if width % 256 == 0 else width


def interleave(make_stages, count, lag):
    rows = [make_stages(index) for index in range(count)]
    running = []
    clock = 0
    while rows or running:
        while rows and clock >= lag * (count - len(rows)):
            running.append(rows.pop(0))
        running = [row for row in running if next(row, None) is not None]
        clock += 1


def for_groups(count, group, one_group):
    group = math.gcd(count, group)

    def step(at, carry):
        one_group(at * group, group)
        return carry

    if count == group:
        step(0, 0)
    else:
        lax.fori_loop(0, count // group, step, 0)


def row_step(rows):
    return math.gcd(rows, 8 if rows > 8 else 4)


def is_direct(rows, crop):
    return rows % 8 == 0 and crop % 128 == 0


def forward_kernel(direct, first, pair_ref, w_bias_ref, *refs):
    if first:
        w_in_ref, w_out_ref, bias_ref, w_in_t_ref, w_out_t_ref = refs[:-1]
    else:
        w_in_t_ref, w_out_t_ref, bias_ref = refs[:-1]
    lines_ref = refs[-1]
    width = w_out_t_ref.shape[1]
    layers, heads, channels = w_bias_ref.shape
    piece = split_width(width)
    step = pair_ref.shape[0]
    first_row = pl.program_id(0) * step

    if first:

        @pl.when(pl.program_id(0) == 0)
        def _():
            w_in_t = w_in_ref[...].T
            w_in_t_ref[:width, :] = w_in_t[:width] * 0.5
            w_in_t_ref[width:, :] = w_in_t[width:]
            w_out_t_ref[...] = w_out_ref[...].T

    def stages(row):
        pair_float = pair_ref[row].T.astype(F32)
        normed_in = normalize(pair_float)[0].astype(BF16)
        yield True
        lifted = pair_float
        for at in range(0, width, piece):
            half_gate = mm(w_in_t_ref[at : at + piece, :], normed_in)
            up_in = mm(w_in_t_ref[width + at : width + at + piece, :], normed_in)
            yield True
            hidden = (half_gate * (1.0 + jnp.tanh(half_gate)) * up_in).astype(BF16)
            lifted = lifted + mm(w_out_t_ref[:, at : at + piece], hidden)
            yield True
        normed_out = normalize(lifted)[0].astype(BF16)
        yield True
        bias = mm(w_bias_ref[...].reshape(layers * heads, channels), normed_out)
        if direct:
            tiles, total, tile = lines_ref.shape
            rows = total // (layers * heads)
            for layer in range(layers):
                at = pl.ds(layer * rows + first_row + row, heads, stride=layers * rows)
                lines = bias[layer * heads : (layer + 1) * heads]
                for index in range(tiles):
                    lines_ref[index, at, :] = lines[:, index * tile : (index + 1) * tile]
        else:
            bias_ref[row] = bias.astype(BF16)

    for_groups(step, 4, lambda at, count: interleave(lambda i: stages(at + i), count, 0))

    if direct:

        @pl.when(pl.program_id(0) == pl.num_programs(0) - 1)
        def _():
            tiles, _, tile = lines_ref.shape
            for index in range(tiles):
                lines = lines_ref[index].reshape(bias_ref.shape[:2] + (tile,))
                bias_ref[:, :, index * tile : (index + 1) * tile] = lines.astype(BF16)


def whole_spec(array):
    return pl.BlockSpec(array.shape, lambda i: (0,) * len(array.shape))


def forward_rows(start, rows, pair, w_in, w_out, w_bias, prepared):
    crop, channels = pair.shape[1:]
    layers, heads, _ = w_bias.shape
    lanes = layers * heads
    step = row_step(rows)
    first_step = start // step
    positions = rows * crop
    width = w_out.shape[0]
    direct = is_direct(rows, crop)
    first = prepared is None
    line_shape = (heads * layers, rows, crop) if direct else (rows, lanes, crop)
    shapes = [jax.ShapeDtypeStruct(line_shape, BF16)]
    out_specs = [
        whole_spec(shapes[0])
        if direct
        else pl.BlockSpec((step, lanes, crop), lambda i: (i, 0, 0))
    ]
    if first:
        operands = [pair, w_bias, w_in, w_out]
        for shape in (w_in.shape[::-1], w_out.shape[::-1]):
            shapes.append(jax.ShapeDtypeStruct(shape, BF16))
            out_specs.append(whole_spec(shapes[-1]))
    else:
        operands = [pair, w_bias, *prepared]
    return pl.pallas_call(
        functools.partial(forward_kernel, direct, first),
        grid=(rows // step,),
        in_specs=[pl.BlockSpec((step, crop, channels), lambda i: (first_step + i, 0, 0))]
        + [whole_spec(array) for array in operands[1:]],
        out_specs=out_specs,
        out_shape=shapes,
        scratch_shapes=[
            pltpu.VMEM((crop // 128, lanes * rows, 128) if direct else (1, 8, 128), F32),
        ],
        compiler_params=pltpu.CompilerParams(vmem_limit_bytes=56 * 2**20),
        cost_estimate=pl.CostEstimate(
            flops=6 * positions * channels * (3 * width + lanes),
            bytes_accessed=positions * (channels + lanes) * 2,
            transcendentals=positions * width,
        ),
        name="pair_forward",
    )(*operands)


def backward_kernel(
    first,
    last,
    sums,
    grads,
    direct,
    base,
    pair_ref,
    d_bias_ref,
    w_bias_ref,
    w_in_t_ref,
    w_out_t_ref,
    w_back_ref,
    w_half_ref,
    *refs,
):
    outs = list(refs[:-1])
    if sums and not first:
        before_ref = outs.pop(0)
    if not first:
        outs.pop(0)
    if not sums:
        outs.pop(0)
    pair_grad_ref = outs.pop(0)
    sums_ref = outs.pop(0) if sums else None
    lines_ref = refs[-1]
    width = w_half_ref.shape[0]
    layers, heads, channels = w_bias_ref.shape
    lanes = layers * heads
    piece = split_width(width)
    step = pair_ref.shape[0]
    first_row = base + pl.program_id(0) * step

    @pl.when(pl.program_id(0) == 0)
    def _():
        if sums and first:
            sums_ref[...] = jnp.zeros_like(sums_ref)
        elif sums:
            sums_ref[...] = before_ref[...]
        if direct:
            tiles, total, tile = lines_ref.shape
            for index in range(tiles):
                lines = d_bias_ref[:, :, index * tile : (index + 1) * tile].astype(F32)
                lines_ref[index] = lines.reshape(total, tile)

    def read_lines(row):
        if not direct:
            return d_bias_ref[row]
        tiles, total, _ = lines_ref.shape
        rows = total // lanes
        found = []
        for layer in range(layers):
            at = pl.ds(layer * rows + first_row + row, heads, stride=layers * rows)
            found.append(jnp.concatenate([lines_ref[index, at, :] for index in range(tiles)], 1))
        return jnp.concatenate(found, 0).astype(BF16)

    def stages(row):
        pair_float = pair_ref[row].T.astype(F32)
        normed_float, inv_in = normalize(pair_float)
        normed_in = normed_float.astype(BF16)
        yield True
        lifted = pair_float
        kept = []
        for at in range(0, width, piece):
            half_gate = mm(w_in_t_ref[at : at + piece, :], normed_in)
            up_in = mm(w_in_t_ref[width + at : width + at + piece, :], normed_in)
            yield True
            one_plus = 1.0 + jnp.tanh(half_gate)
            silu = half_gate * one_plus
            hidden = (silu * up_in).astype(BF16)
            slope = one_plus * (1.0 + half_gate * (2.0 - one_plus)) * up_in
            kept.append((silu, slope, hidden))
            lifted = lifted + mm(w_out_t_ref[:, at : at + piece], hidden)
            yield True
        out_float, inv_out = normalize(lifted)
        normed_out = out_float.astype(BF16)
        yield True
        d_bias = read_lines(row)
        d_normed = mm(w_bias_ref[...].reshape(lanes, channels), d_bias, 0, 0)
        if sums:
            sums_ref[3 * width :, :] += mm(d_bias, normed_out, 1, 1)
        d_lifted = norm_back(out_float, inv_out, d_normed)
        lifted_half = d_lifted.astype(BF16)
        yield True
        d_normed_in = None
        for index, (silu, slope, hidden) in enumerate(kept):
            at = index * piece
            cols = slice(at, at + piece)
            up_cols = slice(width + at, width + at + piece)
            d_hidden = mm(w_half_ref[cols, :], lifted_half)
            if sums:
                out_cols = slice(2 * width + at, 2 * width + at + piece)
                sums_ref[out_cols, :] += mm(hidden, lifted_half, 1, 1)
            yield True
            d_gate = (d_hidden * slope).astype(BF16)
            d_up = (d_hidden * silu).astype(BF16)
            if sums:
                sums_ref[cols, :] += mm(d_gate, normed_in, 1, 1)
                sums_ref[up_cols, :] += mm(d_up, normed_in, 1, 1)
            if grads:
                part = mm(w_back_ref[:, cols], d_gate) + mm(w_back_ref[:, up_cols], d_up)
                d_normed_in = part if d_normed_in is None else d_normed_in + part
            yield True
        if grads:
            pair_grad = d_lifted + norm_back(normed_float, inv_in, d_normed_in)
            pair_grad_ref[row] = pair_grad.astype(BF16).T

    for_groups(step, 4, lambda at, count: interleave(lambda i: stages(at + i), count, 2))

    if last:
        packed_ref = outs.pop(0)

        @pl.when(pl.program_id(0) == pl.num_programs(0) - 1)
        def _():
            done = sums_ref.shape[0]
            packed_ref[:done, :] = sums_ref[...].astype(BF16)
            packed_ref[width : 2 * width, :] = (2.0 * sums_ref[width : 2 * width, :]).astype(BF16)
            packed_ref[done:, :] = jnp.zeros((packed_ref.shape[0] - done, packed_ref.shape[1]), BF16)


def backward_rows(
    start,
    rows,
    base,
    direct,
    packed_rows,
    pair,
    d_bias,
    w_bias,
    prepared,
    state,
    grads=True,
    after=None,
):
    crop, channels = pair.shape[1:]
    layers, heads, _ = w_bias.shape
    lanes = layers * heads
    width = prepared[3].shape[0]
    step = row_step(rows)
    first_step = start // step
    positions = rows * crop
    sums = after is None
    first = start == 0
    last = sums and start + rows == pair.shape[0]
    pair_spec = pl.BlockSpec((step, crop, channels), lambda i: (first_step + i, 0, 0))
    line_spec = whole_spec(d_bias) if direct else pl.BlockSpec((step, lanes, crop), lambda i: (i, 0, 0))
    held_spec = pl.BlockSpec(memory_space=pl.ANY)
    operands = [pair, d_bias, w_bias, *prepared]
    in_specs = [pair_spec, line_spec] + [whole_spec(array) for array in operands[2:]]
    aliases = {}
    if sums and not first:
        operands.append(state[1])
        in_specs.append(whole_spec(state[1]))
    if not first:
        aliases = {len(operands): 0}
        operands.append(state[0])
        in_specs.append(held_spec)
    if not sums:
        operands.append(after)
        in_specs.append(held_spec)
    shapes = [jax.ShapeDtypeStruct(pair.shape, BF16)]
    out_specs = [pair_spec if grads else held_spec]
    if sums:
        shapes.append(jax.ShapeDtypeStruct((3 * width + lanes, channels), F32))
        out_specs.append(whole_spec(shapes[-1]))
    if last:
        shapes.append(jax.ShapeDtypeStruct((packed_rows, channels), BF16))
        out_specs.append(whole_spec(shapes[-1]))
    return pl.pallas_call(
        functools.partial(backward_kernel, first, last, sums, grads, direct, base),
        grid=(rows // step,),
        in_specs=in_specs,
        out_specs=out_specs,
        out_shape=shapes,
        input_output_aliases=aliases,
        scratch_shapes=[
            pltpu.VMEM((crop // 128, lanes * d_bias.shape[1], 128) if direct else (1, 8, 128), F32),
        ],
        compiler_params=pltpu.CompilerParams(vmem_limit_bytes=56 * 2**20),
        cost_estimate=pl.CostEstimate(
            flops=6 * positions * channels * (9 * width + 2 * lanes),
            bytes_accessed=positions * (2 * channels + lanes) * 2,
            transcendentals=positions * width,
        ),
        name="pair_backward" if sums else "pair_grad_rows",
    )(*operands)


def attend_kernel(
    first, last, weight_ref, bias_ref, valid_ref, q_ref, k_ref, v_ref, g_ref, *refs
):
    if first:
        dq_ref, dk_ref, dv_ref, d_bias_ref = refs
    else:
        dk_before_ref, dv_before_ref, dq_ref, dk_ref, dv_ref, d_bias_ref = refs
    samples, depth = q_ref.shape[1:3]
    sources, _, rows, crop = bias_ref.shape
    scaling = 1.0 / math.sqrt(depth)
    bias = bias_ref[:, 0].astype(F32).reshape(sources * rows, crop)
    valid = valid_ref[...] > 0
    total = jnp.zeros_like(bias)
    for s in range(samples):
        query, key, value = q_ref[0, s], k_ref[0, s], v_ref[0, s]
        grad_half = (weight_ref[s] * g_ref[0, s].astype(F32)).astype(BF16)
        scores = mm(query, key, 0, 0) * scaling + bias
        scores = jnp.where(valid, scores, masked_score)
        exp_scores = jnp.exp(scores - jnp.max(scores, -1, keepdims=True))
        attention = exp_scores / jnp.sum(exp_scores, -1, keepdims=True)
        d_attention = mm(grad_half, value, 0, 0)
        d_scores = attention * (
            d_attention - jnp.sum(attention * d_attention, -1, keepdims=True)
        )
        total = total + d_scores
        scores_half = d_scores.astype(BF16)
        d_value = mm(grad_half, attention.astype(BF16))
        d_key = mm(query, scores_half)
        dq_ref[0, s] = (mm(key, scores_half, 1, 1) * scaling).astype(BF16)
        if not first:
            d_value = d_value + dv_before_ref[0, s]
            d_key = d_key + dk_before_ref[0, s]
        if last:
            d_key = d_key * scaling
        dv_ref[0, s] = d_value.astype(dv_ref.dtype)
        dk_ref[0, s] = d_key.astype(dk_ref.dtype)
    d_bias_ref[:, 0] = total.astype(BF16).reshape(sources, rows, crop)


def attend_rows(first, last, weights, bias, valid, query, key, value, grad, state):
    sources, layers, rows, crop = bias.shape
    samples, depth, row_count = query.shape[1:]
    vec = lambda shape: pl.BlockSpec((1,) + shape[1:], lambda l: (l, 0, 0, 0))
    plane = pl.BlockSpec((sources, 1, rows, crop), lambda l: (0, l, 0, 0))
    in_specs = [
        pl.BlockSpec(memory_space=pltpu.SMEM),
        plane,
        pl.BlockSpec(valid.shape, lambda l: (0, 0)),
        vec(query.shape),
        vec(key.shape),
        vec(value.shape),
        vec(grad.shape),
    ]
    operands = [weights, bias, valid, query, key, value, grad]
    if not first:
        operands += list(state)
        in_specs += [vec(key.shape), vec(value.shape)]
    kind = BF16 if last else F32
    return pl.pallas_call(
        functools.partial(attend_kernel, first, last),
        grid=(layers,),
        in_specs=in_specs,
        out_specs=[vec(query.shape), vec(key.shape), vec(value.shape), plane],
        out_shape=[
            jax.ShapeDtypeStruct(query.shape, BF16),
            jax.ShapeDtypeStruct(key.shape, kind),
            jax.ShapeDtypeStruct(value.shape, kind),
            jax.ShapeDtypeStruct(bias.shape, BF16),
        ],
        compiler_params=pltpu.CompilerParams(vmem_limit_bytes=48 * 2**20),
        cost_estimate=pl.CostEstimate(
            flops=200 * layers * samples * depth * row_count * crop,
            bytes_accessed=layers * crop * (4 * row_count + 12 * samples * depth),
            transcendentals=layers * samples * row_count * crop,
        ),
        name="attention_backward",
    )(*operands)


def swap(array, teams=None):
    return lax.all_to_all(
        array, "tok", split_axis=0, concat_axis=0, tiled=True, axis_index_groups=teams
    )


def sum_pairs(array):
    devices = lax.axis_size("tok")
    parity = lax.axis_index("tok") % 2
    across = [(index, index ^ 1) for index in range(devices)]
    halves = array.reshape(2, array.shape[0] // 2, array.shape[1])
    theirs = lax.ppermute(lax.dynamic_index_in_dim(halves, 1 - parity, 0, False), "tok", across)
    mine = lax.dynamic_index_in_dim(halves, parity, 0, False)
    return (mine.astype(F32) + theirs.astype(F32)).astype(BF16)


def sum_team(array):
    devices = lax.axis_size("tok")
    teams = [list(range(odd, devices, 2)) for odd in range(2)]
    members = devices // 2
    parts = swap(array.reshape(members, array.shape[0] // members, array.shape[1]), teams)
    return jnp.sum(parts.astype(F32), 0).astype(BF16)


def gather_shares(share):
    devices = lax.axis_size("tok")
    members = devices // 2
    across = [(index, index ^ 1) for index in range(devices)]
    teams = [list(range(odd, devices, 2)) for odd in range(2)]
    mine = swap(jnp.broadcast_to(share[None], (members,) + share.shape), teams)
    mine = mine.reshape(members * share.shape[0], share.shape[1])
    theirs = lax.ppermute(mine, "tok", across)
    even = lax.axis_index("tok") % 2 == 0
    both = jnp.concatenate([jnp.where(even, mine, theirs), jnp.where(even, theirs, mine)], 0)
    return both.astype(F32)


def body(
    pair_states,
    weight_in,
    weight_out,
    weight_bias,
    key_mask,
    noise_level,
    query_states,
    key_states,
    value_states,
    output_grad,
):
    row_count, crop, channels = pair_states.shape
    layers, _, heads = weight_bias.shape
    width = weight_out.shape[0]
    devices = lax.axis_size("tok")
    groups = devices // heads
    samples, depth = query_states.shape[2:4]
    lanes = heads * layers
    sizes = [row_count]
    if row_count % 16 == 0:
        sizes = [row_count // 2] * 2
    starts = [sum(sizes[:index]) for index in range(len(sizes))]
    w_bias = jnp.transpose(weight_bias, (0, 2, 1))

    group = lax.axis_index("tok") // heads
    weights = sample_weight(lax.dynamic_slice_in_dim(noise_level, group * samples, samples))
    valid = key_mask[None, :]

    def by_chunk(array):
        cut = array[:, 0].reshape(layers, samples, depth, devices, len(sizes), sizes[0])
        cut = jnp.transpose(cut, (4, 0, 1, 2, 3, 5))
        return cut.reshape(len(sizes), layers, samples, depth, devices * sizes[0])

    queries, grads = by_chunk(query_states), by_chunk(output_grad)

    arrived = []
    prepared = None
    for start, rows in zip(starts, sizes):
        bias, *made = forward_rows(
            start, rows, pair_states, weight_in, weight_out, w_bias, prepared
        )
        prepared = prepared or made
        if is_direct(rows, crop):
            bias = bias.reshape(heads, layers, rows, crop)
        else:
            bias = jnp.transpose(bias.reshape(rows, layers, heads, crop), (2, 1, 0, 3))
        if groups > 1:
            bias = jnp.tile(bias, (groups, 1, 1, 1))
        arrived.append(swap(bias))

    returned = []
    d_queries = []
    state = None
    for start, rows, bias in zip(starts, sizes, arrived):
        direct = is_direct(rows, crop)
        if not direct:
            bias = jnp.transpose(bias, (1, 0, 2, 3)).reshape(1, layers, devices * rows, crop)
        d_query, d_key, d_value, d_bias = attend_rows(
            start == 0,
            start + rows == row_count,
            weights,
            bias,
            valid,
            queries[start // rows],
            key_states[:, 0],
            value_states[:, 0],
            grads[start // rows],
            state,
        )
        state = (d_key, d_value)
        d_queries.append(d_query.reshape(layers, samples, depth, devices, rows))
        if not direct:
            d_bias = jnp.transpose(d_bias.reshape(layers, devices, rows, crop), (1, 0, 2, 3))
        returned.append(swap(d_bias))

    sum_rows = 3 * width + lanes
    packed_rows = 8 * devices * -(-sum_rows // (8 * devices))
    doubled = jnp.concatenate([jnp.ones((width,), BF16), jnp.full((width,), 2.0, BF16)])
    prepared = (*prepared, weight_in * doubled[None, :], weight_out * jnp.asarray(0.5, BF16))
    pair_state = None
    for start, rows, d_bias in zip(starts, sizes, returned):
        if groups > 1:
            d_bias = d_bias.reshape(groups, heads, layers, rows, crop).astype(F32)
            d_bias = jnp.sum(d_bias, 0).astype(BF16)
        if is_direct(rows, crop):
            d_bias = d_bias.reshape(lanes, rows, crop)
        else:
            d_bias = jnp.transpose(d_bias, (2, 1, 0, 3)).reshape(rows, lanes, crop)
        make = functools.partial(
            backward_rows,
            direct=is_direct(rows, crop),
            packed_rows=packed_rows,
            pair=pair_states,
            d_bias=d_bias,
            w_bias=w_bias,
            prepared=prepared,
        )
        pair_state = make(start, rows, 0, state=pair_state)
    pair_grad, _, packed = pair_state

    summed = gather_shares(sum_team(sum_pairs(packed)))
    grad_in = summed[: 2 * width].T
    grad_out = summed[2 * width : 3 * width]
    grad_bias = summed[3 * width : sum_rows].reshape(layers, heads, channels)
    grad_bias = jnp.transpose(grad_bias, (0, 2, 1))

    d_query = jnp.concatenate(d_queries, -1).reshape(query_states.shape)
    return (
        pair_grad,
        d_query,
        d_key[:, None],
        d_value[:, None],
        grad_in,
        grad_out,
        grad_bias,
    )


def solution(mesh):
    in_specs = (
        P(("job", "tok"), None, None),
        P(),
        P(),
        P(),
        P("job"),
        P("job"),
        P(None, "tok", "job", None, None),
        P(None, "tok", "job", None, None),
        P(None, "tok", "job", None, None),
        P(None, "tok", "job", None, None),
    )
    out_specs = (
        P(("job", "tok"), None, None),
        P(None, "tok", "job", None, None),
        P(None, "tok", "job", None, None),
        P(None, "tok", "job", None, None),
        P("job", None),
        P("job", None),
        P("job", None, None),
    )
    return jax.shard_map(body, mesh=mesh, in_specs=in_specs, out_specs=out_specs, check_vma=False)
```

```python
import functools
import math

import jax
import jax.numpy as jnp
from jax import lax
from jax.experimental import pallas as pl
from jax.experimental.pallas import tpu as pltpu
from jax.sharding import PartitionSpec as P

LEVELS = 200


sigma_high = 160.0
sigma_low = 0.0004
sigma_data = 16.0
rho_power = 7.0
epsilon = 1e-05
masked_score = -1000000000.0

F32 = jnp.float32
BF16 = jnp.bfloat16


def sample_weight(levels):
    level = levels.astype(jnp.float32)
    top_root = sigma_high ** (1.0 / rho_power)
    low_root = sigma_low ** (1.0 / rho_power)
    sigma_level = (top_root + level / (LEVELS - 1) * (low_root - top_root)) ** rho_power
    return (sigma_level * sigma_level + sigma_data * sigma_data) / (sigma_level + sigma_data) ** 2


def mm(left, right, left_dim=1, right_dim=0):
    return lax.dot_general(
        left, right, (((left_dim,), (right_dim,)), ((), ())), preferred_element_type=F32
    )


def normalize(inputs):
    centered = inputs - jnp.mean(inputs, 0, keepdims=True)
    inv_std = lax.rsqrt(jnp.mean(centered * centered, 0, keepdims=True) + epsilon)
    return centered * inv_std, inv_std


def norm_back(normed, inv_std, upstream):
    return inv_std * (
        upstream
        - jnp.mean(upstream, 0, keepdims=True)
        - normed * jnp.mean(upstream * normed, 0, keepdims=True)
    )


def split_width(width):
    return 256 if width % 256 == 0 else width


def interleave(make_stages, count, lag):
    rows = [make_stages(index) for index in range(count)]
    running = []
    clock = 0
    while rows or running:
        while rows and clock >= lag * (count - len(rows)):
            running.append(rows.pop(0))
        running = [row for row in running if next(row, None) is not None]
        clock += 1


def for_groups(count, group, one_group):
    group = math.gcd(count, group)

    def step(at, carry):
        one_group(at * group, group)
        return carry

    if count == group:
        step(0, 0)
    else:
        lax.fori_loop(0, count // group, step, 0)


def row_step(rows):
    return math.gcd(rows, 8 if rows > 8 else 4)


def is_direct(rows, crop):
    return rows % 8 == 0 and crop % 128 == 0


def forward_kernel(direct, first, pair_ref, w_bias_ref, *refs):
    if first:
        w_in_ref, w_out_ref, bias_ref, w_in_t_ref, w_out_t_ref = refs[:-1]
    else:
        w_in_t_ref, w_out_t_ref, bias_ref = refs[:-1]
    lines_ref = refs[-1]
    width = w_out_t_ref.shape[1]
    layers, heads, channels = w_bias_ref.shape
    piece = split_width(width)
    step = pair_ref.shape[0]
    first_row = pl.program_id(0) * step

    if first:

        @pl.when(pl.program_id(0) == 0)
        def _():
            w_in_t = w_in_ref[...].T
            w_in_t_ref[:width, :] = w_in_t[:width] * 0.5
            w_in_t_ref[width:, :] = w_in_t[width:]
            w_out_t_ref[...] = w_out_ref[...].T

    def stages(row):
        pair_float = pair_ref[row].T.astype(F32)
        normed_in = normalize(pair_float)[0].astype(BF16)
        yield True
        lifted = pair_float
        for at in range(0, width, piece):
            half_gate = mm(w_in_t_ref[at : at + piece, :], normed_in)
            up_in = mm(w_in_t_ref[width + at : width + at + piece, :], normed_in)
            yield True
            hidden = (half_gate * (1.0 + jnp.tanh(half_gate)) * up_in).astype(BF16)
            lifted = lifted + mm(w_out_t_ref[:, at : at + piece], hidden)
            yield True
        normed_out = normalize(lifted)[0].astype(BF16)
        yield True
        bias = mm(w_bias_ref[...].reshape(layers * heads, channels), normed_out)
        if direct:
            tiles, total, tile = lines_ref.shape
            rows = total // (layers * heads)
            for layer in range(layers):
                at = pl.ds(layer * rows + first_row + row, heads, stride=layers * rows)
                lines = bias[layer * heads : (layer + 1) * heads]
                for index in range(tiles):
                    lines_ref[index, at, :] = lines[:, index * tile : (index + 1) * tile]
        else:
            bias_ref[row] = bias.astype(BF16)

    for_groups(step, 2, lambda at, count: interleave(lambda i: stages(at + i), count, 0))

    if direct:

        @pl.when(pl.program_id(0) == pl.num_programs(0) - 1)
        def _():
            tiles, _, tile = lines_ref.shape
            for index in range(tiles):
                lines = lines_ref[index].reshape(bias_ref.shape[:2] + (tile,))
                bias_ref[:, :, index * tile : (index + 1) * tile] = lines.astype(BF16)


def whole_spec(array):
    return pl.BlockSpec(array.shape, lambda i: (0,) * len(array.shape))


def forward_rows(start, rows, pair, w_in, w_out, w_bias, prepared):
    crop, channels = pair.shape[1:]
    layers, heads, _ = w_bias.shape
    lanes = layers * heads
    step = row_step(rows)
    first_step = start // step
    positions = rows * crop
    width = w_out.shape[0]
    direct = is_direct(rows, crop)
    first = prepared is None
    line_shape = (heads * layers, rows, crop) if direct else (rows, lanes, crop)
    shapes = [jax.ShapeDtypeStruct(line_shape, BF16)]
    out_specs = [
        whole_spec(shapes[0])
        if direct
        else pl.BlockSpec((step, lanes, crop), lambda i: (i, 0, 0))
    ]
    if first:
        operands = [pair, w_bias, w_in, w_out]
        for shape in (w_in.shape[::-1], w_out.shape[::-1]):
            shapes.append(jax.ShapeDtypeStruct(shape, BF16))
            out_specs.append(whole_spec(shapes[-1]))
    else:
        operands = [pair, w_bias, *prepared]
    return pl.pallas_call(
        functools.partial(forward_kernel, direct, first),
        grid=(rows // step,),
        in_specs=[pl.BlockSpec((step, crop, channels), lambda i: (first_step + i, 0, 0))]
        + [whole_spec(array) for array in operands[1:]],
        out_specs=out_specs,
        out_shape=shapes,
        scratch_shapes=[
            pltpu.VMEM((crop // 128, lanes * rows, 128) if direct else (1, 8, 128), F32),
        ],
        compiler_params=pltpu.CompilerParams(vmem_limit_bytes=56 * 2**20),
        cost_estimate=pl.CostEstimate(
            flops=6 * positions * channels * (3 * width + lanes),
            bytes_accessed=positions * (channels + lanes) * 2,
            transcendentals=positions * width,
        ),
        name="pair_forward",
    )(*operands)


def backward_kernel(
    first,
    last,
    sums,
    grads,
    direct,
    base,
    pair_ref,
    d_bias_ref,
    w_bias_ref,
    w_in_t_ref,
    w_out_t_ref,
    w_back_ref,
    w_half_ref,
    *refs,
):
    outs = list(refs[:-1])
    if sums and not first:
        before_ref = outs.pop(0)
    if not first:
        outs.pop(0)
    if not sums:
        outs.pop(0)
    pair_grad_ref = outs.pop(0)
    sums_ref = outs.pop(0) if sums else None
    lines_ref = refs[-1]
    width = w_half_ref.shape[0]
    layers, heads, channels = w_bias_ref.shape
    lanes = layers * heads
    piece = split_width(width)
    step = pair_ref.shape[0]
    one, two = jnp.asarray(1.0, BF16), jnp.asarray(2.0, BF16)
    first_row = base + pl.program_id(0) * step

    @pl.when(pl.program_id(0) == 0)
    def _():
        if sums and first:
            sums_ref[...] = jnp.zeros_like(sums_ref)
        elif sums:
            sums_ref[...] = before_ref[...]
        if direct:
            tiles, total, tile = lines_ref.shape
            for index in range(tiles):
                lines = d_bias_ref[:, :, index * tile : (index + 1) * tile].astype(F32)
                lines_ref[index] = lines.reshape(total, tile)

    def read_lines(row):
        if not direct:
            return d_bias_ref[row]
        tiles, total, _ = lines_ref.shape
        rows = total // lanes
        found = []
        for layer in range(layers):
            at = pl.ds(layer * rows + first_row + row, heads, stride=layers * rows)
            found.append(jnp.concatenate([lines_ref[index, at, :] for index in range(tiles)], 1))
        return jnp.concatenate(found, 0).astype(BF16)

    def stages(row):
        pair_float = pair_ref[row].T.astype(F32)
        normed_float, inv_in = normalize(pair_float)
        normed_in = normed_float.astype(BF16)
        yield True
        lifted = pair_float
        kept = []
        for at in range(0, width, piece):
            half_gate = mm(w_in_t_ref[at : at + piece, :], normed_in)
            up_in = mm(w_in_t_ref[width + at : width + at + piece, :], normed_in)
            yield True
            one_plus = (1.0 + jnp.tanh(half_gate)).astype(BF16)
            half_gate, up_in = half_gate.astype(BF16), up_in.astype(BF16)
            silu = half_gate * one_plus
            hidden = silu * up_in
            slope = one_plus * (one + half_gate * (two - one_plus)) * up_in
            kept.append((silu, slope, hidden))
            lifted = lifted + mm(w_out_t_ref[:, at : at + piece], hidden)
            yield True
        out_float, inv_out = normalize(lifted)
        normed_out = out_float.astype(BF16)
        yield True
        d_bias = read_lines(row)
        d_normed = mm(w_bias_ref[...].reshape(lanes, channels), d_bias, 0, 0)
        if sums:
            sums_ref[3 * width :, :] += mm(d_bias, normed_out, 1, 1)
        d_lifted = norm_back(out_float, inv_out, d_normed)
        lifted_half = d_lifted.astype(BF16)
        yield True
        d_normed_in = None
        for index, (silu, slope, hidden) in enumerate(kept):
            at = index * piece
            cols = slice(at, at + piece)
            up_cols = slice(width + at, width + at + piece)
            d_hidden = mm(w_half_ref[cols, :], lifted_half).astype(BF16)
            if sums:
                out_cols = slice(2 * width + at, 2 * width + at + piece)
                sums_ref[out_cols, :] += mm(hidden, lifted_half, 1, 1)
            yield True
            d_gate = d_hidden * slope
            d_up = d_hidden * silu
            if sums:
                sums_ref[cols, :] += mm(d_gate, normed_in, 1, 1)
                sums_ref[up_cols, :] += mm(d_up, normed_in, 1, 1)
            if grads:
                part = mm(w_back_ref[:, cols], d_gate) + mm(w_back_ref[:, up_cols], d_up)
                d_normed_in = part if d_normed_in is None else d_normed_in + part
            yield True
        if grads:
            pair_grad = d_lifted + norm_back(normed_float, inv_in, d_normed_in)
            pair_grad_ref[row] = pair_grad.astype(BF16).T

    for_groups(step, 4, lambda at, count: interleave(lambda i: stages(at + i), count, 2))

    if last:
        packed_ref = outs.pop(0)

        @pl.when(pl.program_id(0) == pl.num_programs(0) - 1)
        def _():
            done = sums_ref.shape[0]
            packed_ref[:done, :] = sums_ref[...].astype(BF16)
            packed_ref[width : 2 * width, :] = (2.0 * sums_ref[width : 2 * width, :]).astype(BF16)
            packed_ref[done:, :] = jnp.zeros((packed_ref.shape[0] - done, packed_ref.shape[1]), BF16)


def backward_rows(
    start,
    rows,
    base,
    direct,
    packed_rows,
    pair,
    d_bias,
    w_bias,
    prepared,
    state,
    grads=True,
    after=None,
):
    crop, channels = pair.shape[1:]
    layers, heads, _ = w_bias.shape
    lanes = layers * heads
    width = prepared[3].shape[0]
    step = row_step(rows)
    first_step = start // step
    positions = rows * crop
    sums = after is None
    first = start == 0
    last = sums and start + rows == pair.shape[0]
    pair_spec = pl.BlockSpec((step, crop, channels), lambda i: (first_step + i, 0, 0))
    line_spec = whole_spec(d_bias) if direct else pl.BlockSpec((step, lanes, crop), lambda i: (i, 0, 0))
    held_spec = pl.BlockSpec(memory_space=pl.ANY)
    operands = [pair, d_bias, w_bias, *prepared]
    in_specs = [pair_spec, line_spec] + [whole_spec(array) for array in operands[2:]]
    aliases = {}
    if sums and not first:
        operands.append(state[1])
        in_specs.append(whole_spec(state[1]))
    if not first:
        aliases = {len(operands): 0}
        operands.append(state[0])
        in_specs.append(held_spec)
    if not sums:
        operands.append(after)
        in_specs.append(held_spec)
    shapes = [jax.ShapeDtypeStruct(pair.shape, BF16)]
    out_specs = [pair_spec if grads else held_spec]
    if sums:
        shapes.append(jax.ShapeDtypeStruct((3 * width + lanes, channels), F32))
        out_specs.append(whole_spec(shapes[-1]))
    if last:
        shapes.append(jax.ShapeDtypeStruct((packed_rows, channels), BF16))
        out_specs.append(whole_spec(shapes[-1]))
    return pl.pallas_call(
        functools.partial(backward_kernel, first, last, sums, grads, direct, base),
        grid=(rows // step,),
        in_specs=in_specs,
        out_specs=out_specs,
        out_shape=shapes,
        input_output_aliases=aliases,
        scratch_shapes=[
            pltpu.VMEM((crop // 128, lanes * d_bias.shape[1], 128) if direct else (1, 8, 128), F32),
        ],
        compiler_params=pltpu.CompilerParams(vmem_limit_bytes=56 * 2**20),
        cost_estimate=pl.CostEstimate(
            flops=6 * positions * channels * (9 * width + 2 * lanes),
            bytes_accessed=positions * (2 * channels + lanes) * 2,
            transcendentals=positions * width,
        ),
        name="pair_backward" if sums else "pair_grad_rows",
    )(*operands)


def attend_kernel(
    first, last, weight_ref, bias_ref, valid_ref, q_ref, k_ref, v_ref, g_ref, *refs
):
    if first:
        dq_ref, dk_ref, dv_ref, d_bias_ref = refs
    else:
        dk_before_ref, dv_before_ref, dq_ref, dk_ref, dv_ref, d_bias_ref = refs
    samples, depth = q_ref.shape[1:3]
    sources, _, rows, crop = bias_ref.shape
    scaling = 1.0 / math.sqrt(depth)
    bias = bias_ref[:, 0].astype(F32).reshape(sources * rows, crop)
    valid = valid_ref[...] > 0
    total = jnp.zeros_like(bias)
    for s in range(samples):
        query, key, value = q_ref[0, s], k_ref[0, s], v_ref[0, s]
        grad_half = (weight_ref[s] * g_ref[0, s].astype(F32)).astype(BF16)
        scores = mm(query, key, 0, 0) * scaling + bias
        scores = jnp.where(valid, scores, masked_score)
        exp_scores = jnp.exp(scores - jnp.max(scores, -1, keepdims=True))
        attention = exp_scores / jnp.sum(exp_scores, -1, keepdims=True)
        d_attention = mm(grad_half, value, 0, 0)
        d_scores = attention * (
            d_attention - jnp.sum(attention * d_attention, -1, keepdims=True)
        )
        total = total + d_scores
        scores_half = d_scores.astype(BF16)
        d_value = mm(grad_half, attention.astype(BF16))
        d_key = mm(query, scores_half)
        dq_ref[0, s] = (mm(key, scores_half, 1, 1) * scaling).astype(BF16)
        if not first:
            d_value = d_value + dv_before_ref[0, s]
            d_key = d_key + dk_before_ref[0, s]
        if last:
            d_key = d_key * scaling
        dv_ref[0, s] = d_value.astype(dv_ref.dtype)
        dk_ref[0, s] = d_key.astype(dk_ref.dtype)
    d_bias_ref[:, 0] = total.astype(BF16).reshape(sources, rows, crop)


def attend_rows(first, last, weights, bias, valid, query, key, value, grad, state):
    sources, layers, rows, crop = bias.shape
    samples, depth, row_count = query.shape[1:]
    vec = lambda shape: pl.BlockSpec((1,) + shape[1:], lambda l: (l, 0, 0, 0))
    plane = pl.BlockSpec((sources, 1, rows, crop), lambda l: (0, l, 0, 0))
    in_specs = [
        pl.BlockSpec(memory_space=pltpu.SMEM),
        plane,
        pl.BlockSpec(valid.shape, lambda l: (0, 0)),
        vec(query.shape),
        vec(key.shape),
        vec(value.shape),
        vec(grad.shape),
    ]
    operands = [weights, bias, valid, query, key, value, grad]
    if not first:
        operands += list(state)
        in_specs += [vec(key.shape), vec(value.shape)]
    kind = BF16 if last else F32
    return pl.pallas_call(
        functools.partial(attend_kernel, first, last),
        grid=(layers,),
        in_specs=in_specs,
        out_specs=[vec(query.shape), vec(key.shape), vec(value.shape), plane],
        out_shape=[
            jax.ShapeDtypeStruct(query.shape, BF16),
            jax.ShapeDtypeStruct(key.shape, kind),
            jax.ShapeDtypeStruct(value.shape, kind),
            jax.ShapeDtypeStruct(bias.shape, BF16),
        ],
        compiler_params=pltpu.CompilerParams(vmem_limit_bytes=48 * 2**20),
        cost_estimate=pl.CostEstimate(
            flops=200 * layers * samples * depth * row_count * crop,
            bytes_accessed=layers * crop * (4 * row_count + 12 * samples * depth),
            transcendentals=layers * samples * row_count * crop,
        ),
        name="attention_backward",
    )(*operands)


def swap(array, teams=None):
    return lax.all_to_all(
        array, "tok", split_axis=0, concat_axis=0, tiled=True, axis_index_groups=teams
    )


def sum_pairs(array):
    devices = lax.axis_size("tok")
    parity = lax.axis_index("tok") % 2
    across = [(index, index ^ 1) for index in range(devices)]
    halves = array.reshape(2, array.shape[0] // 2, array.shape[1])
    theirs = lax.ppermute(lax.dynamic_index_in_dim(halves, 1 - parity, 0, False), "tok", across)
    mine = lax.dynamic_index_in_dim(halves, parity, 0, False)
    return (mine.astype(F32) + theirs.astype(F32)).astype(BF16)


def sum_team(array):
    devices = lax.axis_size("tok")
    teams = [list(range(odd, devices, 2)) for odd in range(2)]
    members = devices // 2
    parts = swap(array.reshape(members, array.shape[0] // members, array.shape[1]), teams)
    return jnp.sum(parts.astype(F32), 0).astype(BF16)


def gather_shares(share):
    devices = lax.axis_size("tok")
    members = devices // 2
    across = [(index, index ^ 1) for index in range(devices)]
    teams = [list(range(odd, devices, 2)) for odd in range(2)]
    mine = swap(jnp.broadcast_to(share[None], (members,) + share.shape), teams)
    mine = mine.reshape(members * share.shape[0], share.shape[1])
    theirs = lax.ppermute(mine, "tok", across)
    even = lax.axis_index("tok") % 2 == 0
    both = jnp.concatenate([jnp.where(even, mine, theirs), jnp.where(even, theirs, mine)], 0)
    return both.astype(F32)


def body(
    pair_states,
    weight_in,
    weight_out,
    weight_bias,
    key_mask,
    noise_level,
    query_states,
    key_states,
    value_states,
    output_grad,
):
    row_count, crop, channels = pair_states.shape
    layers, _, heads = weight_bias.shape
    width = weight_out.shape[0]
    devices = lax.axis_size("tok")
    groups = devices // heads
    samples, depth = query_states.shape[2:4]
    lanes = heads * layers
    sizes = [row_count]
    if row_count % 16 == 0:
        sizes = [row_count // 2] * 2
    starts = [sum(sizes[:index]) for index in range(len(sizes))]
    w_bias = jnp.transpose(weight_bias, (0, 2, 1))

    group = lax.axis_index("tok") // heads
    weights = sample_weight(lax.dynamic_slice_in_dim(noise_level, group * samples, samples))
    valid = key_mask[None, :]

    def by_chunk(array):
        cut = array[:, 0].reshape(layers, samples, depth, devices, len(sizes), sizes[0])
        cut = jnp.transpose(cut, (4, 0, 1, 2, 3, 5))
        return cut.reshape(len(sizes), layers, samples, depth, devices * sizes[0])

    queries, grads = by_chunk(query_states), by_chunk(output_grad)

    arrived = []
    prepared = None
    for start, rows in zip(starts, sizes):
        bias, *made = forward_rows(
            start, rows, pair_states, weight_in, weight_out, w_bias, prepared
        )
        prepared = prepared or made
        if is_direct(rows, crop):
            bias = bias.reshape(heads, layers, rows, crop)
        else:
            bias = jnp.transpose(bias.reshape(rows, layers, heads, crop), (2, 1, 0, 3))
        if groups > 1:
            bias = jnp.tile(bias, (groups, 1, 1, 1))
        arrived.append(swap(bias))

    returned = []
    d_queries = []
    state = None
    for start, rows, bias in zip(starts, sizes, arrived):
        direct = is_direct(rows, crop)
        if not direct:
            bias = jnp.transpose(bias, (1, 0, 2, 3)).reshape(1, layers, devices * rows, crop)
        d_query, d_key, d_value, d_bias = attend_rows(
            start == 0,
            start + rows == row_count,
            weights,
            bias,
            valid,
            queries[start // rows],
            key_states[:, 0],
            value_states[:, 0],
            grads[start // rows],
            state,
        )
        state = (d_key, d_value)
        d_queries.append(d_query.reshape(layers, samples, depth, devices, rows))
        if not direct:
            d_bias = jnp.transpose(d_bias.reshape(layers, devices, rows, crop), (1, 0, 2, 3))
        returned.append(swap(d_bias))

    sum_rows = 3 * width + lanes
    packed_rows = 8 * devices * -(-sum_rows // (8 * devices))
    doubled = jnp.concatenate([jnp.ones((width,), BF16), jnp.full((width,), 2.0, BF16)])
    prepared = (*prepared, weight_in * doubled[None, :], weight_out * jnp.asarray(0.5, BF16))
    pair_state = None
    for start, rows, d_bias in zip(starts, sizes, returned):
        if groups > 1:
            d_bias = d_bias.reshape(groups, heads, layers, rows, crop).astype(F32)
            d_bias = jnp.sum(d_bias, 0).astype(BF16)
        if is_direct(rows, crop):
            d_bias = d_bias.reshape(lanes, rows, crop)
        else:
            d_bias = jnp.transpose(d_bias, (2, 1, 0, 3)).reshape(rows, lanes, crop)
        make = functools.partial(
            backward_rows,
            direct=is_direct(rows, crop),
            packed_rows=packed_rows,
            pair=pair_states,
            d_bias=d_bias,
            w_bias=w_bias,
            prepared=prepared,
        )
        pair_state = make(start, rows, 0, state=pair_state)
    pair_grad, _, packed = pair_state

    summed = gather_shares(sum_team(sum_pairs(packed)))
    grad_in = summed[: 2 * width].T
    grad_out = summed[2 * width : 3 * width]
    grad_bias = summed[3 * width : sum_rows].reshape(layers, heads, channels)
    grad_bias = jnp.transpose(grad_bias, (0, 2, 1))

    d_query = jnp.concatenate(d_queries, -1).reshape(query_states.shape)
    return (
        pair_grad,
        d_query,
        d_key[:, None],
        d_value[:, None],
        grad_in,
        grad_out,
        grad_bias,
    )


def solution(mesh):
    in_specs = (
        P(("job", "tok"), None, None),
        P(),
        P(),
        P(),
        P("job"),
        P("job"),
        P(None, "tok", "job", None, None),
        P(None, "tok", "job", None, None),
        P(None, "tok", "job", None, None),
        P(None, "tok", "job", None, None),
    )
    out_specs = (
        P(("job", "tok"), None, None),
        P(None, "tok", "job", None, None),
        P(None, "tok", "job", None, None),
        P(None, "tok", "job", None, None),
        P("job", None),
        P("job", None),
        P("job", None, None),
    )
    return jax.shard_map(body, mesh=mesh, in_specs=in_specs, out_specs=out_specs, check_vma=False)
```

```python
import functools
import math

import jax
import jax.numpy as jnp
from jax import lax
from jax.experimental import pallas as pl
from jax.experimental.pallas import tpu as pltpu
from jax.sharding import PartitionSpec as P

LEVELS = 200


sigma_high = 160.0
sigma_low = 0.0004
sigma_data = 16.0
rho_power = 7.0
epsilon = 1e-05
masked_score = -1000000000.0

F32 = jnp.float32
BF16 = jnp.bfloat16


def sample_weight(levels):
    level = levels.astype(jnp.float32)
    top_root = sigma_high ** (1.0 / rho_power)
    low_root = sigma_low ** (1.0 / rho_power)
    sigma_level = (top_root + level / (LEVELS - 1) * (low_root - top_root)) ** rho_power
    return (sigma_level * sigma_level + sigma_data * sigma_data) / (sigma_level + sigma_data) ** 2


def mm(left, right, left_dim=1, right_dim=0):
    return lax.dot_general(
        left, right, (((left_dim,), (right_dim,)), ((), ())), preferred_element_type=F32
    )


def normalize(inputs):
    centered = inputs - jnp.mean(inputs, 0, keepdims=True)
    inv_std = lax.rsqrt(jnp.mean(centered * centered, 0, keepdims=True) + epsilon)
    return centered * inv_std, inv_std


def norm_back(normed, inv_std, upstream):
    return inv_std * (
        upstream
        - jnp.mean(upstream, 0, keepdims=True)
        - normed * jnp.mean(upstream * normed, 0, keepdims=True)
    )


def split_width(width):
    return 256 if width % 256 == 0 else width


def interleave(make_stages, count, lag):
    rows = [make_stages(index) for index in range(count)]
    running = []
    clock = 0
    while rows or running:
        while rows and clock >= lag * (count - len(rows)):
            running.append(rows.pop(0))
        running = [row for row in running if next(row, None) is not None]
        clock += 1


def for_groups(count, group, one_group):
    group = math.gcd(count, group)

    def step(at, carry):
        one_group(at * group, group)
        return carry

    if count == group:
        step(0, 0)
    else:
        lax.fori_loop(0, count // group, step, 0)


def row_step(rows):
    return math.gcd(rows, 8 if rows > 8 else 4)


def is_direct(rows, crop):
    return rows % 8 == 0 and crop % 128 == 0


def forward_kernel(direct, first, pair_ref, w_bias_ref, *refs):
    if first:
        w_in_ref, w_out_ref, bias_ref, w_in_t_ref, w_out_t_ref = refs[:-1]
    else:
        w_in_t_ref, w_out_t_ref, bias_ref = refs[:-1]
    lines_ref = refs[-1]
    width = w_out_t_ref.shape[1]
    layers, heads, channels = w_bias_ref.shape
    piece = split_width(width)
    step = pair_ref.shape[0]
    first_row = pl.program_id(0) * step

    if first:

        @pl.when(pl.program_id(0) == 0)
        def _():
            w_in_t = w_in_ref[...].T
            w_in_t_ref[:width, :] = w_in_t[:width] * 0.5
            w_in_t_ref[width:, :] = w_in_t[width:]
            w_out_t_ref[...] = w_out_ref[...].T

    def stages(row):
        pair_float = pair_ref[row].T.astype(F32)
        normed_in = normalize(pair_float)[0].astype(BF16)
        yield True
        lifted = pair_float
        for at in range(0, width, piece):
            half_gate = mm(w_in_t_ref[at : at + piece, :], normed_in)
            up_in = mm(w_in_t_ref[width + at : width + at + piece, :], normed_in)
            yield True
            hidden = (half_gate * (1.0 + jnp.tanh(half_gate)) * up_in).astype(BF16)
            lifted = lifted + mm(w_out_t_ref[:, at : at + piece], hidden)
            yield True
        normed_out = normalize(lifted)[0].astype(BF16)
        yield True
        bias = mm(w_bias_ref[...].reshape(layers * heads, channels), normed_out)
        if direct:
            tiles, total, tile = lines_ref.shape
            rows = total // (layers * heads)
            for layer in range(layers):
                at = pl.ds(layer * rows + first_row + row, heads, stride=layers * rows)
                lines = bias[layer * heads : (layer + 1) * heads]
                for index in range(tiles):
                    lines_ref[index, at, :] = lines[:, index * tile : (index + 1) * tile]
        else:
            bias_ref[row] = bias.astype(BF16)

    for_groups(step, 8, lambda at, count: interleave(lambda i: stages(at + i), count, 0))

    if direct:

        @pl.when(pl.program_id(0) == pl.num_programs(0) - 1)
        def _():
            tiles, _, tile = lines_ref.shape
            for index in range(tiles):
                lines = lines_ref[index].reshape(bias_ref.shape[:2] + (tile,))
                bias_ref[:, :, index * tile : (index + 1) * tile] = lines.astype(BF16)


def whole_spec(array):
    return pl.BlockSpec(array.shape, lambda i: (0,) * len(array.shape))


def forward_rows(start, rows, pair, w_in, w_out, w_bias, prepared):
    crop, channels = pair.shape[1:]
    layers, heads, _ = w_bias.shape
    lanes = layers * heads
    step = row_step(rows)
    first_step = start // step
    positions = rows * crop
    width = w_out.shape[0]
    direct = is_direct(rows, crop)
    first = prepared is None
    line_shape = (heads * layers, rows, crop) if direct else (rows, lanes, crop)
    shapes = [jax.ShapeDtypeStruct(line_shape, BF16)]
    out_specs = [
        whole_spec(shapes[0])
        if direct
        else pl.BlockSpec((step, lanes, crop), lambda i: (i, 0, 0))
    ]
    if first:
        operands = [pair, w_bias, w_in, w_out]
        for shape in (w_in.shape[::-1], w_out.shape[::-1]):
            shapes.append(jax.ShapeDtypeStruct(shape, BF16))
            out_specs.append(whole_spec(shapes[-1]))
    else:
        operands = [pair, w_bias, *prepared]
    return pl.pallas_call(
        functools.partial(forward_kernel, direct, first),
        grid=(rows // step,),
        in_specs=[pl.BlockSpec((step, crop, channels), lambda i: (first_step + i, 0, 0))]
        + [whole_spec(array) for array in operands[1:]],
        out_specs=out_specs,
        out_shape=shapes,
        scratch_shapes=[
            pltpu.VMEM((crop // 128, lanes * rows, 128) if direct else (1, 8, 128), F32),
        ],
        compiler_params=pltpu.CompilerParams(vmem_limit_bytes=56 * 2**20),
        cost_estimate=pl.CostEstimate(
            flops=6 * positions * channels * (3 * width + lanes),
            bytes_accessed=positions * (channels + lanes) * 2,
            transcendentals=positions * width,
        ),
        name="pair_forward",
    )(*operands)


def backward_kernel(
    first,
    last,
    sums,
    grads,
    direct,
    base,
    pair_ref,
    d_bias_ref,
    w_bias_ref,
    w_in_t_ref,
    w_out_t_ref,
    w_back_ref,
    w_half_ref,
    *refs,
):
    outs = list(refs[:-1])
    if sums and not first:
        before_ref = outs.pop(0)
    if not first:
        outs.pop(0)
    if not sums:
        outs.pop(0)
    pair_grad_ref = outs.pop(0)
    sums_ref = outs.pop(0) if sums else None
    lines_ref = refs[-1]
    width = w_half_ref.shape[0]
    layers, heads, channels = w_bias_ref.shape
    lanes = layers * heads
    piece = split_width(width)
    step = pair_ref.shape[0]
    one, two = jnp.asarray(1.0, BF16), jnp.asarray(2.0, BF16)
    first_row = base + pl.program_id(0) * step

    @pl.when(pl.program_id(0) == 0)
    def _():
        if sums and first:
            sums_ref[...] = jnp.zeros_like(sums_ref)
        elif sums:
            sums_ref[...] = before_ref[...]
        if direct:
            tiles, total, tile = lines_ref.shape
            for index in range(tiles):
                lines = d_bias_ref[:, :, index * tile : (index + 1) * tile].astype(F32)
                lines_ref[index] = lines.reshape(total, tile)

    def read_lines(row):
        if not direct:
            return d_bias_ref[row]
        tiles, total, _ = lines_ref.shape
        rows = total // lanes
        found = []
        for layer in range(layers):
            at = pl.ds(layer * rows + first_row + row, heads, stride=layers * rows)
            found.append(jnp.concatenate([lines_ref[index, at, :] for index in range(tiles)], 1))
        return jnp.concatenate(found, 0).astype(BF16)

    def stages(row):
        pair_float = pair_ref[row].T.astype(F32)
        normed_float, inv_in = normalize(pair_float)
        normed_in = normed_float.astype(BF16)
        yield True
        lifted = pair_float
        kept = []
        for at in range(0, width, piece):
            half_gate = mm(w_in_t_ref[at : at + piece, :], normed_in)
            up_in = mm(w_in_t_ref[width + at : width + at + piece, :], normed_in)
            yield True
            one_plus = (1.0 + jnp.tanh(half_gate)).astype(BF16)
            half_gate, up_in = half_gate.astype(BF16), up_in.astype(BF16)
            silu = half_gate * one_plus
            hidden = silu * up_in
            slope = one_plus * (one + half_gate * (two - one_plus)) * up_in
            kept.append((silu, slope, hidden))
            lifted = lifted + mm(w_out_t_ref[:, at : at + piece], hidden)
            yield True
        out_float, inv_out = normalize(lifted)
        normed_out = out_float.astype(BF16)
        yield True
        d_bias = read_lines(row)
        d_normed = mm(w_bias_ref[...].reshape(lanes, channels), d_bias, 0, 0)
        if sums:
            sums_ref[3 * width :, :] += mm(d_bias, normed_out, 1, 1)
        d_lifted = norm_back(out_float, inv_out, d_normed)
        lifted_half = d_lifted.astype(BF16)
        yield True
        d_normed_in = None
        for index, (silu, slope, hidden) in enumerate(kept):
            at = index * piece
            cols = slice(at, at + piece)
            up_cols = slice(width + at, width + at + piece)
            d_hidden = mm(w_half_ref[cols, :], lifted_half).astype(BF16)
            if sums:
                out_cols = slice(2 * width + at, 2 * width + at + piece)
                sums_ref[out_cols, :] += mm(hidden, lifted_half, 1, 1)
            yield True
            d_gate = d_hidden * slope
            d_up = d_hidden * silu
            if sums:
                sums_ref[cols, :] += mm(d_gate, normed_in, 1, 1)
                sums_ref[up_cols, :] += mm(d_up, normed_in, 1, 1)
            if grads:
                part = mm(w_back_ref[:, cols], d_gate) + mm(w_back_ref[:, up_cols], d_up)
                d_normed_in = part if d_normed_in is None else d_normed_in + part
            yield True
        if grads:
            pair_grad = d_lifted + norm_back(normed_float, inv_in, d_normed_in)
            pair_grad_ref[row] = pair_grad.astype(BF16).T

    for_groups(step, 8, lambda at, count: interleave(lambda i: stages(at + i), count, 0))

    if last:
        packed_ref = outs.pop(0)

        @pl.when(pl.program_id(0) == pl.num_programs(0) - 1)
        def _():
            done = sums_ref.shape[0]
            packed_ref[:done, :] = sums_ref[...].astype(BF16)
            packed_ref[width : 2 * width, :] = (2.0 * sums_ref[width : 2 * width, :]).astype(BF16)
            packed_ref[done:, :] = jnp.zeros((packed_ref.shape[0] - done, packed_ref.shape[1]), BF16)


def backward_rows(
    start,
    rows,
    base,
    direct,
    packed_rows,
    pair,
    d_bias,
    w_bias,
    prepared,
    state,
    grads=True,
    after=None,
):
    crop, channels = pair.shape[1:]
    layers, heads, _ = w_bias.shape
    lanes = layers * heads
    width = prepared[3].shape[0]
    step = row_step(rows)
    first_step = start // step
    positions = rows * crop
    sums = after is None
    first = start == 0
    last = sums and start + rows == pair.shape[0]
    pair_spec = pl.BlockSpec((step, crop, channels), lambda i: (first_step + i, 0, 0))
    line_spec = whole_spec(d_bias) if direct else pl.BlockSpec((step, lanes, crop), lambda i: (i, 0, 0))
    held_spec = pl.BlockSpec(memory_space=pl.ANY)
    operands = [pair, d_bias, w_bias, *prepared]
    in_specs = [pair_spec, line_spec] + [whole_spec(array) for array in operands[2:]]
    aliases = {}
    if sums and not first:
        operands.append(state[1])
        in_specs.append(whole_spec(state[1]))
    if not first:
        aliases = {len(operands): 0}
        operands.append(state[0])
        in_specs.append(held_spec)
    if not sums:
        operands.append(after)
        in_specs.append(held_spec)
    shapes = [jax.ShapeDtypeStruct(pair.shape, BF16)]
    out_specs = [pair_spec if grads else held_spec]
    if sums:
        shapes.append(jax.ShapeDtypeStruct((3 * width + lanes, channels), F32))
        out_specs.append(whole_spec(shapes[-1]))
    if last:
        shapes.append(jax.ShapeDtypeStruct((packed_rows, channels), BF16))
        out_specs.append(whole_spec(shapes[-1]))
    return pl.pallas_call(
        functools.partial(backward_kernel, first, last, sums, grads, direct, base),
        grid=(rows // step,),
        in_specs=in_specs,
        out_specs=out_specs,
        out_shape=shapes,
        input_output_aliases=aliases,
        scratch_shapes=[
            pltpu.VMEM((crop // 128, lanes * d_bias.shape[1], 128) if direct else (1, 8, 128), F32),
        ],
        compiler_params=pltpu.CompilerParams(vmem_limit_bytes=56 * 2**20),
        cost_estimate=pl.CostEstimate(
            flops=6 * positions * channels * (9 * width + 2 * lanes),
            bytes_accessed=positions * (2 * channels + lanes) * 2,
            transcendentals=positions * width,
        ),
        name="pair_backward" if sums else "pair_grad_rows",
    )(*operands)


def attend_kernel(
    first, last, weight_ref, bias_ref, valid_ref, q_ref, k_ref, v_ref, g_ref, *refs
):
    if first:
        dq_ref, dk_ref, dv_ref, d_bias_ref = refs
    else:
        dk_before_ref, dv_before_ref, dq_ref, dk_ref, dv_ref, d_bias_ref = refs
    samples, depth = q_ref.shape[1:3]
    sources, _, rows, crop = bias_ref.shape
    scaling = 1.0 / math.sqrt(depth)
    bias = bias_ref[:, 0].astype(F32).reshape(sources * rows, crop)
    valid = valid_ref[...] > 0
    total = jnp.zeros_like(bias)
    for s in range(samples):
        query, key, value = q_ref[0, s], k_ref[0, s], v_ref[0, s]
        grad_half = (weight_ref[s] * g_ref[0, s].astype(F32)).astype(BF16)
        scores = mm(query, key, 0, 0) * scaling + bias
        scores = jnp.where(valid, scores, masked_score)
        exp_scores = jnp.exp(scores - jnp.max(scores, -1, keepdims=True))
        attention = exp_scores / jnp.sum(exp_scores, -1, keepdims=True)
        d_attention = mm(grad_half, value, 0, 0)
        d_scores = attention * (
            d_attention - jnp.sum(attention * d_attention, -1, keepdims=True)
        )
        total = total + d_scores
        scores_half = d_scores.astype(BF16)
        d_value = mm(grad_half, attention.astype(BF16))
        d_key = mm(query, scores_half)
        dq_ref[0, s] = (mm(key, scores_half, 1, 1) * scaling).astype(BF16)
        if not first:
            d_value = d_value + dv_before_ref[0, s]
            d_key = d_key + dk_before_ref[0, s]
        if last:
            d_key = d_key * scaling
        dv_ref[0, s] = d_value.astype(dv_ref.dtype)
        dk_ref[0, s] = d_key.astype(dk_ref.dtype)
    d_bias_ref[:, 0] = total.astype(BF16).reshape(sources, rows, crop)


def attend_rows(first, last, weights, bias, valid, query, key, value, grad, state):
    sources, layers, rows, crop = bias.shape
    samples, depth, row_count = query.shape[1:]
    vec = lambda shape: pl.BlockSpec((1,) + shape[1:], lambda l: (l, 0, 0, 0))
    plane = pl.BlockSpec((sources, 1, rows, crop), lambda l: (0, l, 0, 0))
    in_specs = [
        pl.BlockSpec(memory_space=pltpu.SMEM),
        plane,
        pl.BlockSpec(valid.shape, lambda l: (0, 0)),
        vec(query.shape),
        vec(key.shape),
        vec(value.shape),
        vec(grad.shape),
    ]
    operands = [weights, bias, valid, query, key, value, grad]
    if not first:
        operands += list(state)
        in_specs += [vec(key.shape), vec(value.shape)]
    kind = BF16 if last else F32
    return pl.pallas_call(
        functools.partial(attend_kernel, first, last),
        grid=(layers,),
        in_specs=in_specs,
        out_specs=[vec(query.shape), vec(key.shape), vec(value.shape), plane],
        out_shape=[
            jax.ShapeDtypeStruct(query.shape, BF16),
            jax.ShapeDtypeStruct(key.shape, kind),
            jax.ShapeDtypeStruct(value.shape, kind),
            jax.ShapeDtypeStruct(bias.shape, BF16),
        ],
        compiler_params=pltpu.CompilerParams(vmem_limit_bytes=48 * 2**20),
        cost_estimate=pl.CostEstimate(
            flops=200 * layers * samples * depth * row_count * crop,
            bytes_accessed=layers * crop * (4 * row_count + 12 * samples * depth),
            transcendentals=layers * samples * row_count * crop,
        ),
        name="attention_backward",
    )(*operands)


def swap(array, teams=None):
    return lax.all_to_all(
        array, "tok", split_axis=0, concat_axis=0, tiled=True, axis_index_groups=teams
    )


def sum_pairs(array):
    devices = lax.axis_size("tok")
    parity = lax.axis_index("tok") % 2
    across = [(index, index ^ 1) for index in range(devices)]
    halves = array.reshape(2, array.shape[0] // 2, array.shape[1])
    theirs = lax.ppermute(lax.dynamic_index_in_dim(halves, 1 - parity, 0, False), "tok", across)
    mine = lax.dynamic_index_in_dim(halves, parity, 0, False)
    return (mine.astype(F32) + theirs.astype(F32)).astype(BF16)


def sum_team(array):
    devices = lax.axis_size("tok")
    teams = [list(range(odd, devices, 2)) for odd in range(2)]
    members = devices // 2
    parts = swap(array.reshape(members, array.shape[0] // members, array.shape[1]), teams)
    return jnp.sum(parts.astype(F32), 0).astype(BF16)


def gather_shares(share):
    devices = lax.axis_size("tok")
    members = devices // 2
    across = [(index, index ^ 1) for index in range(devices)]
    teams = [list(range(odd, devices, 2)) for odd in range(2)]
    mine = swap(jnp.broadcast_to(share[None], (members,) + share.shape), teams)
    mine = mine.reshape(members * share.shape[0], share.shape[1])
    theirs = lax.ppermute(mine, "tok", across)
    even = lax.axis_index("tok") % 2 == 0
    both = jnp.concatenate([jnp.where(even, mine, theirs), jnp.where(even, theirs, mine)], 0)
    return both.astype(F32)


def body(
    pair_states,
    weight_in,
    weight_out,
    weight_bias,
    key_mask,
    noise_level,
    query_states,
    key_states,
    value_states,
    output_grad,
):
    row_count, crop, channels = pair_states.shape
    layers, _, heads = weight_bias.shape
    width = weight_out.shape[0]
    devices = lax.axis_size("tok")
    groups = devices // heads
    samples, depth = query_states.shape[2:4]
    lanes = heads * layers
    sizes = [row_count]
    if row_count % 16 == 0:
        sizes = [row_count // 2] * 2
    starts = [sum(sizes[:index]) for index in range(len(sizes))]
    w_bias = jnp.transpose(weight_bias, (0, 2, 1))

    group = lax.axis_index("tok") // heads
    weights = sample_weight(lax.dynamic_slice_in_dim(noise_level, group * samples, samples))
    valid = key_mask[None, :]

    def by_chunk(array):
        cut = array[:, 0].reshape(layers, samples, depth, devices, len(sizes), sizes[0])
        cut = jnp.transpose(cut, (4, 0, 1, 2, 3, 5))
        return cut.reshape(len(sizes), layers, samples, depth, devices * sizes[0])

    queries, grads = by_chunk(query_states), by_chunk(output_grad)

    arrived = []
    prepared = None
    for start, rows in zip(starts, sizes):
        bias, *made = forward_rows(
            start, rows, pair_states, weight_in, weight_out, w_bias, prepared
        )
        prepared = prepared or made
        if is_direct(rows, crop):
            bias = bias.reshape(heads, layers, rows, crop)
        else:
            bias = jnp.transpose(bias.reshape(rows, layers, heads, crop), (2, 1, 0, 3))
        if groups > 1:
            bias = jnp.tile(bias, (groups, 1, 1, 1))
        arrived.append(swap(bias))

    returned = []
    d_queries = []
    state = None
    for start, rows, bias in zip(starts, sizes, arrived):
        direct = is_direct(rows, crop)
        if not direct:
            bias = jnp.transpose(bias, (1, 0, 2, 3)).reshape(1, layers, devices * rows, crop)
        d_query, d_key, d_value, d_bias = attend_rows(
            start == 0,
            start + rows == row_count,
            weights,
            bias,
            valid,
            queries[start // rows],
            key_states[:, 0],
            value_states[:, 0],
            grads[start // rows],
            state,
        )
        state = (d_key, d_value)
        d_queries.append(d_query.reshape(layers, samples, depth, devices, rows))
        if not direct:
            d_bias = jnp.transpose(d_bias.reshape(layers, devices, rows, crop), (1, 0, 2, 3))
        returned.append(swap(d_bias))

    sum_rows = 3 * width + lanes
    packed_rows = 8 * devices * -(-sum_rows // (8 * devices))
    doubled = jnp.concatenate([jnp.ones((width,), BF16), jnp.full((width,), 2.0, BF16)])
    prepared = (*prepared, weight_in * doubled[None, :], weight_out * jnp.asarray(0.5, BF16))
    pair_state = None
    for start, rows, d_bias in zip(starts, sizes, returned):
        if groups > 1:
            d_bias = d_bias.reshape(groups, heads, layers, rows, crop).astype(F32)
            d_bias = jnp.sum(d_bias, 0).astype(BF16)
        if is_direct(rows, crop):
            d_bias = d_bias.reshape(lanes, rows, crop)
        else:
            d_bias = jnp.transpose(d_bias, (2, 1, 0, 3)).reshape(rows, lanes, crop)
        make = functools.partial(
            backward_rows,
            direct=is_direct(rows, crop),
            packed_rows=packed_rows,
            pair=pair_states,
            d_bias=d_bias,
            w_bias=w_bias,
            prepared=prepared,
        )
        pair_state = make(start, rows, 0, state=pair_state)
    pair_grad, _, packed = pair_state

    summed = gather_shares(sum_team(sum_pairs(packed)))
    grad_in = summed[: 2 * width].T
    grad_out = summed[2 * width : 3 * width]
    grad_bias = summed[3 * width : sum_rows].reshape(layers, heads, channels)
    grad_bias = jnp.transpose(grad_bias, (0, 2, 1))

    d_query = jnp.concatenate(d_queries, -1).reshape(query_states.shape)
    return (
        pair_grad,
        d_query,
        d_key[:, None],
        d_value[:, None],
        grad_in,
        grad_out,
        grad_bias,
    )


def solution(mesh):
    in_specs = (
        P(("job", "tok"), None, None),
        P(),
        P(),
        P(),
        P("job"),
        P("job"),
        P(None, "tok", "job", None, None),
        P(None, "tok", "job", None, None),
        P(None, "tok", "job", None, None),
        P(None, "tok", "job", None, None),
    )
    out_specs = (
        P(("job", "tok"), None, None),
        P(None, "tok", "job", None, None),
        P(None, "tok", "job", None, None),
        P(None, "tok", "job", None, None),
        P("job", None),
        P("job", None),
        P("job", None, None),
    )
    return jax.shard_map(body, mesh=mesh, in_specs=in_specs, out_specs=out_specs, check_vma=False)
```

```python
import functools
import math

import jax
import jax.numpy as jnp
from jax import lax
from jax.experimental import pallas as pl
from jax.experimental.pallas import tpu as pltpu
from jax.sharding import PartitionSpec as P

LEVELS = 200


sigma_high = 160.0
sigma_low = 0.0004
sigma_data = 16.0
rho_power = 7.0
epsilon = 1e-05
masked_score = -1000000000.0

F32 = jnp.float32
BF16 = jnp.bfloat16


def sample_weight(levels):
    level = levels.astype(jnp.float32)
    top_root = sigma_high ** (1.0 / rho_power)
    low_root = sigma_low ** (1.0 / rho_power)
    sigma_level = (top_root + level / (LEVELS - 1) * (low_root - top_root)) ** rho_power
    return (sigma_level * sigma_level + sigma_data * sigma_data) / (sigma_level + sigma_data) ** 2


def mm(left, right, left_dim=1, right_dim=0):
    return lax.dot_general(
        left, right, (((left_dim,), (right_dim,)), ((), ())), preferred_element_type=F32
    )


def normalize(inputs):
    centered = inputs - jnp.mean(inputs, 0, keepdims=True)
    inv_std = lax.rsqrt(jnp.mean(centered * centered, 0, keepdims=True) + epsilon)
    return centered * inv_std, inv_std


def norm_back(normed, inv_std, upstream):
    return inv_std * (
        upstream
        - jnp.mean(upstream, 0, keepdims=True)
        - normed * jnp.mean(upstream * normed, 0, keepdims=True)
    )


def split_width(width):
    return 256 if width % 256 == 0 else width


def interleave(make_stages, count, lag):
    rows = [make_stages(index) for index in range(count)]
    running = []
    clock = 0
    while rows or running:
        while rows and clock >= lag * (count - len(rows)):
            running.append(rows.pop(0))
        running = [row for row in running if next(row, None) is not None]
        clock += 1


def for_groups(count, group, one_group):
    group = math.gcd(count, group)

    def step(at, carry):
        one_group(at * group, group)
        return carry

    if count == group:
        step(0, 0)
    else:
        lax.fori_loop(0, count // group, step, 0)


def row_step(rows):
    return math.gcd(rows, 8 if rows > 8 else 4)


def is_direct(rows, crop):
    return rows % 8 == 0 and crop % 128 == 0


def forward_kernel(direct, first, taken, emit, base, after, pair_ref, w_bias_ref, *refs):
    refs = list(refs)
    if first:
        w_in_ref, w_out_ref = refs.pop(0), refs.pop(0)
    else:
        w_in_t_ref, w_out_t_ref = refs.pop(0), refs.pop(0)
    taken_ref = refs.pop(0) if taken else None
    if after:
        refs.pop(0)
    bias_ref = refs.pop(0) if emit else None
    if first:
        w_in_t_ref, w_out_t_ref = refs.pop(0), refs.pop(0)
    lines_ref = refs.pop(0)
    width = w_out_t_ref.shape[1]
    layers, heads, channels = w_bias_ref.shape
    piece = split_width(width)
    step = pair_ref.shape[0]
    first_row = base + pl.program_id(0) * step

    if taken:

        @pl.when(pl.program_id(0) == 0)
        def _():
            lines_ref[...] = taken_ref[...]

    if first:

        @pl.when(pl.program_id(0) == 0)
        def _():
            w_in_t = w_in_ref[...].T
            w_in_t_ref[:width, :] = w_in_t[:width] * 0.5
            w_in_t_ref[width:, :] = w_in_t[width:]
            w_out_t_ref[...] = w_out_ref[...].T

    def stages(row):
        pair_float = pair_ref[row].T.astype(F32)
        normed_in = normalize(pair_float)[0].astype(BF16)
        yield True
        lifted = pair_float
        for at in range(0, width, piece):
            half_gate = mm(w_in_t_ref[at : at + piece, :], normed_in)
            up_in = mm(w_in_t_ref[width + at : width + at + piece, :], normed_in)
            yield True
            hidden = (half_gate * (1.0 + jnp.tanh(half_gate)) * up_in).astype(BF16)
            lifted = lifted + mm(w_out_t_ref[:, at : at + piece], hidden)
            yield True
        normed_out = normalize(lifted)[0].astype(BF16)
        yield True
        bias = mm(w_bias_ref[...].reshape(layers * heads, channels), normed_out)
        if direct:
            tiles, total, tile = lines_ref.shape
            rows = total // (layers * heads)
            for layer in range(layers):
                at = pl.ds(layer * rows + first_row + row, heads, stride=layers * rows)
                lines = bias[layer * heads : (layer + 1) * heads]
                for index in range(tiles):
                    lines_ref[index, at, :] = lines[:, index * tile : (index + 1) * tile]
        else:
            bias_ref[row] = bias.astype(BF16)

    for_groups(step, 8, lambda at, count: interleave(lambda i: stages(at + i), count, 0))

    if direct and emit:

        @pl.when(pl.program_id(0) == pl.num_programs(0) - 1)
        def _():
            tiles, _, tile = lines_ref.shape
            for index in range(tiles):
                lines = lines_ref[index].reshape(bias_ref.shape[:2] + (tile,))
                bias_ref[:, :, index * tile : (index + 1) * tile] = lines.astype(BF16)


def whole_spec(array):
    return pl.BlockSpec(array.shape, lambda i: (0,) * len(array.shape))


def forward_rows(
    start, rows, pair, w_in, w_out, w_bias, prepared, base=0, chunk_rows=None, taken=None, after=None
):
    crop, channels = pair.shape[1:]
    layers, heads, _ = w_bias.shape
    lanes = layers * heads
    chunk_rows = chunk_rows or rows
    step = row_step(rows)
    first_step = start // step
    positions = rows * crop
    width = w_out.shape[0]
    direct = is_direct(chunk_rows, crop)
    first = prepared is None
    emit = base + rows == chunk_rows
    shapes, out_specs, scratch = [], [], []
    line_shape = (crop // 128, lanes * chunk_rows, 128) if direct else (1, 8, 128)
    if not emit:
        shapes.append(jax.ShapeDtypeStruct(line_shape, F32))
        out_specs.append(whole_spec(shapes[0]))
    elif direct:
        shapes.append(jax.ShapeDtypeStruct((lanes, chunk_rows, crop), BF16))
        out_specs.append(whole_spec(shapes[0]))
    else:
        shapes.append(jax.ShapeDtypeStruct((rows, lanes, crop), BF16))
        out_specs.append(pl.BlockSpec((step, lanes, crop), lambda i: (i, 0, 0)))
    if emit:
        scratch.append(pltpu.VMEM(line_shape, F32))
    operands = [pair, w_bias, *((w_in, w_out) if first else prepared)]
    if first:
        for shape in (w_in.shape[::-1], w_out.shape[::-1]):
            shapes.append(jax.ShapeDtypeStruct(shape, BF16))
            out_specs.append(whole_spec(shapes[-1]))
    if taken is not None:
        operands.append(taken)
    in_specs = [pl.BlockSpec((step, crop, channels), lambda i: (first_step + i, 0, 0))]
    in_specs += [whole_spec(array) for array in operands[1:]]
    if after is not None:
        operands.append(after)
        in_specs.append(pl.BlockSpec(memory_space=pl.ANY))
    return pl.pallas_call(
        functools.partial(
            forward_kernel, direct, first, taken is not None, emit, base, after is not None
        ),
        grid=(rows // step,),
        in_specs=in_specs,
        out_specs=out_specs,
        out_shape=shapes,
        scratch_shapes=scratch,
        compiler_params=pltpu.CompilerParams(vmem_limit_bytes=56 * 2**20),
        cost_estimate=pl.CostEstimate(
            flops=6 * positions * channels * (3 * width + lanes),
            bytes_accessed=positions * (channels + lanes) * 2,
            transcendentals=positions * width,
        ),
        name="pair_forward",
    )(*operands)


def backward_kernel(
    first,
    last,
    direct,
    base,
    pair_ref,
    d_bias_ref,
    w_bias_ref,
    w_in_t_ref,
    w_out_t_ref,
    w_back_ref,
    w_half_ref,
    *refs,
):
    outs = list(refs[:-1])
    parity_ref = outs.pop(0) if last else None
    if not first:
        before_ref = outs.pop(0)
        outs.pop(0)
    pair_grad_ref, sums_ref = outs.pop(0), outs.pop(0)
    lines_ref = refs[-1]
    width = w_half_ref.shape[0]
    layers, heads, channels = w_bias_ref.shape
    lanes = layers * heads
    piece = split_width(width)
    step = pair_ref.shape[0]
    one, two = jnp.asarray(1.0, BF16), jnp.asarray(2.0, BF16)
    first_row = base + pl.program_id(0) * step

    @pl.when(pl.program_id(0) == 0)
    def _():
        if first:
            sums_ref[...] = jnp.zeros_like(sums_ref)
        else:
            sums_ref[...] = before_ref[...]
        if direct:
            tiles, total, tile = lines_ref.shape
            for index in range(tiles):
                lines = d_bias_ref[:, :, index * tile : (index + 1) * tile].astype(F32)
                lines_ref[index] = lines.reshape(total, tile)

    def read_lines(row):
        if not direct:
            return d_bias_ref[row]
        tiles, total, _ = lines_ref.shape
        rows = total // lanes
        found = []
        for layer in range(layers):
            at = pl.ds(layer * rows + first_row + row, heads, stride=layers * rows)
            found.append(jnp.concatenate([lines_ref[index, at, :] for index in range(tiles)], 1))
        return jnp.concatenate(found, 0).astype(BF16)

    def stages(row):
        pair_float = pair_ref[row].T.astype(F32)
        normed_float, inv_in = normalize(pair_float)
        normed_in = normed_float.astype(BF16)
        yield True
        lifted = pair_float
        kept = []
        for at in range(0, width, piece):
            half_gate = mm(w_in_t_ref[at : at + piece, :], normed_in)
            up_in = mm(w_in_t_ref[width + at : width + at + piece, :], normed_in)
            yield True
            one_plus = (1.0 + jnp.tanh(half_gate)).astype(BF16)
            half_gate, up_in = half_gate.astype(BF16), up_in.astype(BF16)
            silu = half_gate * one_plus
            hidden = silu * up_in
            slope = one_plus * (one + half_gate * (two - one_plus)) * up_in
            kept.append((silu, slope, hidden))
            lifted = lifted + mm(w_out_t_ref[:, at : at + piece], hidden)
            yield True
        out_float, inv_out = normalize(lifted)
        normed_out = out_float.astype(BF16)
        yield True
        d_bias = read_lines(row)
        d_normed = mm(w_bias_ref[...].reshape(lanes, channels), d_bias, 0, 0)
        sums_ref[3 * width : 3 * width + lanes, :] += mm(d_bias, normed_out, 1, 1)
        d_lifted = norm_back(out_float, inv_out, d_normed)
        lifted_half = d_lifted.astype(BF16)
        yield True
        d_normed_in = None
        for index, (silu, slope, hidden) in enumerate(kept):
            at = index * piece
            cols = slice(at, at + piece)
            up_cols = slice(width + at, width + at + piece)
            d_hidden = mm(w_half_ref[cols, :], lifted_half).astype(BF16)
            out_cols = slice(2 * width + at, 2 * width + at + piece)
            sums_ref[out_cols, :] += mm(hidden, lifted_half, 1, 1)
            yield True
            d_gate = d_hidden * slope
            d_up = d_hidden * silu
            sums_ref[cols, :] += mm(d_gate, normed_in, 1, 1)
            sums_ref[up_cols, :] += mm(d_up, normed_in, 1, 1)
            part = mm(w_back_ref[:, cols], d_gate) + mm(w_back_ref[:, up_cols], d_up)
            d_normed_in = part if d_normed_in is None else d_normed_in + part
            yield True
        pair_grad = d_lifted + norm_back(normed_float, inv_in, d_normed_in)
        pair_grad_ref[row] = pair_grad.astype(BF16).T

    for_groups(step, 8, lambda at, count: interleave(lambda i: stages(at + i), count, 0))

    if last:
        keep_ref, send_ref = outs

        @pl.when(pl.program_id(0) == pl.num_programs(0) - 1)
        def _():
            half = sums_ref.shape[0] // 2
            parity = parity_ref[0]
            sums_ref[width : 2 * width, :] = 2.0 * sums_ref[width : 2 * width, :]
            keep_ref[...] = sums_ref[pl.ds(pl.multiple_of(parity * half, 8), half), :]
            other = pl.ds(pl.multiple_of((1 - parity) * half, 8), half)
            send_ref[...] = sums_ref[other, :].astype(BF16)


def backward_rows(start, rows, base, direct, sum_rows, pair, d_bias, w_bias, prepared, state, parity):
    crop, channels = pair.shape[1:]
    layers, heads, _ = w_bias.shape
    lanes = layers * heads
    width = prepared[3].shape[0]
    step = row_step(rows)
    first_step = start // step
    positions = rows * crop
    first, last = start == 0, start + rows == pair.shape[0]
    pair_spec = pl.BlockSpec((step, crop, channels), lambda i: (first_step + i, 0, 0))
    line_spec = whole_spec(d_bias) if direct else pl.BlockSpec((step, lanes, crop), lambda i: (i, 0, 0))
    operands = [pair, d_bias, w_bias, *prepared]
    in_specs = [pair_spec, line_spec] + [whole_spec(array) for array in operands[2:]]
    aliases = {}
    if last:
        operands.append(parity)
        in_specs.append(pl.BlockSpec(memory_space=pltpu.SMEM))
    if not first:
        pair_grad, sums = state
        operands += [sums, pair_grad]
        in_specs += [whole_spec(sums), pl.BlockSpec(memory_space=pl.ANY)]
        aliases = {len(operands) - 1: 0}
    shapes = [
        jax.ShapeDtypeStruct(pair.shape, BF16),
        jax.ShapeDtypeStruct((sum_rows, channels), F32),
    ]
    if last:
        shapes.append(jax.ShapeDtypeStruct((sum_rows // 2, channels), F32))
        shapes.append(jax.ShapeDtypeStruct((sum_rows // 2, channels), BF16))
    out_specs = [pair_spec] + [whole_spec(shape) for shape in shapes[1:]]
    line_rows = lanes * d_bias.shape[1]
    return pl.pallas_call(
        functools.partial(backward_kernel, first, last, direct, base),
        grid=(rows // step,),
        in_specs=in_specs,
        out_specs=out_specs,
        out_shape=shapes,
        input_output_aliases=aliases,
        scratch_shapes=[
            pltpu.VMEM((crop // 128, line_rows, 128) if direct else (1, 8, 128), F32),
        ],
        compiler_params=pltpu.CompilerParams(vmem_limit_bytes=56 * 2**20),
        cost_estimate=pl.CostEstimate(
            flops=6 * positions * channels * (9 * width + 2 * lanes),
            bytes_accessed=positions * (2 * channels + lanes) * 2,
            transcendentals=positions * width,
        ),
        name="pair_backward",
    )(*operands)


def attend_kernel(
    first, last, weight_ref, bias_ref, valid_ref, q_ref, k_ref, v_ref, g_ref, *refs
):
    if first:
        dq_ref, dk_ref, dv_ref, d_bias_ref = refs
    else:
        dk_before_ref, dv_before_ref, _, dq_ref, dk_ref, dv_ref, d_bias_ref = refs
    samples, depth = q_ref.shape[1:3]
    sources, _, rows, crop = bias_ref.shape
    scaling = 1.0 / math.sqrt(depth)
    bias = bias_ref[:, 0].astype(F32).reshape(sources * rows, crop)
    valid = valid_ref[...] > 0
    total = jnp.zeros_like(bias)
    for s in range(samples):
        query, key, value = q_ref[0, s], k_ref[0, s], v_ref[0, s]
        grad_half = (weight_ref[s] * g_ref[0, s].astype(F32)).astype(BF16)
        scores = mm(query, key, 0, 0) * scaling + bias
        scores = jnp.where(valid, scores, masked_score)
        exp_scores = jnp.exp(scores - jnp.max(scores, -1, keepdims=True))
        attention = exp_scores / jnp.sum(exp_scores, -1, keepdims=True)
        d_attention = mm(grad_half, value, 0, 0)
        d_scores = attention * (
            d_attention - jnp.sum(attention * d_attention, -1, keepdims=True)
        )
        total = total + d_scores
        scores_half = d_scores.astype(BF16)
        d_value = mm(grad_half, attention.astype(BF16))
        d_key = mm(query, scores_half)
        dq_ref[0, s] = (mm(key, scores_half, 1, 1) * scaling).astype(BF16)
        if not first:
            d_value = d_value + dv_before_ref[0, s]
            d_key = d_key + dk_before_ref[0, s]
        if last:
            d_key = d_key * scaling
        dv_ref[0, s] = d_value.astype(dv_ref.dtype)
        dk_ref[0, s] = d_key.astype(dk_ref.dtype)
    d_bias_ref[:, 0] = total.astype(BF16).reshape(sources, rows, crop)


def attend_rows(first, last, weights, bias, valid, query, key, value, grad, state, after):
    sources, layers, rows, crop = bias.shape
    samples, depth, row_count = query.shape[1:]
    vec = lambda shape: pl.BlockSpec((1,) + shape[1:], lambda l: (l, 0, 0, 0))
    plane = pl.BlockSpec((sources, 1, rows, crop), lambda l: (0, l, 0, 0))
    in_specs = [
        pl.BlockSpec(memory_space=pltpu.SMEM),
        plane,
        pl.BlockSpec(valid.shape, lambda l: (0, 0)),
        vec(query.shape),
        vec(key.shape),
        vec(value.shape),
        vec(grad.shape),
    ]
    operands = [weights, bias, valid, query, key, value, grad]
    if not first:
        operands += [*state, after]
        in_specs += [vec(key.shape), vec(value.shape), pl.BlockSpec(memory_space=pl.ANY)]
    kind = BF16 if last else F32
    return pl.pallas_call(
        functools.partial(attend_kernel, first, last),
        grid=(layers,),
        in_specs=in_specs,
        out_specs=[vec(query.shape), vec(key.shape), vec(value.shape), plane],
        out_shape=[
            jax.ShapeDtypeStruct(query.shape, BF16),
            jax.ShapeDtypeStruct(key.shape, kind),
            jax.ShapeDtypeStruct(value.shape, kind),
            jax.ShapeDtypeStruct(bias.shape, BF16),
        ],
        compiler_params=pltpu.CompilerParams(vmem_limit_bytes=48 * 2**20),
        cost_estimate=pl.CostEstimate(
            flops=200 * layers * samples * depth * row_count * crop,
            bytes_accessed=layers * crop * (4 * row_count + 12 * samples * depth),
            transcendentals=layers * samples * row_count * crop,
        ),
        name="attention_backward",
    )(*operands)


def swap(array, teams=None):
    return lax.all_to_all(
        array, "tok", split_axis=0, concat_axis=0, tiled=True, axis_index_groups=teams
    )


def sum_pairs(keep, send):
    across = [(index, index ^ 1) for index in range(lax.axis_size("tok"))]
    return (keep + lax.ppermute(send, "tok", across).astype(F32)).astype(BF16)


def sum_team(array):
    devices = lax.axis_size("tok")
    teams = [list(range(odd, devices, 2)) for odd in range(2)]
    members = devices // 2
    parts = swap(array.reshape(members, array.shape[0] // members, array.shape[1]), teams)
    return jnp.sum(parts.astype(F32), 0).astype(BF16)


def gather_shares(share):
    devices = lax.axis_size("tok")
    members = devices // 2
    across = [(index, index ^ 1) for index in range(devices)]
    teams = [list(range(odd, devices, 2)) for odd in range(2)]
    mine = swap(jnp.broadcast_to(share[None], (members,) + share.shape), teams)
    mine = mine.reshape(members * share.shape[0], share.shape[1])
    theirs = lax.ppermute(mine, "tok", across)
    even = lax.axis_index("tok") % 2 == 0
    both = jnp.concatenate([jnp.where(even, mine, theirs), jnp.where(even, theirs, mine)], 0)
    return both.astype(F32)


def body(
    pair_states,
    weight_in,
    weight_out,
    weight_bias,
    key_mask,
    noise_level,
    query_states,
    key_states,
    value_states,
    output_grad,
):
    row_count, crop, channels = pair_states.shape
    layers, _, heads = weight_bias.shape
    width = weight_out.shape[0]
    devices = lax.axis_size("tok")
    groups = devices // heads
    samples, depth = query_states.shape[2:4]
    lanes = heads * layers
    sizes = [row_count]
    if row_count % 16 == 0:
        sizes = [row_count // 2] * 2
    w_bias = jnp.transpose(weight_bias, (0, 2, 1))

    group = lax.axis_index("tok") // heads
    weights = sample_weight(lax.dynamic_slice_in_dim(noise_level, group * samples, samples))
    valid = key_mask[None, :]

    def by_chunk(array):
        cut = array[:, 0].reshape(layers, samples, depth, devices, len(sizes), sizes[0])
        cut = jnp.transpose(cut, (4, 0, 1, 2, 3, 5))
        return cut.reshape(len(sizes), layers, samples, depth, devices * sizes[0])

    queries, grads = by_chunk(query_states), by_chunk(output_grad)

    sum_rows = 3 * width + lanes
    padded_rows = 8 * devices * -(-sum_rows // (8 * devices))
    parity = (lax.axis_index("tok") % 2).astype(jnp.int32).reshape(1)
    doubled = jnp.concatenate([jnp.ones((width,), BF16), jnp.full((width,), 2.0, BF16)])
    scaled = (weight_in * doubled[None, :], weight_out * jnp.asarray(0.5, BF16))
    rows = sizes[0]
    direct = is_direct(rows, crop)

    def forward(start, count, prepared, **more):
        return forward_rows(
            start, count, pair_states, weight_in, weight_out, w_bias, prepared, **more
        )

    def send_bias(bias):
        if direct:
            bias = bias.reshape(heads, layers, rows, crop)
        else:
            bias = jnp.transpose(bias.reshape(rows, layers, heads, crop), (2, 1, 0, 3))
        if groups > 1:
            bias = jnp.tile(bias, (groups, 1, 1, 1))
        return swap(bias)

    def attend(start, bias, state=None, after=None):
        if not direct:
            bias = jnp.transpose(bias, (1, 0, 2, 3)).reshape(1, layers, devices * rows, crop)
        *grads_made, d_bias = attend_rows(
            start == 0,
            start + rows == row_count,
            weights,
            bias,
            valid,
            queries[start // rows],
            key_states[:, 0],
            value_states[:, 0],
            grads[start // rows],
            state,
            after,
        )
        if not direct:
            d_bias = jnp.transpose(d_bias.reshape(layers, devices, rows, crop), (1, 0, 2, 3))
        return grads_made, d_bias

    def send_back(d_bias):
        d_bias = swap(d_bias)
        if groups > 1:
            d_bias = d_bias.reshape(groups, heads, layers, rows, crop).astype(F32)
            d_bias = jnp.sum(d_bias, 0).astype(BF16)
        if direct:
            return d_bias.reshape(lanes, rows, crop)
        return jnp.transpose(d_bias, (2, 1, 0, 3)).reshape(rows, lanes, crop)

    def backward(start, count, base, d_bias, prepared, state=None):
        weights_used = (*prepared, *scaled)
        return backward_rows(
            start,
            count,
            base,
            direct,
            padded_rows,
            pair_states,
            d_bias,
            w_bias,
            weights_used,
            state,
            parity,
        )

    bias, *prepared = forward(0, rows, None)
    bias = send_bias(bias)
    if len(sizes) == 1:
        (d_query, d_key, d_value), d_bias = attend(0, bias)
        d_queries = [d_query]
        pair_grad, _, keep, send = backward(0, rows, 0, send_back(d_bias), prepared)
    else:
        half = rows // 2
        (lines,) = forward(rows, half, prepared, chunk_rows=rows)
        (d_query, *state), d_bias = attend(0, bias)
        d_queries = [d_query]
        (bias,) = forward(
            rows + half,
            half,
            prepared,
            base=half,
            chunk_rows=rows,
            taken=lines,
            after=d_bias,
        )
        d_bias = send_back(d_bias)
        bias = send_bias(bias)
        pair_state = backward(0, half, 0, d_bias, prepared)
        (d_query, d_key, d_value), d_bias_later = attend(rows, bias, state, pair_state[1])
        d_queries.append(d_query)
        d_bias_later = send_back(d_bias_later)
        pair_state = backward(half, half, half, d_bias, prepared, pair_state)
        pair_grad, _, keep, send = backward(rows, rows, 0, d_bias_later, prepared, pair_state)

    summed = gather_shares(sum_team(sum_pairs(keep, send)))
    grad_in = summed[: 2 * width].T
    grad_out = summed[2 * width : 3 * width]
    grad_bias = summed[3 * width : sum_rows].reshape(layers, heads, channels)
    grad_bias = jnp.transpose(grad_bias, (0, 2, 1))

    d_queries = [part.reshape(layers, samples, depth, devices, rows) for part in d_queries]
    d_query = jnp.concatenate(d_queries, -1).reshape(query_states.shape)
    return (
        pair_grad,
        d_query,
        d_key[:, None],
        d_value[:, None],
        grad_in,
        grad_out,
        grad_bias,
    )


def solution(mesh):
    in_specs = (
        P(("job", "tok"), None, None),
        P(),
        P(),
        P(),
        P("job"),
        P("job"),
        P(None, "tok", "job", None, None),
        P(None, "tok", "job", None, None),
        P(None, "tok", "job", None, None),
        P(None, "tok", "job", None, None),
    )
    out_specs = (
        P(("job", "tok"), None, None),
        P(None, "tok", "job", None, None),
        P(None, "tok", "job", None, None),
        P(None, "tok", "job", None, None),
        P("job", None),
        P("job", None),
        P("job", None, None),
    )
    return jax.shard_map(body, mesh=mesh, in_specs=in_specs, out_specs=out_specs, check_vma=False)
```

```python
import functools
import math

import jax
import jax.numpy as jnp
from jax import lax
from jax.experimental import pallas as pl
from jax.experimental.pallas import tpu as pltpu
from jax.sharding import PartitionSpec as P

LEVELS = 200


sigma_high = 160.0
sigma_low = 0.0004
sigma_data = 16.0
rho_power = 7.0
epsilon = 1e-05
masked_score = -1000000000.0

F32 = jnp.float32
BF16 = jnp.bfloat16


def sample_weight(levels):
    level = levels.astype(jnp.float32)
    top_root = sigma_high ** (1.0 / rho_power)
    low_root = sigma_low ** (1.0 / rho_power)
    sigma_level = (top_root + level / (LEVELS - 1) * (low_root - top_root)) ** rho_power
    return (sigma_level * sigma_level + sigma_data * sigma_data) / (sigma_level + sigma_data) ** 2


def mm(left, right, left_dim=1, right_dim=0):
    return lax.dot_general(
        left, right, (((left_dim,), (right_dim,)), ((), ())), preferred_element_type=F32
    )


def normalize(inputs):
    centered = inputs - jnp.mean(inputs, 0, keepdims=True)
    inv_std = lax.rsqrt(jnp.mean(centered * centered, 0, keepdims=True) + epsilon)
    return centered * inv_std, inv_std


def norm_back(normed, inv_std, upstream):
    return inv_std * (
        upstream
        - jnp.mean(upstream, 0, keepdims=True)
        - normed * jnp.mean(upstream * normed, 0, keepdims=True)
    )


def split_width(width):
    return 256 if width % 256 == 0 else width


def interleave(make_stages, count, lag):
    rows = [make_stages(index) for index in range(count)]
    running = []
    clock = 0
    while rows or running:
        while rows and clock >= lag * (count - len(rows)):
            running.append(rows.pop(0))
        running = [row for row in running if next(row, None) is not None]
        clock += 1


def for_groups(count, group, one_group):
    group = math.gcd(count, group)

    def step(at, carry):
        one_group(at * group, group)
        return carry

    if count == group:
        step(0, 0)
    else:
        lax.fori_loop(0, count // group, step, 0)


def row_step(rows):
    return math.gcd(rows, 8 if rows > 8 else 4)


def is_direct(rows, crop):
    return rows % 8 == 0 and crop % 128 == 0


def forward_kernel(direct, first, pair_ref, w_bias_ref, *refs):
    refs = list(refs)
    if first:
        w_in_ref, w_out_ref = refs.pop(0), refs.pop(0)
    else:
        w_in_t_ref, w_out_t_ref = refs.pop(0), refs.pop(0)
    bias_ref = refs.pop(0)
    if first:
        w_in_t_ref, w_out_t_ref = refs.pop(0), refs.pop(0)
    lines_ref = refs.pop(0)
    width = w_out_t_ref.shape[1]
    layers, heads, channels = w_bias_ref.shape
    piece = split_width(width)
    step = pair_ref.shape[0]
    first_row = pl.program_id(0) * step

    if first:

        @pl.when(pl.program_id(0) == 0)
        def _():
            w_in_t = w_in_ref[...].T
            w_in_t_ref[:width, :] = w_in_t[:width] * 0.5
            w_in_t_ref[width:, :] = w_in_t[width:]
            w_out_t_ref[...] = w_out_ref[...].T

    def stages(row):
        pair_float = pair_ref[row].T.astype(F32)
        normed_in = normalize(pair_float)[0].astype(BF16)
        yield True
        hiddens = []
        for at in range(0, width, piece):
            half_gate = mm(w_in_t_ref[at : at + piece, :], normed_in)
            up_in = mm(w_in_t_ref[width + at : width + at + piece, :], normed_in)
            yield True
            hidden = half_gate * (1.0 + jnp.tanh(half_gate)) * up_in
            hiddens.append(hidden.astype(BF16))
            yield True
        lifted = pair_float + mm(w_out_t_ref[...], jnp.concatenate(hiddens, 0))
        yield True
        normed_out = normalize(lifted)[0].astype(BF16)
        yield True
        bias = mm(w_bias_ref[...].reshape(layers * heads, channels), normed_out)
        if direct:
            tiles, total, tile = lines_ref.shape
            rows = total // (layers * heads)
            for layer in range(layers):
                at = pl.ds(layer * rows + first_row + row, heads, stride=layers * rows)
                lines = bias[layer * heads : (layer + 1) * heads]
                for index in range(tiles):
                    lines_ref[index, at, :] = lines[:, index * tile : (index + 1) * tile]
        else:
            bias_ref[row] = bias.astype(BF16)

    for_groups(step, 8, lambda at, count: interleave(lambda i: stages(at + i), count, 0))

    if direct:

        @pl.when(pl.program_id(0) == pl.num_programs(0) - 1)
        def _():
            tiles, _, tile = lines_ref.shape
            for index in range(tiles):
                lines = lines_ref[index].reshape(bias_ref.shape[:2] + (tile,))
                bias_ref[:, :, index * tile : (index + 1) * tile] = lines.astype(BF16)


def whole_spec(array):
    return pl.BlockSpec(array.shape, lambda i: (0,) * len(array.shape))


def forward_rows(start, rows, pair, w_in, w_out, w_bias, prepared):
    crop, channels = pair.shape[1:]
    layers, heads, _ = w_bias.shape
    lanes = layers * heads
    step = row_step(rows)
    first_step = start // step
    positions = rows * crop
    width = w_out.shape[0]
    direct = is_direct(rows, crop)
    first = prepared is None
    line_shape = (lanes, rows, crop) if direct else (rows, lanes, crop)
    shapes = [jax.ShapeDtypeStruct(line_shape, BF16)]
    out_specs = [
        whole_spec(shapes[0])
        if direct
        else pl.BlockSpec((step, lanes, crop), lambda i: (i, 0, 0))
    ]
    operands = [pair, w_bias, *((w_in, w_out) if first else prepared)]
    if first:
        for shape in (w_in.shape[::-1], w_out.shape[::-1]):
            shapes.append(jax.ShapeDtypeStruct(shape, BF16))
            out_specs.append(whole_spec(shapes[-1]))
    return pl.pallas_call(
        functools.partial(forward_kernel, direct, first),
        grid=(rows // step,),
        in_specs=[pl.BlockSpec((step, crop, channels), lambda i: (first_step + i, 0, 0))]
        + [whole_spec(array) for array in operands[1:]],
        out_specs=out_specs,
        out_shape=shapes,
        scratch_shapes=[
            pltpu.VMEM((crop // 128, lanes * rows, 128) if direct else (1, 8, 128), F32),
        ],
        compiler_params=pltpu.CompilerParams(vmem_limit_bytes=56 * 2**20),
        cost_estimate=pl.CostEstimate(
            flops=6 * positions * channels * (3 * width + lanes),
            bytes_accessed=positions * (channels + lanes) * 2,
            transcendentals=positions * width,
        ),
        name="pair_forward",
    )(*operands)


def backward_kernel(
    first,
    last,
    direct,
    pair_ref,
    d_bias_ref,
    w_bias_ref,
    w_in_t_ref,
    w_out_t_ref,
    w_back_ref,
    w_half_ref,
    *refs,
):
    outs = list(refs[:-1])
    parity_ref = outs.pop(0) if last else None
    if not first:
        before_ref = outs.pop(0)
        outs.pop(0)
    pair_grad_ref, sums_ref = outs.pop(0), outs.pop(0)
    lines_ref = refs[-1]
    width = w_half_ref.shape[0]
    layers, heads, channels = w_bias_ref.shape
    lanes = layers * heads
    piece = split_width(width)
    step = pair_ref.shape[0]
    one, two = jnp.asarray(1.0, BF16), jnp.asarray(2.0, BF16)
    first_row = pl.program_id(0) * step

    @pl.when(pl.program_id(0) == 0)
    def _():
        if first:
            sums_ref[...] = jnp.zeros_like(sums_ref)
        else:
            sums_ref[...] = before_ref[...]
        if direct:
            tiles, total, tile = lines_ref.shape
            for index in range(tiles):
                lines = d_bias_ref[:, :, index * tile : (index + 1) * tile].astype(F32)
                lines_ref[index] = lines.reshape(total, tile)

    def read_lines(row):
        if not direct:
            return d_bias_ref[row]
        tiles, total, _ = lines_ref.shape
        rows = total // lanes
        found = []
        for layer in range(layers):
            at = pl.ds(layer * rows + first_row + row, heads, stride=layers * rows)
            found.append(jnp.concatenate([lines_ref[index, at, :] for index in range(tiles)], 1))
        return jnp.concatenate(found, 0).astype(BF16)

    def add_sums(gathered, at, left, right):
        parts = gathered.setdefault(at, [])
        parts.append((left, right))
        if len(parts) == group:
            lefts, rights = (jnp.concatenate(side, 1) for side in zip(*parts))
            sums_ref[at : at + left.shape[0], :] += mm(lefts, rights, 1, 1)

    def stages(row, gathered):
        pair_float = pair_ref[row].T.astype(F32)
        normed_float, inv_in = normalize(pair_float)
        normed_in = normed_float.astype(BF16)
        yield True
        kept = []
        for at in range(0, width, piece):
            half_gate = mm(w_in_t_ref[at : at + piece, :], normed_in)
            up_in = mm(w_in_t_ref[width + at : width + at + piece, :], normed_in)
            yield True
            one_plus = (1.0 + jnp.tanh(half_gate)).astype(BF16)
            half_gate, up_in = half_gate.astype(BF16), up_in.astype(BF16)
            silu = half_gate * one_plus
            hidden = silu * up_in
            slope = one_plus * (one + half_gate * (two - one_plus)) * up_in
            kept.append((silu, slope, hidden))
            yield True
        hidden = jnp.concatenate([hidden for _, _, hidden in kept], 0)
        lifted = pair_float + mm(w_out_t_ref[...], hidden)
        yield True
        out_float, inv_out = normalize(lifted)
        normed_out = out_float.astype(BF16)
        yield True
        d_bias = read_lines(row)
        d_normed = mm(w_bias_ref[...].reshape(lanes, channels), d_bias, 0, 0)
        add_sums(gathered, 3 * width, d_bias, normed_out)
        d_lifted = norm_back(out_float, inv_out, d_normed)
        lifted_half = d_lifted.astype(BF16)
        yield True
        d_normed_in = None
        for index, (silu, slope, hidden) in enumerate(kept):
            at = index * piece
            d_hidden = mm(w_half_ref[at : at + piece, :], lifted_half).astype(BF16)
            add_sums(gathered, 2 * width + at, hidden, lifted_half)
            yield True
            d_both = jnp.concatenate([d_hidden * slope, d_hidden * silu], 0)
            add_sums(gathered, 2 * at, d_both, normed_in)
            part = mm(w_back_ref[:, 2 * at : 2 * at + 2 * piece], d_both)
            d_normed_in = part if d_normed_in is None else d_normed_in + part
            yield True
        pair_grad = d_lifted + norm_back(normed_float, inv_in, d_normed_in)
        pair_grad_ref[row] = pair_grad.astype(BF16).T

    group = math.gcd(step, 8)

    def one_group(at, count):
        gathered = {}
        interleave(lambda index: stages(at + index, gathered), count, 0)

    for_groups(step, group, one_group)

    if last:
        keep_ref, send_ref = outs

        @pl.when(pl.program_id(0) == pl.num_programs(0) - 1)
        def _():
            half = sums_ref.shape[0] // 2
            parity = parity_ref[0]
            gates, ups = [], []
            for at in range(0, 2 * width, 2 * piece):
                gates.append(sums_ref[at : at + piece, :])
                ups.append(2.0 * sums_ref[at + piece : at + 2 * piece, :])
            sums_ref[: 2 * width, :] = jnp.concatenate(gates + ups, 0)
            keep_ref[...] = sums_ref[pl.ds(pl.multiple_of(parity * half, 8), half), :]
            other = pl.ds(pl.multiple_of((1 - parity) * half, 8), half)
            send_ref[...] = sums_ref[other, :].astype(BF16)


def backward_rows(start, rows, direct, sum_rows, pair, d_bias, w_bias, prepared, state, parity):
    crop, channels = pair.shape[1:]
    layers, heads, _ = w_bias.shape
    lanes = layers * heads
    width = prepared[3].shape[0]
    step = row_step(rows)
    first_step = start // step
    positions = rows * crop
    first, last = start == 0, start + rows == pair.shape[0]
    pair_spec = pl.BlockSpec((step, crop, channels), lambda i: (first_step + i, 0, 0))
    line_spec = whole_spec(d_bias) if direct else pl.BlockSpec((step, lanes, crop), lambda i: (i, 0, 0))
    operands = [pair, d_bias, w_bias, *prepared]
    in_specs = [pair_spec, line_spec] + [whole_spec(array) for array in operands[2:]]
    aliases = {}
    if last:
        operands.append(parity)
        in_specs.append(pl.BlockSpec(memory_space=pltpu.SMEM))
    if not first:
        pair_grad, sums = state
        operands += [sums, pair_grad]
        in_specs += [whole_spec(sums), pl.BlockSpec(memory_space=pl.ANY)]
        aliases = {len(operands) - 1: 0}
    shapes = [
        jax.ShapeDtypeStruct(pair.shape, BF16),
        jax.ShapeDtypeStruct((sum_rows, channels), F32),
    ]
    if last:
        shapes.append(jax.ShapeDtypeStruct((sum_rows // 2, channels), F32))
        shapes.append(jax.ShapeDtypeStruct((sum_rows // 2, channels), BF16))
    out_specs = [pair_spec] + [whole_spec(shape) for shape in shapes[1:]]
    line_rows = lanes * d_bias.shape[1]
    return pl.pallas_call(
        functools.partial(backward_kernel, first, last, direct),
        grid=(rows // step,),
        in_specs=in_specs,
        out_specs=out_specs,
        out_shape=shapes,
        input_output_aliases=aliases,
        scratch_shapes=[
            pltpu.VMEM((crop // 128, line_rows, 128) if direct else (1, 8, 128), F32),
        ],
        compiler_params=pltpu.CompilerParams(vmem_limit_bytes=56 * 2**20),
        cost_estimate=pl.CostEstimate(
            flops=6 * positions * channels * (9 * width + 2 * lanes),
            bytes_accessed=positions * (2 * channels + lanes) * 2,
            transcendentals=positions * width,
        ),
        name="pair_backward",
    )(*operands)


def attend_kernel(
    first, last, weight_ref, bias_ref, valid_ref, q_ref, k_ref, v_ref, g_ref, *refs
):
    if first:
        dq_ref, dk_ref, dv_ref, d_bias_ref = refs
    else:
        dk_before_ref, dv_before_ref, dq_ref, dk_ref, dv_ref, d_bias_ref = refs
    samples, depth = q_ref.shape[1:3]
    sources, _, rows, crop = bias_ref.shape
    scaling = 1.0 / math.sqrt(depth)
    bias = bias_ref[:, 0].astype(F32).reshape(sources * rows, crop)
    valid = valid_ref[...] > 0
    total = jnp.zeros_like(bias)
    for s in range(samples):
        query, key, value = q_ref[0, s], k_ref[0, s], v_ref[0, s]
        grad_half = (weight_ref[s] * g_ref[0, s].astype(F32)).astype(BF16)
        scores = mm(query, key, 0, 0) * scaling + bias
        scores = jnp.where(valid, scores, masked_score)
        exp_scores = jnp.exp(scores - jnp.max(scores, -1, keepdims=True))
        attention = exp_scores / jnp.sum(exp_scores, -1, keepdims=True)
        d_attention = mm(grad_half, value, 0, 0)
        d_scores = attention * (
            d_attention - jnp.sum(attention * d_attention, -1, keepdims=True)
        )
        total = total + d_scores
        scores_half = d_scores.astype(BF16)
        d_value = mm(grad_half, attention.astype(BF16))
        d_key = mm(query, scores_half)
        dq_ref[0, s] = (mm(key, scores_half, 1, 1) * scaling).astype(BF16)
        if not first:
            d_value = d_value + dv_before_ref[0, s]
            d_key = d_key + dk_before_ref[0, s]
        if last:
            d_key = d_key * scaling
        dv_ref[0, s] = d_value.astype(dv_ref.dtype)
        dk_ref[0, s] = d_key.astype(dk_ref.dtype)
    d_bias_ref[:, 0] = total.astype(BF16).reshape(sources, rows, crop)


def attend_rows(first, last, weights, bias, valid, query, key, value, grad, state):
    sources, layers, rows, crop = bias.shape
    samples, depth, row_count = query.shape[1:]
    vec = lambda shape: pl.BlockSpec((1,) + shape[1:], lambda l: (l, 0, 0, 0))
    plane = pl.BlockSpec((sources, 1, rows, crop), lambda l: (0, l, 0, 0))
    in_specs = [
        pl.BlockSpec(memory_space=pltpu.SMEM),
        plane,
        pl.BlockSpec(valid.shape, lambda l: (0, 0)),
        vec(query.shape),
        vec(key.shape),
        vec(value.shape),
        vec(grad.shape),
    ]
    operands = [weights, bias, valid, query, key, value, grad]
    if not first:
        operands += list(state)
        in_specs += [vec(key.shape), vec(value.shape)]
    kind = BF16 if last else F32
    return pl.pallas_call(
        functools.partial(attend_kernel, first, last),
        grid=(layers,),
        in_specs=in_specs,
        out_specs=[vec(query.shape), vec(key.shape), vec(value.shape), plane],
        out_shape=[
            jax.ShapeDtypeStruct(query.shape, BF16),
            jax.ShapeDtypeStruct(key.shape, kind),
            jax.ShapeDtypeStruct(value.shape, kind),
            jax.ShapeDtypeStruct(bias.shape, BF16),
        ],
        compiler_params=pltpu.CompilerParams(vmem_limit_bytes=48 * 2**20),
        cost_estimate=pl.CostEstimate(
            flops=200 * layers * samples * depth * row_count * crop,
            bytes_accessed=layers * crop * (4 * row_count + 12 * samples * depth),
            transcendentals=layers * samples * row_count * crop,
        ),
        name="attention_backward",
    )(*operands)


def swap(array, teams=None):
    return lax.all_to_all(
        array, "tok", split_axis=0, concat_axis=0, tiled=True, axis_index_groups=teams
    )


def sum_pairs(keep, send):
    across = [(index, index ^ 1) for index in range(lax.axis_size("tok"))]
    return (keep + lax.ppermute(send, "tok", across).astype(F32)).astype(BF16)


def sum_team(array):
    devices = lax.axis_size("tok")
    teams = [list(range(odd, devices, 2)) for odd in range(2)]
    members = devices // 2
    parts = swap(array.reshape(members, array.shape[0] // members, array.shape[1]), teams)
    return jnp.sum(parts.astype(F32), 0).astype(BF16)


def gather_shares(share):
    devices = lax.axis_size("tok")
    members = devices // 2
    across = [(index, index ^ 1) for index in range(devices)]
    teams = [list(range(odd, devices, 2)) for odd in range(2)]
    mine = swap(jnp.broadcast_to(share[None], (members,) + share.shape), teams)
    mine = mine.reshape(members * share.shape[0], share.shape[1])
    theirs = lax.ppermute(mine, "tok", across)
    even = lax.axis_index("tok") % 2 == 0
    both = jnp.concatenate([jnp.where(even, mine, theirs), jnp.where(even, theirs, mine)], 0)
    return both.astype(F32)


def body(
    pair_states,
    weight_in,
    weight_out,
    weight_bias,
    key_mask,
    noise_level,
    query_states,
    key_states,
    value_states,
    output_grad,
):
    row_count, crop, channels = pair_states.shape
    layers, _, heads = weight_bias.shape
    width = weight_out.shape[0]
    devices = lax.axis_size("tok")
    groups = devices // heads
    samples, depth = query_states.shape[2:4]
    lanes = heads * layers
    sizes = [row_count]
    if row_count % 16 == 0:
        sizes = [row_count // 2] * 2
    w_bias = jnp.transpose(weight_bias, (0, 2, 1))

    group = lax.axis_index("tok") // heads
    weights = sample_weight(lax.dynamic_slice_in_dim(noise_level, group * samples, samples))
    valid = key_mask[None, :]

    def by_chunk(array):
        cut = array[:, 0].reshape(layers, samples, depth, devices, len(sizes), sizes[0])
        cut = jnp.transpose(cut, (4, 0, 1, 2, 3, 5))
        return cut.reshape(len(sizes), layers, samples, depth, devices * sizes[0])

    queries, grads = by_chunk(query_states), by_chunk(output_grad)

    sum_rows = 3 * width + lanes
    padded_rows = 8 * devices * -(-sum_rows // (8 * devices))
    parity = (lax.axis_index("tok") % 2).astype(jnp.int32).reshape(1)
    piece = split_width(width)
    two = jnp.asarray(2.0, BF16)
    columns = []
    for at in range(0, width, piece):
        columns.append(weight_in[:, at : at + piece])
        columns.append(weight_in[:, width + at : width + at + piece] * two)
    scaled = (jnp.concatenate(columns, 1), weight_out * jnp.asarray(0.5, BF16))
    rows = sizes[0]
    direct = is_direct(rows, crop)

    def forward(start, count, prepared):
        return forward_rows(start, count, pair_states, weight_in, weight_out, w_bias, prepared)

    def send_bias(bias):
        if direct:
            bias = bias.reshape(heads, layers, rows, crop)
        else:
            bias = jnp.transpose(bias.reshape(rows, layers, heads, crop), (2, 1, 0, 3))
        if groups > 1:
            bias = jnp.tile(bias, (groups, 1, 1, 1))
        return swap(bias)

    def attend(start, bias, state):
        if not direct:
            bias = jnp.transpose(bias, (1, 0, 2, 3)).reshape(1, layers, devices * rows, crop)
        *grads_made, d_bias = attend_rows(
            start == 0,
            start + rows == row_count,
            weights,
            bias,
            valid,
            queries[start // rows],
            key_states[:, 0],
            value_states[:, 0],
            grads[start // rows],
            state,
        )
        if not direct:
            d_bias = jnp.transpose(d_bias.reshape(layers, devices, rows, crop), (1, 0, 2, 3))
        return grads_made, d_bias

    def send_back(d_bias):
        d_bias = swap(d_bias)
        if groups > 1:
            d_bias = d_bias.reshape(groups, heads, layers, rows, crop).astype(F32)
            d_bias = jnp.sum(d_bias, 0).astype(BF16)
        if direct:
            return d_bias.reshape(lanes, rows, crop)
        return jnp.transpose(d_bias, (2, 1, 0, 3)).reshape(rows, lanes, crop)

    def backward(start, count, d_bias, prepared, state):
        weights_used = (*prepared, *scaled)
        return backward_rows(
            start,
            count,
            direct,
            padded_rows,
            pair_states,
            d_bias,
            w_bias,
            weights_used,
            state,
            parity,
        )

    bias, *prepared = forward(0, rows, None)
    arrived = [send_bias(bias)]
    for start in range(rows, row_count, rows):
        arrived.append(send_bias(*forward(start, rows, prepared)))
    d_queries, returned = [], []
    state = None
    for start, bias in zip(range(0, row_count, rows), arrived):
        (d_query, *state), d_bias = attend(start, bias, state)
        d_queries.append(d_query)
        returned.append(send_back(d_bias))
    d_key, d_value = state
    state = None
    for start, d_bias in zip(range(0, row_count, rows), returned):
        state = backward(start, rows, d_bias, prepared, state)
    pair_grad, _, keep, send = state

    summed = gather_shares(sum_team(sum_pairs(keep, send)))
    grad_in = summed[: 2 * width].T
    grad_out = summed[2 * width : 3 * width]
    grad_bias = summed[3 * width : sum_rows].reshape(layers, heads, channels)
    grad_bias = jnp.transpose(grad_bias, (0, 2, 1))

    d_queries = [part.reshape(layers, samples, depth, devices, rows) for part in d_queries]
    d_query = jnp.concatenate(d_queries, -1).reshape(query_states.shape)
    return (
        pair_grad,
        d_query,
        d_key[:, None],
        d_value[:, None],
        grad_in,
        grad_out,
        grad_bias,
    )


def solution(mesh):
    in_specs = (
        P(("job", "tok"), None, None),
        P(),
        P(),
        P(),
        P("job"),
        P("job"),
        P(None, "tok", "job", None, None),
        P(None, "tok", "job", None, None),
        P(None, "tok", "job", None, None),
        P(None, "tok", "job", None, None),
    )
    out_specs = (
        P(("job", "tok"), None, None),
        P(None, "tok", "job", None, None),
        P(None, "tok", "job", None, None),
        P(None, "tok", "job", None, None),
        P("job", None),
        P("job", None),
        P("job", None, None),
    )
    return jax.shard_map(body, mesh=mesh, in_specs=in_specs, out_specs=out_specs, check_vma=False)
```

```python
import functools
import math

import jax
import jax.numpy as jnp
from jax import lax
from jax.experimental import pallas as pl
from jax.experimental.pallas import tpu as pltpu
from jax.sharding import PartitionSpec as P

LEVELS = 200


sigma_high = 160.0
sigma_low = 0.0004
sigma_data = 16.0
rho_power = 7.0
epsilon = 1e-05
masked_score = -1000000000.0

F32 = jnp.float32
BF16 = jnp.bfloat16


def sample_weight(levels):
    level = levels.astype(jnp.float32)
    top_root = sigma_high ** (1.0 / rho_power)
    low_root = sigma_low ** (1.0 / rho_power)
    sigma_level = (top_root + level / (LEVELS - 1) * (low_root - top_root)) ** rho_power
    return (sigma_level * sigma_level + sigma_data * sigma_data) / (sigma_level + sigma_data) ** 2


def mm(left, right, left_dim=1, right_dim=0):
    return lax.dot_general(
        left, right, (((left_dim,), (right_dim,)), ((), ())), preferred_element_type=F32
    )


def normalize(inputs):
    centered = inputs - jnp.mean(inputs, 0, keepdims=True)
    inv_std = lax.rsqrt(jnp.mean(centered * centered, 0, keepdims=True) + epsilon)
    return centered * inv_std, inv_std


def norm_back(normed, inv_std, upstream):
    return inv_std * (
        upstream
        - jnp.mean(upstream, 0, keepdims=True)
        - normed * jnp.mean(upstream * normed, 0, keepdims=True)
    )


def split_width(width):
    return 256 if width % 256 == 0 else width


def interleave(make_stages, count, lag):
    rows = [make_stages(index) for index in range(count)]
    running = []
    clock = 0
    while rows or running:
        while rows and clock >= lag * (count - len(rows)):
            running.append(rows.pop(0))
        running = [row for row in running if next(row, None) is not None]
        clock += 1


def for_groups(count, group, one_group):
    group = math.gcd(count, group)

    def step(at, carry):
        one_group(at * group, group)
        return carry

    if count == group:
        step(0, 0)
    else:
        lax.fori_loop(0, count // group, step, 0)


def row_step(rows):
    return math.gcd(rows, 8 if rows > 8 else 4)


def is_direct(rows, crop):
    return rows % 8 == 0 and crop % 128 == 0


def forward_kernel(direct, first, pair_ref, w_bias_ref, *refs):
    refs = list(refs)
    if first:
        w_in_ref, w_out_ref = refs.pop(0), refs.pop(0)
    else:
        w_in_t_ref, w_out_t_ref = refs.pop(0), refs.pop(0)
    bias_ref = refs.pop(0)
    if first:
        w_in_t_ref, w_out_t_ref = refs.pop(0), refs.pop(0)
    lines_ref = refs.pop(0)
    width = w_out_t_ref.shape[1]
    layers, heads, channels = w_bias_ref.shape
    piece = split_width(width)
    step = pair_ref.shape[0]
    first_row = pl.program_id(0) * step

    if first:

        @pl.when(pl.program_id(0) == 0)
        def _():
            w_in_t = w_in_ref[...].T
            w_in_t_ref[:width, :] = w_in_t[:width] * 0.5
            w_in_t_ref[width:, :] = w_in_t[width:]
            w_out_t_ref[...] = w_out_ref[...].T

    def stages(row):
        pair_float = pair_ref[row].T.astype(F32)
        normed_in = normalize(pair_float)[0].astype(BF16)
        yield True
        hiddens = []
        for at in range(0, width, piece):
            half_gate = mm(w_in_t_ref[at : at + piece, :], normed_in)
            up_in = mm(w_in_t_ref[width + at : width + at + piece, :], normed_in)
            yield True
            hidden = half_gate * (1.0 + jnp.tanh(half_gate)) * up_in
            hiddens.append(hidden.astype(BF16))
            yield True
        lifted = pair_float + mm(w_out_t_ref[...], jnp.concatenate(hiddens, 0))
        yield True
        normed_out = normalize(lifted)[0].astype(BF16)
        yield True
        bias = mm(w_bias_ref[...].reshape(layers * heads, channels), normed_out)
        if direct:
            tiles, total, tile = lines_ref.shape
            rows = total // (layers * heads)
            for layer in range(layers):
                at = pl.ds(layer * rows + first_row + row, heads, stride=layers * rows)
                lines = bias[layer * heads : (layer + 1) * heads]
                for index in range(tiles):
                    lines_ref[index, at, :] = lines[:, index * tile : (index + 1) * tile]
        else:
            bias_ref[row] = bias.astype(BF16)

    for_groups(step, 8, lambda at, count: interleave(lambda i: stages(at + i), count, 0))

    if direct:

        @pl.when(pl.program_id(0) == pl.num_programs(0) - 1)
        def _():
            tiles, _, tile = lines_ref.shape
            for index in range(tiles):
                lines = lines_ref[index].reshape(bias_ref.shape[:2] + (tile,))
                bias_ref[:, :, index * tile : (index + 1) * tile] = lines.astype(BF16)


def whole_spec(array):
    return pl.BlockSpec(array.shape, lambda i: (0,) * len(array.shape))


def forward_rows(start, rows, pair, w_in, w_out, w_bias, prepared):
    crop, channels = pair.shape[1:]
    layers, heads, _ = w_bias.shape
    lanes = layers * heads
    step = row_step(rows)
    first_step = start // step
    positions = rows * crop
    width = w_out.shape[0]
    direct = is_direct(rows, crop)
    first = prepared is None
    line_shape = (lanes, rows, crop) if direct else (rows, lanes, crop)
    shapes = [jax.ShapeDtypeStruct(line_shape, BF16)]
    out_specs = [
        whole_spec(shapes[0])
        if direct
        else pl.BlockSpec((step, lanes, crop), lambda i: (i, 0, 0))
    ]
    operands = [pair, w_bias, *((w_in, w_out) if first else prepared)]
    if first:
        for shape in (w_in.shape[::-1], w_out.shape[::-1]):
            shapes.append(jax.ShapeDtypeStruct(shape, BF16))
            out_specs.append(whole_spec(shapes[-1]))
    return pl.pallas_call(
        functools.partial(forward_kernel, direct, first),
        grid=(rows // step,),
        in_specs=[pl.BlockSpec((step, crop, channels), lambda i: (first_step + i, 0, 0))]
        + [whole_spec(array) for array in operands[1:]],
        out_specs=out_specs,
        out_shape=shapes,
        scratch_shapes=[
            pltpu.VMEM((crop // 128, lanes * rows, 128) if direct else (1, 8, 128), F32),
        ],
        compiler_params=pltpu.CompilerParams(vmem_limit_bytes=56 * 2**20),
        cost_estimate=pl.CostEstimate(
            flops=6 * positions * channels * (3 * width + lanes),
            bytes_accessed=positions * (channels + lanes) * 2,
            transcendentals=positions * width,
        ),
        name="pair_forward",
    )(*operands)


def backward_kernel(
    first,
    last,
    direct,
    pair_ref,
    d_bias_ref,
    w_bias_ref,
    w_in_t_ref,
    w_out_t_ref,
    w_back_ref,
    w_half_ref,
    *refs,
):
    outs = list(refs[:-1])
    parity_ref = outs.pop(0) if last else None
    if not first:
        before_ref = outs.pop(0)
        outs.pop(0)
    pair_grad_ref, sums_ref = outs.pop(0), outs.pop(0)
    lines_ref = refs[-1]
    width = w_half_ref.shape[0]
    layers, heads, channels = w_bias_ref.shape
    lanes = layers * heads
    piece = split_width(width)
    step = pair_ref.shape[0]
    one, two = jnp.asarray(1.0, BF16), jnp.asarray(2.0, BF16)
    first_row = pl.program_id(0) * step

    @pl.when(pl.program_id(0) == 0)
    def _():
        if first:
            sums_ref[...] = jnp.zeros_like(sums_ref)
        else:
            sums_ref[...] = before_ref[...]
        if direct:
            tiles, total, tile = lines_ref.shape
            for index in range(tiles):
                lines = d_bias_ref[:, :, index * tile : (index + 1) * tile].astype(F32)
                lines_ref[index] = lines.reshape(total, tile)

    def read_lines(row):
        if not direct:
            return d_bias_ref[row]
        tiles, total, _ = lines_ref.shape
        rows = total // lanes
        found = []
        for layer in range(layers):
            at = pl.ds(layer * rows + first_row + row, heads, stride=layers * rows)
            found.append(jnp.concatenate([lines_ref[index, at, :] for index in range(tiles)], 1))
        return jnp.concatenate(found, 0).astype(BF16)

    def add_sums(at, left, right):
        sums_ref[at : at + left.shape[0], :] += mm(left, right, 1, 1)

    def stages(row):
        pair_float = pair_ref[row].T.astype(F32)
        normed_float, inv_in = normalize(pair_float)
        normed_in = normed_float.astype(BF16)
        yield True
        kept = []
        for at in range(0, width, piece):
            half_gate = mm(w_in_t_ref[at : at + piece, :], normed_in)
            up_in = mm(w_in_t_ref[width + at : width + at + piece, :], normed_in)
            yield True
            one_plus = (1.0 + jnp.tanh(half_gate)).astype(BF16)
            half_gate, up_in = half_gate.astype(BF16), up_in.astype(BF16)
            silu = half_gate * one_plus
            hidden = silu * up_in
            slope = one_plus * (one + half_gate * (two - one_plus)) * up_in
            kept.append((silu, slope, hidden))
            yield True
        hidden = jnp.concatenate([hidden for _, _, hidden in kept], 0)
        lifted = pair_float + mm(w_out_t_ref[...], hidden)
        yield True
        out_float, inv_out = normalize(lifted)
        normed_out = out_float.astype(BF16)
        yield True
        d_bias = read_lines(row)
        d_normed = mm(w_bias_ref[...].reshape(lanes, channels), d_bias, 0, 0)
        add_sums(3 * width, d_bias, normed_out)
        d_lifted = norm_back(out_float, inv_out, d_normed)
        lifted_half = d_lifted.astype(BF16)
        yield True
        d_normed_in = None
        for index, (silu, slope, hidden) in enumerate(kept):
            at = index * piece
            d_hidden = mm(w_half_ref[at : at + piece, :], lifted_half).astype(BF16)
            add_sums(2 * width + at, hidden, lifted_half)
            yield True
            d_both = jnp.concatenate([d_hidden * slope, d_hidden * silu], 0)
            add_sums(2 * at, d_both, normed_in)
            part = mm(w_back_ref[:, 2 * at : 2 * at + 2 * piece], d_both)
            d_normed_in = part if d_normed_in is None else d_normed_in + part
            yield True
        pair_grad = d_lifted + norm_back(normed_float, inv_in, d_normed_in)
        pair_grad_ref[row] = pair_grad.astype(BF16).T

    for_groups(step, 8, lambda at, count: interleave(lambda i: stages(at + i), count, 0))

    if last:
        keep_ref, send_ref = outs

        @pl.when(pl.program_id(0) == pl.num_programs(0) - 1)
        def _():
            half = sums_ref.shape[0] // 2
            parity = parity_ref[0]
            gates, ups = [], []
            for at in range(0, 2 * width, 2 * piece):
                gates.append(sums_ref[at : at + piece, :])
                ups.append(2.0 * sums_ref[at + piece : at + 2 * piece, :])
            sums_ref[: 2 * width, :] = jnp.concatenate(gates + ups, 0)
            keep_ref[...] = sums_ref[pl.ds(pl.multiple_of(parity * half, 8), half), :]
            other = pl.ds(pl.multiple_of((1 - parity) * half, 8), half)
            send_ref[...] = sums_ref[other, :].astype(BF16)


def backward_rows(start, rows, direct, sum_rows, pair, d_bias, w_bias, prepared, state, parity):
    crop, channels = pair.shape[1:]
    layers, heads, _ = w_bias.shape
    lanes = layers * heads
    width = prepared[3].shape[0]
    step = row_step(rows)
    first_step = start // step
    positions = rows * crop
    first, last = start == 0, start + rows == pair.shape[0]
    pair_spec = pl.BlockSpec((step, crop, channels), lambda i: (first_step + i, 0, 0))
    line_spec = whole_spec(d_bias) if direct else pl.BlockSpec((step, lanes, crop), lambda i: (i, 0, 0))
    operands = [pair, d_bias, w_bias, *prepared]
    in_specs = [pair_spec, line_spec] + [whole_spec(array) for array in operands[2:]]
    aliases = {}
    if last:
        operands.append(parity)
        in_specs.append(pl.BlockSpec(memory_space=pltpu.SMEM))
    if not first:
        pair_grad, sums = state
        operands += [sums, pair_grad]
        in_specs += [whole_spec(sums), pl.BlockSpec(memory_space=pl.ANY)]
        aliases = {len(operands) - 1: 0}
    shapes = [
        jax.ShapeDtypeStruct(pair.shape, BF16),
        jax.ShapeDtypeStruct((sum_rows, channels), F32),
    ]
    if last:
        shapes.append(jax.ShapeDtypeStruct((sum_rows // 2, channels), F32))
        shapes.append(jax.ShapeDtypeStruct((sum_rows // 2, channels), BF16))
    out_specs = [pair_spec] + [whole_spec(shape) for shape in shapes[1:]]
    line_rows = lanes * d_bias.shape[1]
    return pl.pallas_call(
        functools.partial(backward_kernel, first, last, direct),
        grid=(rows // step,),
        in_specs=in_specs,
        out_specs=out_specs,
        out_shape=shapes,
        input_output_aliases=aliases,
        scratch_shapes=[
            pltpu.VMEM((crop // 128, line_rows, 128) if direct else (1, 8, 128), F32),
        ],
        compiler_params=pltpu.CompilerParams(vmem_limit_bytes=56 * 2**20),
        cost_estimate=pl.CostEstimate(
            flops=6 * positions * channels * (9 * width + 2 * lanes),
            bytes_accessed=positions * (2 * channels + lanes) * 2,
            transcendentals=positions * width,
        ),
        name="pair_backward",
    )(*operands)


def attend_kernel(
    first, last, weight_ref, bias_ref, valid_ref, q_ref, k_ref, v_ref, g_ref, *refs
):
    if first:
        dq_ref, dk_ref, dv_ref, d_bias_ref = refs
    else:
        dk_before_ref, dv_before_ref, dq_ref, dk_ref, dv_ref, d_bias_ref = refs
    samples, depth = q_ref.shape[1:3]
    sources, _, rows, crop = bias_ref.shape
    scaling = 1.0 / math.sqrt(depth)
    bias = bias_ref[:, 0].astype(F32).reshape(sources * rows, crop)
    valid = valid_ref[...] > 0
    total = jnp.zeros_like(bias)
    for s in range(samples):
        query, key, value = q_ref[0, s], k_ref[0, s], v_ref[0, s]
        grad_half = (weight_ref[s] * g_ref[0, s].astype(F32)).astype(BF16)
        scores = mm(query, key, 0, 0) * scaling + bias
        scores = jnp.where(valid, scores, masked_score)
        exp_scores = jnp.exp(scores - jnp.max(scores, -1, keepdims=True))
        attention = exp_scores / jnp.sum(exp_scores, -1, keepdims=True)
        d_attention = mm(grad_half, value, 0, 0)
        d_scores = attention * (
            d_attention - jnp.sum(attention * d_attention, -1, keepdims=True)
        )
        total = total + d_scores
        scores_half = d_scores.astype(BF16)
        d_value = mm(grad_half, attention.astype(BF16))
        d_key = mm(query, scores_half)
        dq_ref[0, s] = (mm(key, scores_half, 1, 1) * scaling).astype(BF16)
        if not first:
            d_value = d_value + dv_before_ref[0, s]
            d_key = d_key + dk_before_ref[0, s]
        if last:
            d_key = d_key * scaling
        dv_ref[0, s] = d_value.astype(dv_ref.dtype)
        dk_ref[0, s] = d_key.astype(dk_ref.dtype)
    d_bias_ref[:, 0] = total.astype(BF16).reshape(sources, rows, crop)


def attend_rows(first, last, weights, bias, valid, query, key, value, grad, state):
    sources, layers, rows, crop = bias.shape
    samples, depth, row_count = query.shape[1:]
    vec = lambda shape: pl.BlockSpec((1,) + shape[1:], lambda l: (l, 0, 0, 0))
    plane = pl.BlockSpec((sources, 1, rows, crop), lambda l: (0, l, 0, 0))
    in_specs = [
        pl.BlockSpec(memory_space=pltpu.SMEM),
        plane,
        pl.BlockSpec(valid.shape, lambda l: (0, 0)),
        vec(query.shape),
        vec(key.shape),
        vec(value.shape),
        vec(grad.shape),
    ]
    operands = [weights, bias, valid, query, key, value, grad]
    if not first:
        operands += list(state)
        in_specs += [vec(key.shape), vec(value.shape)]
    kind = BF16 if last else F32
    return pl.pallas_call(
        functools.partial(attend_kernel, first, last),
        grid=(layers,),
        in_specs=in_specs,
        out_specs=[vec(query.shape), vec(key.shape), vec(value.shape), plane],
        out_shape=[
            jax.ShapeDtypeStruct(query.shape, BF16),
            jax.ShapeDtypeStruct(key.shape, kind),
            jax.ShapeDtypeStruct(value.shape, kind),
            jax.ShapeDtypeStruct(bias.shape, BF16),
        ],
        compiler_params=pltpu.CompilerParams(vmem_limit_bytes=48 * 2**20),
        cost_estimate=pl.CostEstimate(
            flops=200 * layers * samples * depth * row_count * crop,
            bytes_accessed=layers * crop * (4 * row_count + 12 * samples * depth),
            transcendentals=layers * samples * row_count * crop,
        ),
        name="attention_backward",
    )(*operands)


def swap(array, teams=None):
    return lax.all_to_all(
        array, "tok", split_axis=0, concat_axis=0, tiled=True, axis_index_groups=teams
    )


def sum_pairs(keep, send):
    across = [(index, index ^ 1) for index in range(lax.axis_size("tok"))]
    return (keep + lax.ppermute(send, "tok", across).astype(F32)).astype(BF16)


def sum_team(array):
    devices = lax.axis_size("tok")
    teams = [list(range(odd, devices, 2)) for odd in range(2)]
    members = devices // 2
    parts = swap(array.reshape(members, array.shape[0] // members, array.shape[1]), teams)
    return jnp.sum(parts.astype(F32), 0).astype(BF16)


def finish_kernel(parity_ref, mine_ref, theirs_ref, in_ref, out_ref, bias_ref):
    mine, theirs = mine_ref[...].astype(F32), theirs_ref[...].astype(F32)
    even = parity_ref[0] == 0
    summed = jnp.concatenate([jnp.where(even, mine, theirs), jnp.where(even, theirs, mine)], 0)
    done = in_ref.shape[1]
    in_ref[...] = summed[:done].T
    out_ref[...] = summed[done : done + out_ref.shape[0]]
    done += out_ref.shape[0]
    bias_ref[...] = summed[done : done + bias_ref.shape[0]]


def gather_sums(share, parity, width, lanes):
    devices = lax.axis_size("tok")
    members = devices // 2
    channels = share.shape[1]
    across = [(index, index ^ 1) for index in range(devices)]
    teams = [list(range(odd, devices, 2)) for odd in range(2)]
    mine = swap(jnp.broadcast_to(share[None], (members,) + share.shape), teams)
    mine = mine.reshape(members * share.shape[0], channels)
    theirs = lax.ppermute(mine, "tok", across)
    return pl.pallas_call(
        finish_kernel,
        in_specs=[
            pl.BlockSpec(memory_space=pltpu.SMEM),
            pl.BlockSpec(memory_space=pltpu.VMEM),
            pl.BlockSpec(memory_space=pltpu.VMEM),
        ],
        out_shape=[
            jax.ShapeDtypeStruct((channels, 2 * width), F32),
            jax.ShapeDtypeStruct((width, channels), F32),
            jax.ShapeDtypeStruct((lanes, channels), F32),
        ],
        compiler_params=pltpu.CompilerParams(vmem_limit_bytes=32 * 2**20),
        name="weight_grads",
    )(parity, mine, theirs)


def body(
    pair_states,
    weight_in,
    weight_out,
    weight_bias,
    key_mask,
    noise_level,
    query_states,
    key_states,
    value_states,
    output_grad,
):
    row_count, crop, channels = pair_states.shape
    layers, _, heads = weight_bias.shape
    width = weight_out.shape[0]
    devices = lax.axis_size("tok")
    groups = devices // heads
    samples, depth = query_states.shape[2:4]
    lanes = heads * layers
    sizes = [row_count]
    if row_count % 16 == 0:
        sizes = [row_count // 2] * 2
    w_bias = jnp.transpose(weight_bias, (0, 2, 1))

    group = lax.axis_index("tok") // heads
    weights = sample_weight(lax.dynamic_slice_in_dim(noise_level, group * samples, samples))
    valid = key_mask[None, :]

    def by_chunk(array):
        cut = array[:, 0].reshape(layers, samples, depth, devices, len(sizes), sizes[0])
        cut = jnp.transpose(cut, (4, 0, 1, 2, 3, 5))
        return cut.reshape(len(sizes), layers, samples, depth, devices * sizes[0])

    queries, grads = by_chunk(query_states), by_chunk(output_grad)

    sum_rows = 3 * width + lanes
    padded_rows = 8 * devices * -(-sum_rows // (8 * devices))
    parity = (lax.axis_index("tok") % 2).astype(jnp.int32).reshape(1)
    piece = split_width(width)
    two = jnp.asarray(2.0, BF16)
    columns = []
    for at in range(0, width, piece):
        columns.append(weight_in[:, at : at + piece])
        columns.append(weight_in[:, width + at : width + at + piece] * two)
    scaled = (jnp.concatenate(columns, 1), weight_out * jnp.asarray(0.5, BF16))
    rows = sizes[0]
    direct = is_direct(rows, crop)

    def forward(start, count, prepared):
        return forward_rows(start, count, pair_states, weight_in, weight_out, w_bias, prepared)

    def send_bias(bias):
        if direct:
            bias = bias.reshape(heads, layers, rows, crop)
        else:
            bias = jnp.transpose(bias.reshape(rows, layers, heads, crop), (2, 1, 0, 3))
        if groups > 1:
            bias = jnp.tile(bias, (groups, 1, 1, 1))
        return swap(bias)

    def attend(start, bias, state):
        if not direct:
            bias = jnp.transpose(bias, (1, 0, 2, 3)).reshape(1, layers, devices * rows, crop)
        *grads_made, d_bias = attend_rows(
            start == 0,
            start + rows == row_count,
            weights,
            bias,
            valid,
            queries[start // rows],
            key_states[:, 0],
            value_states[:, 0],
            grads[start // rows],
            state,
        )
        if not direct:
            d_bias = jnp.transpose(d_bias.reshape(layers, devices, rows, crop), (1, 0, 2, 3))
        return grads_made, d_bias

    def send_back(d_bias):
        d_bias = swap(d_bias)
        if groups > 1:
            d_bias = d_bias.reshape(groups, heads, layers, rows, crop).astype(F32)
            d_bias = jnp.sum(d_bias, 0).astype(BF16)
        if direct:
            return d_bias.reshape(lanes, rows, crop)
        return jnp.transpose(d_bias, (2, 1, 0, 3)).reshape(rows, lanes, crop)

    def backward(start, count, d_bias, prepared, state):
        weights_used = (*prepared, *scaled)
        return backward_rows(
            start,
            count,
            direct,
            padded_rows,
            pair_states,
            d_bias,
            w_bias,
            weights_used,
            state,
            parity,
        )

    bias, *prepared = forward(0, rows, None)
    arrived = [send_bias(bias)]
    for start in range(rows, row_count, rows):
        arrived.append(send_bias(*forward(start, rows, prepared)))
    d_queries, returned = [], []
    state = None
    for start, bias in zip(range(0, row_count, rows), arrived):
        (d_query, *state), d_bias = attend(start, bias, state)
        d_queries.append(d_query)
        returned.append(send_back(d_bias))
    d_key, d_value = state
    state = None
    for start, d_bias in zip(range(0, row_count, rows), returned):
        state = backward(start, rows, d_bias, prepared, state)
    pair_grad, _, keep, send = state

    share = sum_team(sum_pairs(keep, send))
    grad_in, grad_out, grad_bias = gather_sums(share, parity, width, lanes)
    grad_bias = jnp.transpose(grad_bias.reshape(layers, heads, channels), (0, 2, 1))

    d_queries = [part.reshape(layers, samples, depth, devices, rows) for part in d_queries]
    d_query = jnp.concatenate(d_queries, -1).reshape(query_states.shape)
    return (
        pair_grad,
        d_query,
        d_key[:, None],
        d_value[:, None],
        grad_in,
        grad_out,
        grad_bias,
    )


def solution(mesh):
    in_specs = (
        P(("job", "tok"), None, None),
        P(),
        P(),
        P(),
        P("job"),
        P("job"),
        P(None, "tok", "job", None, None),
        P(None, "tok", "job", None, None),
        P(None, "tok", "job", None, None),
        P(None, "tok", "job", None, None),
    )
    out_specs = (
        P(("job", "tok"), None, None),
        P(None, "tok", "job", None, None),
        P(None, "tok", "job", None, None),
        P(None, "tok", "job", None, None),
        P("job", None),
        P("job", None),
        P("job", None, None),
    )
    return jax.shard_map(body, mesh=mesh, in_specs=in_specs, out_specs=out_specs, check_vma=False)
```

```python
import functools
import math

import jax
import jax.numpy as jnp
from jax import lax
from jax.experimental import pallas as pl
from jax.experimental.pallas import tpu as pltpu
from jax.sharding import PartitionSpec as P

LEVELS = 200


sigma_high = 160.0
sigma_low = 0.0004
sigma_data = 16.0
rho_power = 7.0
epsilon = 1e-05
masked_score = -1000000000.0

F32 = jnp.float32
BF16 = jnp.bfloat16


def sample_weight(levels):
    level = levels.astype(jnp.float32)
    top_root = sigma_high ** (1.0 / rho_power)
    low_root = sigma_low ** (1.0 / rho_power)
    sigma_level = (top_root + level / (LEVELS - 1) * (low_root - top_root)) ** rho_power
    return (sigma_level * sigma_level + sigma_data * sigma_data) / (sigma_level + sigma_data) ** 2


def mm(left, right, left_dim=1, right_dim=0):
    return lax.dot_general(
        left, right, (((left_dim,), (right_dim,)), ((), ())), preferred_element_type=F32
    )


def normalize(inputs):
    centered = inputs - jnp.mean(inputs, 0, keepdims=True)
    inv_std = lax.rsqrt(jnp.mean(centered * centered, 0, keepdims=True) + epsilon)
    return centered * inv_std, inv_std


def norm_back(normed, inv_std, upstream):
    return inv_std * (
        upstream
        - jnp.mean(upstream, 0, keepdims=True)
        - normed * jnp.mean(upstream * normed, 0, keepdims=True)
    )


def split_width(width):
    return 256 if width % 256 == 0 else width


def interleave(make_stages, count, lag):
    rows = [make_stages(index) for index in range(count)]
    running = []
    clock = 0
    while rows or running:
        while rows and clock >= lag * (count - len(rows)):
            running.append(rows.pop(0))
        running = [row for row in running if next(row, None) is not None]
        clock += 1


def for_groups(count, group, one_group):
    group = math.gcd(count, group)

    def step(at, carry):
        one_group(at * group, group)
        return carry

    if count == group:
        step(0, 0)
    else:
        lax.fori_loop(0, count // group, step, 0)


def row_step(rows):
    return math.gcd(rows, 8 if rows > 8 else 4)


def is_direct(rows, crop):
    return rows % 8 == 0 and crop % 128 == 0


def forward_kernel(direct, first, pair_ref, w_bias_ref, *refs):
    refs = list(refs)
    if first:
        w_in_ref, w_out_ref = refs.pop(0), refs.pop(0)
    else:
        w_in_t_ref, w_out_t_ref = refs.pop(0), refs.pop(0)
    bias_ref, normed_ref, inv_ref = refs.pop(0), refs.pop(0), refs.pop(0)
    if first:
        w_in_t_ref, w_out_t_ref = refs.pop(0), refs.pop(0)
    lines_ref = refs.pop(0)
    width = w_out_t_ref.shape[1]
    layers, heads, channels = w_bias_ref.shape
    piece = split_width(width)
    step = pair_ref.shape[0]
    first_row = pl.program_id(0) * step

    if first:

        @pl.when(pl.program_id(0) == 0)
        def _():
            w_in_t = w_in_ref[...].T
            w_in_t_ref[:width, :] = w_in_t[:width] * 0.5
            w_in_t_ref[width:, :] = w_in_t[width:]
            w_out_t_ref[...] = w_out_ref[...].T

    def stages(row):
        pair_float = pair_ref[row].T.astype(F32)
        normed_float, inv_in = normalize(pair_float)
        normed_in = normed_float.astype(BF16)
        normed_ref[row, :channels, :] = normed_in
        inv_ref[row, 0:1, :] = inv_in
        yield True
        hiddens = []
        for at in range(0, width, piece):
            half_gate = mm(w_in_t_ref[at : at + piece, :], normed_in)
            up_in = mm(w_in_t_ref[width + at : width + at + piece, :], normed_in)
            yield True
            hidden = half_gate * (1.0 + jnp.tanh(half_gate)) * up_in
            hiddens.append(hidden.astype(BF16))
            yield True
        lifted = pair_float + mm(w_out_t_ref[...], jnp.concatenate(hiddens, 0))
        yield True
        normed_float, inv_out = normalize(lifted)
        normed_out = normed_float.astype(BF16)
        normed_ref[row, channels:, :] = normed_out
        inv_ref[row, 1:2, :] = inv_out
        yield True
        bias = mm(w_bias_ref[...].reshape(layers * heads, channels), normed_out)
        if direct:
            tiles, total, tile = lines_ref.shape
            rows = total // (layers * heads)
            for layer in range(layers):
                at = pl.ds(layer * rows + first_row + row, heads, stride=layers * rows)
                lines = bias[layer * heads : (layer + 1) * heads]
                for index in range(tiles):
                    lines_ref[index, at, :] = lines[:, index * tile : (index + 1) * tile]
        else:
            bias_ref[row] = bias.astype(BF16)

    for_groups(step, 8, lambda at, count: interleave(lambda i: stages(at + i), count, 0))

    if direct:

        @pl.when(pl.program_id(0) == pl.num_programs(0) - 1)
        def _():
            tiles, _, tile = lines_ref.shape
            for index in range(tiles):
                lines = lines_ref[index].reshape(bias_ref.shape[:2] + (tile,))
                bias_ref[:, :, index * tile : (index + 1) * tile] = lines.astype(BF16)


def whole_spec(array):
    return pl.BlockSpec(array.shape, lambda i: (0,) * len(array.shape))


def forward_rows(start, rows, pair, w_in, w_out, w_bias, prepared):
    crop, channels = pair.shape[1:]
    layers, heads, _ = w_bias.shape
    lanes = layers * heads
    step = row_step(rows)
    first_step = start // step
    positions = rows * crop
    width = w_out.shape[0]
    direct = is_direct(rows, crop)
    first = prepared is None
    line_shape = (lanes, rows, crop) if direct else (rows, lanes, crop)
    shapes = [jax.ShapeDtypeStruct(line_shape, BF16)]
    out_specs = [
        whole_spec(shapes[0])
        if direct
        else pl.BlockSpec((step, lanes, crop), lambda i: (i, 0, 0))
    ]
    for height, kind in ((2 * channels, BF16), (2, F32)):
        shapes.append(jax.ShapeDtypeStruct((rows, height, crop), kind))
        out_specs.append(pl.BlockSpec((step, height, crop), lambda i: (i, 0, 0)))
    operands = [pair, w_bias, *((w_in, w_out) if first else prepared)]
    if first:
        for shape in (w_in.shape[::-1], w_out.shape[::-1]):
            shapes.append(jax.ShapeDtypeStruct(shape, BF16))
            out_specs.append(whole_spec(shapes[-1]))
    return pl.pallas_call(
        functools.partial(forward_kernel, direct, first),
        grid=(rows // step,),
        in_specs=[pl.BlockSpec((step, crop, channels), lambda i: (first_step + i, 0, 0))]
        + [whole_spec(array) for array in operands[1:]],
        out_specs=out_specs,
        out_shape=shapes,
        scratch_shapes=[
            pltpu.VMEM((crop // 128, lanes * rows, 128) if direct else (1, 8, 128), F32),
        ],
        compiler_params=pltpu.CompilerParams(vmem_limit_bytes=56 * 2**20),
        cost_estimate=pl.CostEstimate(
            flops=6 * positions * channels * (3 * width + lanes),
            bytes_accessed=positions * (channels + lanes) * 2,
            transcendentals=positions * width,
        ),
        name="pair_forward",
    )(*operands)


def backward_kernel(
    first,
    last,
    direct,
    normed_ref,
    inv_ref,
    d_bias_ref,
    w_bias_ref,
    w_in_t_ref,
    w_back_ref,
    w_half_ref,
    *refs,
):
    outs = list(refs[:-1])
    parity_ref = outs.pop(0) if last else None
    if not first:
        before_ref = outs.pop(0)
        outs.pop(0)
    pair_grad_ref, sums_ref = outs.pop(0), outs.pop(0)
    lines_ref = refs[-1]
    width = w_half_ref.shape[0]
    layers, heads, channels = w_bias_ref.shape
    lanes = layers * heads
    piece = split_width(width)
    step = normed_ref.shape[0]
    one, two = jnp.asarray(1.0, BF16), jnp.asarray(2.0, BF16)
    first_row = pl.program_id(0) * step

    @pl.when(pl.program_id(0) == 0)
    def _():
        if first:
            sums_ref[...] = jnp.zeros_like(sums_ref)
        else:
            sums_ref[...] = before_ref[...]
        if direct:
            tiles, total, tile = lines_ref.shape
            for index in range(tiles):
                lines = d_bias_ref[:, :, index * tile : (index + 1) * tile].astype(F32)
                lines_ref[index] = lines.reshape(total, tile)

    def read_lines(row):
        if not direct:
            return d_bias_ref[row]
        tiles, total, _ = lines_ref.shape
        rows = total // lanes
        found = []
        for layer in range(layers):
            at = pl.ds(layer * rows + first_row + row, heads, stride=layers * rows)
            found.append(jnp.concatenate([lines_ref[index, at, :] for index in range(tiles)], 1))
        return jnp.concatenate(found, 0).astype(BF16)

    def add_sums(at, left, right):
        sums_ref[at : at + left.shape[0], :] += mm(left, right, 1, 1)

    def stages(row):
        normed_in, normed_out = normed_ref[row, :channels, :], normed_ref[row, channels:, :]
        inv_in, inv_out = inv_ref[row, 0:1, :], inv_ref[row, 1:2, :]
        kept = []
        for at in range(0, width, piece):
            half_gate = mm(w_in_t_ref[at : at + piece, :], normed_in)
            up_in = mm(w_in_t_ref[width + at : width + at + piece, :], normed_in)
            yield True
            one_plus = (1.0 + jnp.tanh(half_gate)).astype(BF16)
            half_gate, up_in = half_gate.astype(BF16), up_in.astype(BF16)
            silu = half_gate * one_plus
            hidden = silu * up_in
            slope = one_plus * (one + half_gate * (two - one_plus)) * up_in
            kept.append((silu, slope, hidden))
            yield True
        d_bias = read_lines(row)
        d_normed = mm(w_bias_ref[...].reshape(lanes, channels), d_bias, 0, 0)
        add_sums(3 * width, d_bias, normed_out)
        d_lifted = norm_back(normed_out.astype(F32), inv_out, d_normed)
        lifted_half = d_lifted.astype(BF16)
        yield True
        d_normed_in = None
        for index, (silu, slope, hidden) in enumerate(kept):
            at = index * piece
            d_hidden = mm(w_half_ref[at : at + piece, :], lifted_half).astype(BF16)
            add_sums(2 * width + at, hidden, lifted_half)
            yield True
            d_both = jnp.concatenate([d_hidden * slope, d_hidden * silu], 0)
            add_sums(2 * at, d_both, normed_in)
            part = mm(w_back_ref[:, 2 * at : 2 * at + 2 * piece], d_both)
            d_normed_in = part if d_normed_in is None else d_normed_in + part
            yield True
        pair_grad = d_lifted + norm_back(normed_in.astype(F32), inv_in, d_normed_in)
        pair_grad_ref[row] = pair_grad.astype(BF16).T

    for_groups(step, 8, lambda at, count: interleave(lambda i: stages(at + i), count, 0))

    if last:
        keep_ref, send_ref = outs

        @pl.when(pl.program_id(0) == pl.num_programs(0) - 1)
        def _():
            half = sums_ref.shape[0] // 2
            parity = parity_ref[0]
            gates, ups = [], []
            for at in range(0, 2 * width, 2 * piece):
                gates.append(sums_ref[at : at + piece, :])
                ups.append(2.0 * sums_ref[at + piece : at + 2 * piece, :])
            sums_ref[: 2 * width, :] = jnp.concatenate(gates + ups, 0)
            keep_ref[...] = sums_ref[pl.ds(pl.multiple_of(parity * half, 8), half), :]
            other = pl.ds(pl.multiple_of((1 - parity) * half, 8), half)
            send_ref[...] = sums_ref[other, :].astype(BF16)


def backward_rows(
    start, rows, direct, sum_rows, shape, stored, d_bias, w_bias, prepared, state, parity
):
    crop, channels = shape[1:]
    layers, heads, _ = w_bias.shape
    lanes = layers * heads
    width = prepared[2].shape[0]
    step = row_step(rows)
    first_step = start // step
    positions = rows * crop
    first, last = start == 0, start + rows == shape[0]
    pair_spec = pl.BlockSpec((step, crop, channels), lambda i: (first_step + i, 0, 0))
    line_spec = whole_spec(d_bias) if direct else pl.BlockSpec((step, lanes, crop), lambda i: (i, 0, 0))
    operands = [*stored, d_bias, w_bias, *prepared]
    in_specs = [
        pl.BlockSpec((step,) + array.shape[1:], lambda i: (i, 0, 0)) for array in stored
    ]
    in_specs += [line_spec] + [whole_spec(array) for array in operands[len(stored) + 1 :]]
    aliases = {}
    if last:
        operands.append(parity)
        in_specs.append(pl.BlockSpec(memory_space=pltpu.SMEM))
    if not first:
        pair_grad, sums = state
        operands += [sums, pair_grad]
        in_specs += [whole_spec(sums), pl.BlockSpec(memory_space=pl.ANY)]
        aliases = {len(operands) - 1: 0}
    shapes = [
        jax.ShapeDtypeStruct(shape, BF16),
        jax.ShapeDtypeStruct((sum_rows, channels), F32),
    ]
    if last:
        shapes.append(jax.ShapeDtypeStruct((sum_rows // 2, channels), F32))
        shapes.append(jax.ShapeDtypeStruct((sum_rows // 2, channels), BF16))
    out_specs = [pair_spec] + [whole_spec(shape) for shape in shapes[1:]]
    line_rows = lanes * d_bias.shape[1]
    return pl.pallas_call(
        functools.partial(backward_kernel, first, last, direct),
        grid=(rows // step,),
        in_specs=in_specs,
        out_specs=out_specs,
        out_shape=shapes,
        input_output_aliases=aliases,
        scratch_shapes=[
            pltpu.VMEM((crop // 128, line_rows, 128) if direct else (1, 8, 128), F32),
        ],
        compiler_params=pltpu.CompilerParams(vmem_limit_bytes=56 * 2**20),
        cost_estimate=pl.CostEstimate(
            flops=6 * positions * channels * (8 * width + 2 * lanes),
            bytes_accessed=positions * (3 * channels + lanes) * 2,
            transcendentals=positions * width,
        ),
        name="pair_backward",
    )(*operands)


def attend_kernel(
    first, last, weight_ref, bias_ref, valid_ref, q_ref, k_ref, v_ref, g_ref, *refs
):
    if first:
        dq_ref, dk_ref, dv_ref, d_bias_ref = refs
    else:
        dk_before_ref, dv_before_ref, dq_ref, dk_ref, dv_ref, d_bias_ref = refs
    samples, depth = q_ref.shape[1:3]
    sources, _, rows, crop = bias_ref.shape
    scaling = 1.0 / math.sqrt(depth)
    bias = bias_ref[:, 0].astype(F32).reshape(sources * rows, crop)
    valid = valid_ref[...] > 0
    total = jnp.zeros_like(bias)
    for s in range(samples):
        query, key, value = q_ref[0, s], k_ref[0, s], v_ref[0, s]
        grad_half = (weight_ref[s] * g_ref[0, s].astype(F32)).astype(BF16)
        scores = mm(query, key, 0, 0) * scaling + bias
        scores = jnp.where(valid, scores, masked_score)
        exp_scores = jnp.exp(scores - jnp.max(scores, -1, keepdims=True))
        attention = exp_scores / jnp.sum(exp_scores, -1, keepdims=True)
        d_attention = mm(grad_half, value, 0, 0)
        d_scores = attention * (
            d_attention - jnp.sum(attention * d_attention, -1, keepdims=True)
        )
        total = total + d_scores
        scores_half = d_scores.astype(BF16)
        d_value = mm(grad_half, attention.astype(BF16))
        d_key = mm(query, scores_half)
        dq_ref[0, s] = (mm(key, scores_half, 1, 1) * scaling).astype(BF16)
        if not first:
            d_value = d_value + dv_before_ref[0, s]
            d_key = d_key + dk_before_ref[0, s]
        if last:
            d_key = d_key * scaling
        dv_ref[0, s] = d_value.astype(dv_ref.dtype)
        dk_ref[0, s] = d_key.astype(dk_ref.dtype)
    d_bias_ref[:, 0] = total.astype(BF16).reshape(sources, rows, crop)


def attend_rows(first, last, weights, bias, valid, query, key, value, grad, state):
    sources, layers, rows, crop = bias.shape
    samples, depth, row_count = query.shape[1:]
    vec = lambda shape: pl.BlockSpec((1,) + shape[1:], lambda l: (l, 0, 0, 0))
    plane = pl.BlockSpec((sources, 1, rows, crop), lambda l: (0, l, 0, 0))
    in_specs = [
        pl.BlockSpec(memory_space=pltpu.SMEM),
        plane,
        pl.BlockSpec(valid.shape, lambda l: (0, 0)),
        vec(query.shape),
        vec(key.shape),
        vec(value.shape),
        vec(grad.shape),
    ]
    operands = [weights, bias, valid, query, key, value, grad]
    if not first:
        operands += list(state)
        in_specs += [vec(key.shape), vec(value.shape)]
    kind = BF16 if last else F32
    return pl.pallas_call(
        functools.partial(attend_kernel, first, last),
        grid=(layers,),
        in_specs=in_specs,
        out_specs=[vec(query.shape), vec(key.shape), vec(value.shape), plane],
        out_shape=[
            jax.ShapeDtypeStruct(query.shape, BF16),
            jax.ShapeDtypeStruct(key.shape, kind),
            jax.ShapeDtypeStruct(value.shape, kind),
            jax.ShapeDtypeStruct(bias.shape, BF16),
        ],
        compiler_params=pltpu.CompilerParams(vmem_limit_bytes=48 * 2**20),
        cost_estimate=pl.CostEstimate(
            flops=200 * layers * samples * depth * row_count * crop,
            bytes_accessed=layers * crop * (4 * row_count + 12 * samples * depth),
            transcendentals=layers * samples * row_count * crop,
        ),
        name="attention_backward",
    )(*operands)


def swap(array, teams=None):
    return lax.all_to_all(
        array, "tok", split_axis=0, concat_axis=0, tiled=True, axis_index_groups=teams
    )


def sum_pairs(keep, send):
    across = [(index, index ^ 1) for index in range(lax.axis_size("tok"))]
    return (keep + lax.ppermute(send, "tok", across).astype(F32)).astype(BF16)


def sum_team(array):
    devices = lax.axis_size("tok")
    teams = [list(range(odd, devices, 2)) for odd in range(2)]
    members = devices // 2
    parts = swap(array.reshape(members, array.shape[0] // members, array.shape[1]), teams)
    return jnp.sum(parts.astype(F32), 0).astype(BF16)


def finish_kernel(parity_ref, mine_ref, theirs_ref, in_ref, out_ref, bias_ref):
    mine, theirs = mine_ref[...].astype(F32), theirs_ref[...].astype(F32)
    even = parity_ref[0] == 0
    summed = jnp.concatenate([jnp.where(even, mine, theirs), jnp.where(even, theirs, mine)], 0)
    done = in_ref.shape[1]
    in_ref[...] = summed[:done].T
    out_ref[...] = summed[done : done + out_ref.shape[0]]
    done += out_ref.shape[0]
    bias_ref[...] = summed[done : done + bias_ref.shape[0]]


def gather_sums(share, parity, width, lanes):
    devices = lax.axis_size("tok")
    members = devices // 2
    channels = share.shape[1]
    across = [(index, index ^ 1) for index in range(devices)]
    teams = [list(range(odd, devices, 2)) for odd in range(2)]
    mine = swap(jnp.broadcast_to(share[None], (members,) + share.shape), teams)
    mine = mine.reshape(members * share.shape[0], channels)
    theirs = lax.ppermute(mine, "tok", across)
    return pl.pallas_call(
        finish_kernel,
        in_specs=[
            pl.BlockSpec(memory_space=pltpu.SMEM),
            pl.BlockSpec(memory_space=pltpu.VMEM),
            pl.BlockSpec(memory_space=pltpu.VMEM),
        ],
        out_shape=[
            jax.ShapeDtypeStruct((channels, 2 * width), F32),
            jax.ShapeDtypeStruct((width, channels), F32),
            jax.ShapeDtypeStruct((lanes, channels), F32),
        ],
        compiler_params=pltpu.CompilerParams(vmem_limit_bytes=32 * 2**20),
        name="weight_grads",
    )(parity, mine, theirs)


def body(
    pair_states,
    weight_in,
    weight_out,
    weight_bias,
    key_mask,
    noise_level,
    query_states,
    key_states,
    value_states,
    output_grad,
):
    row_count, crop, channels = pair_states.shape
    layers, _, heads = weight_bias.shape
    width = weight_out.shape[0]
    devices = lax.axis_size("tok")
    groups = devices // heads
    samples, depth = query_states.shape[2:4]
    lanes = heads * layers
    sizes = [row_count]
    if row_count % 16 == 0:
        sizes = [row_count // 2] * 2
    w_bias = jnp.transpose(weight_bias, (0, 2, 1))

    group = lax.axis_index("tok") // heads
    weights = sample_weight(lax.dynamic_slice_in_dim(noise_level, group * samples, samples))
    valid = key_mask[None, :]

    def by_chunk(array):
        cut = array[:, 0].reshape(layers, samples, depth, devices, len(sizes), sizes[0])
        cut = jnp.transpose(cut, (4, 0, 1, 2, 3, 5))
        return cut.reshape(len(sizes), layers, samples, depth, devices * sizes[0])

    queries, grads = by_chunk(query_states), by_chunk(output_grad)

    sum_rows = 3 * width + lanes
    padded_rows = 8 * devices * -(-sum_rows // (8 * devices))
    parity = (lax.axis_index("tok") % 2).astype(jnp.int32).reshape(1)
    piece = split_width(width)
    two = jnp.asarray(2.0, BF16)
    columns = []
    for at in range(0, width, piece):
        columns.append(weight_in[:, at : at + piece])
        columns.append(weight_in[:, width + at : width + at + piece] * two)
    scaled = (jnp.concatenate(columns, 1), weight_out * jnp.asarray(0.5, BF16))
    rows = sizes[0]
    direct = is_direct(rows, crop)

    def forward(start, count, prepared):
        return forward_rows(start, count, pair_states, weight_in, weight_out, w_bias, prepared)

    def send_bias(bias):
        if direct:
            bias = bias.reshape(heads, layers, rows, crop)
        else:
            bias = jnp.transpose(bias.reshape(rows, layers, heads, crop), (2, 1, 0, 3))
        if groups > 1:
            bias = jnp.tile(bias, (groups, 1, 1, 1))
        return swap(bias)

    def attend(start, bias, state):
        if not direct:
            bias = jnp.transpose(bias, (1, 0, 2, 3)).reshape(1, layers, devices * rows, crop)
        *grads_made, d_bias = attend_rows(
            start == 0,
            start + rows == row_count,
            weights,
            bias,
            valid,
            queries[start // rows],
            key_states[:, 0],
            value_states[:, 0],
            grads[start // rows],
            state,
        )
        if not direct:
            d_bias = jnp.transpose(d_bias.reshape(layers, devices, rows, crop), (1, 0, 2, 3))
        return grads_made, d_bias

    def send_back(d_bias):
        d_bias = swap(d_bias)
        if groups > 1:
            d_bias = d_bias.reshape(groups, heads, layers, rows, crop).astype(F32)
            d_bias = jnp.sum(d_bias, 0).astype(BF16)
        if direct:
            return d_bias.reshape(lanes, rows, crop)
        return jnp.transpose(d_bias, (2, 1, 0, 3)).reshape(rows, lanes, crop)

    def backward(start, count, stored, d_bias, prepared, state):
        weights_used = (prepared[0], *scaled)
        return backward_rows(
            start,
            count,
            direct,
            padded_rows,
            pair_states.shape,
            stored,
            d_bias,
            w_bias,
            weights_used,
            state,
            parity,
        )

    bias, *kept, w_in_t, w_out_t = forward(0, rows, None)
    prepared = (w_in_t, w_out_t)
    arrived, stored = [send_bias(bias)], [kept]
    for start in range(rows, row_count, rows):
        bias, *kept = forward(start, rows, prepared)
        arrived.append(send_bias(bias))
        stored.append(kept)
    d_queries, returned = [], []
    state = None
    for start, bias in zip(range(0, row_count, rows), arrived):
        (d_query, *state), d_bias = attend(start, bias, state)
        d_queries.append(d_query)
        returned.append(send_back(d_bias))
    d_key, d_value = state
    state = None
    for start, kept, d_bias in zip(range(0, row_count, rows), stored, returned):
        state = backward(start, rows, kept, d_bias, prepared, state)
    pair_grad, _, keep, send = state

    share = sum_team(sum_pairs(keep, send))
    grad_in, grad_out, grad_bias = gather_sums(share, parity, width, lanes)
    grad_bias = jnp.transpose(grad_bias.reshape(layers, heads, channels), (0, 2, 1))

    d_queries = [part.reshape(layers, samples, depth, devices, rows) for part in d_queries]
    d_query = jnp.concatenate(d_queries, -1).reshape(query_states.shape)
    return (
        pair_grad,
        d_query,
        d_key[:, None],
        d_value[:, None],
        grad_in,
        grad_out,
        grad_bias,
    )


def solution(mesh):
    in_specs = (
        P(("job", "tok"), None, None),
        P(),
        P(),
        P(),
        P("job"),
        P("job"),
        P(None, "tok", "job", None, None),
        P(None, "tok", "job", None, None),
        P(None, "tok", "job", None, None),
        P(None, "tok", "job", None, None),
    )
    out_specs = (
        P(("job", "tok"), None, None),
        P(None, "tok", "job", None, None),
        P(None, "tok", "job", None, None),
        P(None, "tok", "job", None, None),
        P("job", None),
        P("job", None),
        P("job", None, None),
    )
    return jax.shard_map(body, mesh=mesh, in_specs=in_specs, out_specs=out_specs, check_vma=False)
```

```python
import functools
import math

import jax
import jax.numpy as jnp
from jax import lax
from jax.experimental import pallas as pl
from jax.experimental.pallas import tpu as pltpu
from jax.sharding import PartitionSpec as P

LEVELS = 200


sigma_high = 160.0
sigma_low = 0.0004
sigma_data = 16.0
rho_power = 7.0
epsilon = 1e-05
masked_score = -1000000000.0

F32 = jnp.float32
BF16 = jnp.bfloat16


def sample_weight(levels):
    level = levels.astype(jnp.float32)
    top_root = sigma_high ** (1.0 / rho_power)
    low_root = sigma_low ** (1.0 / rho_power)
    sigma_level = (top_root + level / (LEVELS - 1) * (low_root - top_root)) ** rho_power
    return (sigma_level * sigma_level + sigma_data * sigma_data) / (sigma_level + sigma_data) ** 2


def mm(left, right, left_dim=1, right_dim=0):
    return lax.dot_general(
        left, right, (((left_dim,), (right_dim,)), ((), ())), preferred_element_type=F32
    )


def normalize(inputs):
    centered = inputs - jnp.mean(inputs, 0, keepdims=True)
    inv_std = lax.rsqrt(jnp.mean(centered * centered, 0, keepdims=True) + epsilon)
    return centered * inv_std, inv_std


def norm_back(normed, inv_std, upstream):
    return inv_std * (
        upstream
        - jnp.mean(upstream, 0, keepdims=True)
        - normed * jnp.mean(upstream * normed, 0, keepdims=True)
    )


def split_width(width):
    return 512 if width % 512 == 0 else width


def interleave(make_stages, count, lag):
    rows = [make_stages(index) for index in range(count)]
    running = []
    clock = 0
    while rows or running:
        while rows and clock >= lag * (count - len(rows)):
            running.append(rows.pop(0))
        running = [row for row in running if next(row, None) is not None]
        clock += 1


def for_groups(count, group, one_group):
    group = math.gcd(count, group)

    def step(at, carry):
        one_group(at * group, group)
        return carry

    if count == group:
        step(0, 0)
    else:
        lax.fori_loop(0, count // group, step, 0)


def row_step(rows):
    return math.gcd(rows, 8 if rows > 8 else 4)


def is_direct(rows, crop):
    return rows % 8 == 0 and crop % 128 == 0


def forward_kernel(direct, first, pair_ref, w_bias_ref, *refs):
    refs = list(refs)
    if first:
        w_in_ref, w_out_ref = refs.pop(0), refs.pop(0)
    else:
        w_in_t_ref, w_out_t_ref = refs.pop(0), refs.pop(0)
    bias_ref, normed_ref, inv_ref = refs.pop(0), refs.pop(0), refs.pop(0)
    if first:
        w_in_t_ref, w_out_t_ref = refs.pop(0), refs.pop(0)
    lines_ref = refs.pop(0)
    width = w_out_t_ref.shape[1]
    layers, heads, channels = w_bias_ref.shape
    piece = split_width(width)
    step = pair_ref.shape[0]
    first_row = pl.program_id(0) * step

    if first:

        @pl.when(pl.program_id(0) == 0)
        def _():
            w_in_t = w_in_ref[...].T
            w_in_t_ref[:width, :] = w_in_t[:width] * 0.5
            w_in_t_ref[width:, :] = w_in_t[width:]
            w_out_t_ref[...] = w_out_ref[...].T

    def stages(row):
        pair_float = pair_ref[row].T.astype(F32)
        normed_float, inv_in = normalize(pair_float)
        normed_in = normed_float.astype(BF16)
        normed_ref[row, :channels, :] = normed_in
        inv_ref[row, 0:1, :] = inv_in
        yield True
        hiddens = []
        for at in range(0, width, piece):
            half_gate = mm(w_in_t_ref[at : at + piece, :], normed_in)
            up_in = mm(w_in_t_ref[width + at : width + at + piece, :], normed_in)
            yield True
            hidden = half_gate * (1.0 + jnp.tanh(half_gate)) * up_in
            hiddens.append(hidden.astype(BF16))
            yield True
        lifted = pair_float + mm(w_out_t_ref[...], jnp.concatenate(hiddens, 0))
        yield True
        normed_float, inv_out = normalize(lifted)
        normed_out = normed_float.astype(BF16)
        normed_ref[row, channels:, :] = normed_out
        inv_ref[row, 1:2, :] = inv_out
        yield True
        bias = mm(w_bias_ref[...].reshape(layers * heads, channels), normed_out)
        if direct:
            tiles, total, tile = lines_ref.shape
            rows = total // (layers * heads)
            for layer in range(layers):
                at = pl.ds(layer * rows + first_row + row, heads, stride=layers * rows)
                lines = bias[layer * heads : (layer + 1) * heads]
                for index in range(tiles):
                    lines_ref[index, at, :] = lines[:, index * tile : (index + 1) * tile]
        else:
            bias_ref[row] = bias.astype(BF16)

    for_groups(step, 8, lambda at, count: interleave(lambda i: stages(at + i), count, 0))

    if direct:

        @pl.when(pl.program_id(0) == pl.num_programs(0) - 1)
        def _():
            tiles, _, tile = lines_ref.shape
            for index in range(tiles):
                lines = lines_ref[index].reshape(bias_ref.shape[:2] + (tile,))
                bias_ref[:, :, index * tile : (index + 1) * tile] = lines.astype(BF16)


def whole_spec(array):
    return pl.BlockSpec(array.shape, lambda i: (0,) * len(array.shape))


def forward_rows(start, rows, pair, w_in, w_out, w_bias, prepared):
    crop, channels = pair.shape[1:]
    layers, heads, _ = w_bias.shape
    lanes = layers * heads
    step = row_step(rows)
    first_step = start // step
    positions = rows * crop
    width = w_out.shape[0]
    direct = is_direct(rows, crop)
    first = prepared is None
    line_shape = (lanes, rows, crop) if direct else (rows, lanes, crop)
    shapes = [jax.ShapeDtypeStruct(line_shape, BF16)]
    out_specs = [
        whole_spec(shapes[0])
        if direct
        else pl.BlockSpec((step, lanes, crop), lambda i: (i, 0, 0))
    ]
    for height, kind in ((2 * channels, BF16), (2, F32)):
        shapes.append(jax.ShapeDtypeStruct((rows, height, crop), kind))
        out_specs.append(pl.BlockSpec((step, height, crop), lambda i: (i, 0, 0)))
    operands = [pair, w_bias, *((w_in, w_out) if first else prepared)]
    if first:
        for shape in (w_in.shape[::-1], w_out.shape[::-1]):
            shapes.append(jax.ShapeDtypeStruct(shape, BF16))
            out_specs.append(whole_spec(shapes[-1]))
    return pl.pallas_call(
        functools.partial(forward_kernel, direct, first),
        grid=(rows // step,),
        in_specs=[pl.BlockSpec((step, crop, channels), lambda i: (first_step + i, 0, 0))]
        + [whole_spec(array) for array in operands[1:]],
        out_specs=out_specs,
        out_shape=shapes,
        scratch_shapes=[
            pltpu.VMEM((crop // 128, lanes * rows, 128) if direct else (1, 8, 128), F32),
        ],
        compiler_params=pltpu.CompilerParams(vmem_limit_bytes=56 * 2**20),
        cost_estimate=pl.CostEstimate(
            flops=6 * positions * channels * (3 * width + lanes),
            bytes_accessed=positions * (channels + lanes) * 2,
            transcendentals=positions * width,
        ),
        name="pair_forward",
    )(*operands)


def backward_kernel(
    first,
    last,
    direct,
    normed_ref,
    inv_ref,
    d_bias_ref,
    w_bias_ref,
    w_in_t_ref,
    w_back_ref,
    w_half_ref,
    *refs,
):
    outs = list(refs[:-1])
    parity_ref = outs.pop(0) if last else None
    if not first:
        before_ref = outs.pop(0)
        outs.pop(0)
    pair_grad_ref, sums_ref = outs.pop(0), outs.pop(0)
    lines_ref = refs[-1]
    width = w_half_ref.shape[0]
    layers, heads, channels = w_bias_ref.shape
    lanes = layers * heads
    piece = split_width(width)
    step = normed_ref.shape[0]
    one, two = jnp.asarray(1.0, BF16), jnp.asarray(2.0, BF16)
    first_row = pl.program_id(0) * step

    @pl.when(pl.program_id(0) == 0)
    def _():
        if first:
            sums_ref[...] = jnp.zeros_like(sums_ref)
        else:
            sums_ref[...] = before_ref[...]
        if direct:
            tiles, total, tile = lines_ref.shape
            for index in range(tiles):
                lines = d_bias_ref[:, :, index * tile : (index + 1) * tile].astype(F32)
                lines_ref[index] = lines.reshape(total, tile)

    def read_lines(row):
        if not direct:
            return d_bias_ref[row]
        tiles, total, _ = lines_ref.shape
        rows = total // lanes
        found = []
        for layer in range(layers):
            at = pl.ds(layer * rows + first_row + row, heads, stride=layers * rows)
            found.append(jnp.concatenate([lines_ref[index, at, :] for index in range(tiles)], 1))
        return jnp.concatenate(found, 0).astype(BF16)

    def add_sums(at, left, right):
        sums_ref[at : at + left.shape[0], :] += mm(left, right, 1, 1)

    def stages(row):
        normed_in, normed_out = normed_ref[row, :channels, :], normed_ref[row, channels:, :]
        inv_in, inv_out = inv_ref[row, 0:1, :], inv_ref[row, 1:2, :]
        kept = []
        for at in range(0, width, piece):
            half_gate = mm(w_in_t_ref[at : at + piece, :], normed_in)
            up_in = mm(w_in_t_ref[width + at : width + at + piece, :], normed_in)
            yield True
            one_plus = (1.0 + jnp.tanh(half_gate)).astype(BF16)
            half_gate, up_in = half_gate.astype(BF16), up_in.astype(BF16)
            silu = half_gate * one_plus
            hidden = silu * up_in
            slope = one_plus * (one + half_gate * (two - one_plus)) * up_in
            kept.append((silu, slope, hidden))
            yield True
        d_bias = read_lines(row)
        d_normed = mm(w_bias_ref[...].reshape(lanes, channels), d_bias, 0, 0)
        add_sums(3 * width, d_bias, normed_out)
        d_lifted = norm_back(normed_out.astype(F32), inv_out, d_normed)
        lifted_half = d_lifted.astype(BF16)
        yield True
        d_normed_in = None
        for index, (silu, slope, hidden) in enumerate(kept):
            at = index * piece
            d_hidden = mm(w_half_ref[at : at + piece, :], lifted_half).astype(BF16)
            add_sums(2 * width + at, hidden, lifted_half)
            yield True
            d_both = jnp.concatenate([d_hidden * slope, d_hidden * silu], 0)
            add_sums(2 * at, d_both, normed_in)
            part = mm(w_back_ref[:, 2 * at : 2 * at + 2 * piece], d_both)
            d_normed_in = part if d_normed_in is None else d_normed_in + part
            yield True
        pair_grad = d_lifted + norm_back(normed_in.astype(F32), inv_in, d_normed_in)
        pair_grad_ref[row] = pair_grad.astype(BF16).T

    for_groups(step, 8, lambda at, count: interleave(lambda i: stages(at + i), count, 0))

    if last:
        keep_ref, send_ref = outs

        @pl.when(pl.program_id(0) == pl.num_programs(0) - 1)
        def _():
            half = sums_ref.shape[0] // 2
            parity = parity_ref[0]
            gates, ups = [], []
            for at in range(0, 2 * width, 2 * piece):
                gates.append(sums_ref[at : at + piece, :])
                ups.append(2.0 * sums_ref[at + piece : at + 2 * piece, :])
            sums_ref[: 2 * width, :] = jnp.concatenate(gates + ups, 0)
            keep_ref[...] = sums_ref[pl.ds(pl.multiple_of(parity * half, 8), half), :]
            other = pl.ds(pl.multiple_of((1 - parity) * half, 8), half)
            send_ref[...] = sums_ref[other, :].astype(BF16)


def backward_rows(
    start, rows, direct, sum_rows, shape, stored, d_bias, w_bias, prepared, state, parity
):
    crop, channels = shape[1:]
    layers, heads, _ = w_bias.shape
    lanes = layers * heads
    width = prepared[2].shape[0]
    step = row_step(rows)
    first_step = start // step
    positions = rows * crop
    first, last = start == 0, start + rows == shape[0]
    pair_spec = pl.BlockSpec((step, crop, channels), lambda i: (first_step + i, 0, 0))
    line_spec = whole_spec(d_bias) if direct else pl.BlockSpec((step, lanes, crop), lambda i: (i, 0, 0))
    operands = [*stored, d_bias, w_bias, *prepared]
    in_specs = [
        pl.BlockSpec((step,) + array.shape[1:], lambda i: (i, 0, 0)) for array in stored
    ]
    in_specs += [line_spec] + [whole_spec(array) for array in operands[len(stored) + 1 :]]
    aliases = {}
    if last:
        operands.append(parity)
        in_specs.append(pl.BlockSpec(memory_space=pltpu.SMEM))
    if not first:
        pair_grad, sums = state
        operands += [sums, pair_grad]
        in_specs += [whole_spec(sums), pl.BlockSpec(memory_space=pl.ANY)]
        aliases = {len(operands) - 1: 0}
    shapes = [
        jax.ShapeDtypeStruct(shape, BF16),
        jax.ShapeDtypeStruct((sum_rows, channels), F32),
    ]
    if last:
        shapes.append(jax.ShapeDtypeStruct((sum_rows // 2, channels), F32))
        shapes.append(jax.ShapeDtypeStruct((sum_rows // 2, channels), BF16))
    out_specs = [pair_spec] + [whole_spec(shape) for shape in shapes[1:]]
    line_rows = lanes * d_bias.shape[1]
    return pl.pallas_call(
        functools.partial(backward_kernel, first, last, direct),
        grid=(rows // step,),
        in_specs=in_specs,
        out_specs=out_specs,
        out_shape=shapes,
        input_output_aliases=aliases,
        scratch_shapes=[
            pltpu.VMEM((crop // 128, line_rows, 128) if direct else (1, 8, 128), F32),
        ],
        compiler_params=pltpu.CompilerParams(vmem_limit_bytes=56 * 2**20),
        cost_estimate=pl.CostEstimate(
            flops=6 * positions * channels * (8 * width + 2 * lanes),
            bytes_accessed=positions * (3 * channels + lanes) * 2,
            transcendentals=positions * width,
        ),
        name="pair_backward",
    )(*operands)


def attend_kernel(
    first, last, weight_ref, bias_ref, valid_ref, q_ref, k_ref, v_ref, g_ref, *refs
):
    if first:
        dq_ref, dk_ref, dv_ref, d_bias_ref = refs
    else:
        dk_before_ref, dv_before_ref, dq_ref, dk_ref, dv_ref, d_bias_ref = refs
    samples, depth = q_ref.shape[1:3]
    sources, _, rows, crop = bias_ref.shape
    scaling = 1.0 / math.sqrt(depth)
    bias = bias_ref[:, 0].astype(F32).reshape(sources * rows, crop)
    valid = valid_ref[...] > 0
    total = jnp.zeros_like(bias)
    for s in range(samples):
        query, key, value = q_ref[0, s], k_ref[0, s], v_ref[0, s]
        grad_half = (weight_ref[s] * g_ref[0, s].astype(F32)).astype(BF16)
        scores = mm(query, key, 0, 0) * scaling + bias
        scores = jnp.where(valid, scores, masked_score)
        exp_scores = jnp.exp(scores - jnp.max(scores, -1, keepdims=True))
        attention = exp_scores / jnp.sum(exp_scores, -1, keepdims=True)
        d_attention = mm(grad_half, value, 0, 0)
        d_scores = attention * (
            d_attention - jnp.sum(attention * d_attention, -1, keepdims=True)
        )
        total = total + d_scores
        scores_half = d_scores.astype(BF16)
        d_value = mm(grad_half, attention.astype(BF16))
        d_key = mm(query, scores_half)
        dq_ref[0, s] = (mm(key, scores_half, 1, 1) * scaling).astype(BF16)
        if not first:
            d_value = d_value + dv_before_ref[0, s]
            d_key = d_key + dk_before_ref[0, s]
        if last:
            d_key = d_key * scaling
        dv_ref[0, s] = d_value.astype(dv_ref.dtype)
        dk_ref[0, s] = d_key.astype(dk_ref.dtype)
    d_bias_ref[:, 0] = total.astype(BF16).reshape(sources, rows, crop)


def attend_rows(first, last, weights, bias, valid, query, key, value, grad, state):
    sources, layers, rows, crop = bias.shape
    samples, depth, row_count = query.shape[1:]
    vec = lambda shape: pl.BlockSpec((1,) + shape[1:], lambda l: (l, 0, 0, 0))
    plane = pl.BlockSpec((sources, 1, rows, crop), lambda l: (0, l, 0, 0))
    in_specs = [
        pl.BlockSpec(memory_space=pltpu.SMEM),
        plane,
        pl.BlockSpec(valid.shape, lambda l: (0, 0)),
        vec(query.shape),
        vec(key.shape),
        vec(value.shape),
        vec(grad.shape),
    ]
    operands = [weights, bias, valid, query, key, value, grad]
    if not first:
        operands += list(state)
        in_specs += [vec(key.shape), vec(value.shape)]
    kind = BF16 if last else F32
    return pl.pallas_call(
        functools.partial(attend_kernel, first, last),
        grid=(layers,),
        in_specs=in_specs,
        out_specs=[vec(query.shape), vec(key.shape), vec(value.shape), plane],
        out_shape=[
            jax.ShapeDtypeStruct(query.shape, BF16),
            jax.ShapeDtypeStruct(key.shape, kind),
            jax.ShapeDtypeStruct(value.shape, kind),
            jax.ShapeDtypeStruct(bias.shape, BF16),
        ],
        compiler_params=pltpu.CompilerParams(vmem_limit_bytes=48 * 2**20),
        cost_estimate=pl.CostEstimate(
            flops=200 * layers * samples * depth * row_count * crop,
            bytes_accessed=layers * crop * (4 * row_count + 12 * samples * depth),
            transcendentals=layers * samples * row_count * crop,
        ),
        name="attention_backward",
    )(*operands)


def swap(array, teams=None):
    return lax.all_to_all(
        array, "tok", split_axis=0, concat_axis=0, tiled=True, axis_index_groups=teams
    )


def sum_pairs(keep, send):
    across = [(index, index ^ 1) for index in range(lax.axis_size("tok"))]
    return (keep + lax.ppermute(send, "tok", across).astype(F32)).astype(BF16)


def sum_team(array):
    devices = lax.axis_size("tok")
    teams = [list(range(odd, devices, 2)) for odd in range(2)]
    members = devices // 2
    parts = swap(array.reshape(members, array.shape[0] // members, array.shape[1]), teams)
    return jnp.sum(parts.astype(F32), 0).astype(BF16)


def finish_kernel(parity_ref, mine_ref, theirs_ref, in_ref, out_ref, bias_ref):
    mine, theirs = mine_ref[...].astype(F32), theirs_ref[...].astype(F32)
    even = parity_ref[0] == 0
    summed = jnp.concatenate([jnp.where(even, mine, theirs), jnp.where(even, theirs, mine)], 0)
    done = in_ref.shape[1]
    in_ref[...] = summed[:done].T
    out_ref[...] = summed[done : done + out_ref.shape[0]]
    done += out_ref.shape[0]
    bias_ref[...] = summed[done : done + bias_ref.shape[0]]


def gather_sums(share, parity, width, lanes):
    devices = lax.axis_size("tok")
    members = devices // 2
    channels = share.shape[1]
    across = [(index, index ^ 1) for index in range(devices)]
    teams = [list(range(odd, devices, 2)) for odd in range(2)]
    mine = swap(jnp.broadcast_to(share[None], (members,) + share.shape), teams)
    mine = mine.reshape(members * share.shape[0], channels)
    theirs = lax.ppermute(mine, "tok", across)
    return pl.pallas_call(
        finish_kernel,
        in_specs=[
            pl.BlockSpec(memory_space=pltpu.SMEM),
            pl.BlockSpec(memory_space=pltpu.VMEM),
            pl.BlockSpec(memory_space=pltpu.VMEM),
        ],
        out_shape=[
            jax.ShapeDtypeStruct((channels, 2 * width), F32),
            jax.ShapeDtypeStruct((width, channels), F32),
            jax.ShapeDtypeStruct((lanes, channels), F32),
        ],
        compiler_params=pltpu.CompilerParams(vmem_limit_bytes=32 * 2**20),
        name="weight_grads",
    )(parity, mine, theirs)


def body(
    pair_states,
    weight_in,
    weight_out,
    weight_bias,
    key_mask,
    noise_level,
    query_states,
    key_states,
    value_states,
    output_grad,
):
    row_count, crop, channels = pair_states.shape
    layers, _, heads = weight_bias.shape
    width = weight_out.shape[0]
    devices = lax.axis_size("tok")
    groups = devices // heads
    samples, depth = query_states.shape[2:4]
    lanes = heads * layers
    sizes = [row_count]
    if row_count % 16 == 0:
        sizes = [row_count // 2] * 2
    w_bias = jnp.transpose(weight_bias, (0, 2, 1))

    group = lax.axis_index("tok") // heads
    weights = sample_weight(lax.dynamic_slice_in_dim(noise_level, group * samples, samples))
    valid = key_mask[None, :]

    def by_chunk(array):
        cut = array[:, 0].reshape(layers, samples, depth, devices, len(sizes), sizes[0])
        cut = jnp.transpose(cut, (4, 0, 1, 2, 3, 5))
        return cut.reshape(len(sizes), layers, samples, depth, devices * sizes[0])

    queries, grads = by_chunk(query_states), by_chunk(output_grad)

    sum_rows = 3 * width + lanes
    padded_rows = 8 * devices * -(-sum_rows // (8 * devices))
    parity = (lax.axis_index("tok") % 2).astype(jnp.int32).reshape(1)
    piece = split_width(width)
    two = jnp.asarray(2.0, BF16)
    columns = []
    for at in range(0, width, piece):
        columns.append(weight_in[:, at : at + piece])
        columns.append(weight_in[:, width + at : width + at + piece] * two)
    scaled = (jnp.concatenate(columns, 1), weight_out * jnp.asarray(0.5, BF16))
    rows = sizes[0]
    direct = is_direct(rows, crop)

    def forward(start, count, prepared):
        return forward_rows(start, count, pair_states, weight_in, weight_out, w_bias, prepared)

    def send_bias(bias):
        if direct:
            bias = bias.reshape(heads, layers, rows, crop)
        else:
            bias = jnp.transpose(bias.reshape(rows, layers, heads, crop), (2, 1, 0, 3))
        if groups > 1:
            bias = jnp.tile(bias, (groups, 1, 1, 1))
        return swap(bias)

    def attend(start, bias, state):
        if not direct:
            bias = jnp.transpose(bias, (1, 0, 2, 3)).reshape(1, layers, devices * rows, crop)
        *grads_made, d_bias = attend_rows(
            start == 0,
            start + rows == row_count,
            weights,
            bias,
            valid,
            queries[start // rows],
            key_states[:, 0],
            value_states[:, 0],
            grads[start // rows],
            state,
        )
        if not direct:
            d_bias = jnp.transpose(d_bias.reshape(layers, devices, rows, crop), (1, 0, 2, 3))
        return grads_made, d_bias

    def send_back(d_bias):
        d_bias = swap(d_bias)
        if groups > 1:
            d_bias = d_bias.reshape(groups, heads, layers, rows, crop).astype(F32)
            d_bias = jnp.sum(d_bias, 0).astype(BF16)
        if direct:
            return d_bias.reshape(lanes, rows, crop)
        return jnp.transpose(d_bias, (2, 1, 0, 3)).reshape(rows, lanes, crop)

    def backward(start, count, stored, d_bias, prepared, state):
        weights_used = (prepared[0], *scaled)
        return backward_rows(
            start,
            count,
            direct,
            padded_rows,
            pair_states.shape,
            stored,
            d_bias,
            w_bias,
            weights_used,
            state,
            parity,
        )

    bias, *kept, w_in_t, w_out_t = forward(0, rows, None)
    prepared = (w_in_t, w_out_t)
    arrived, stored = [send_bias(bias)], [kept]
    for start in range(rows, row_count, rows):
        bias, *kept = forward(start, rows, prepared)
        arrived.append(send_bias(bias))
        stored.append(kept)
    d_queries, returned = [], []
    state = None
    for start, bias in zip(range(0, row_count, rows), arrived):
        (d_query, *state), d_bias = attend(start, bias, state)
        d_queries.append(d_query)
        returned.append(send_back(d_bias))
    d_key, d_value = state
    state = None
    for start, kept, d_bias in zip(range(0, row_count, rows), stored, returned):
        state = backward(start, rows, kept, d_bias, prepared, state)
    pair_grad, _, keep, send = state

    share = sum_team(sum_pairs(keep, send))
    grad_in, grad_out, grad_bias = gather_sums(share, parity, width, lanes)
    grad_bias = jnp.transpose(grad_bias.reshape(layers, heads, channels), (0, 2, 1))

    d_queries = [part.reshape(layers, samples, depth, devices, rows) for part in d_queries]
    d_query = jnp.concatenate(d_queries, -1).reshape(query_states.shape)
    return (
        pair_grad,
        d_query,
        d_key[:, None],
        d_value[:, None],
        grad_in,
        grad_out,
        grad_bias,
    )


def solution(mesh):
    in_specs = (
        P(("job", "tok"), None, None),
        P(),
        P(),
        P(),
        P("job"),
        P("job"),
        P(None, "tok", "job", None, None),
        P(None, "tok", "job", None, None),
        P(None, "tok", "job", None, None),
        P(None, "tok", "job", None, None),
    )
    out_specs = (
        P(("job", "tok"), None, None),
        P(None, "tok", "job", None, None),
        P(None, "tok", "job", None, None),
        P(None, "tok", "job", None, None),
        P("job", None),
        P("job", None),
        P("job", None, None),
    )
    return jax.shard_map(body, mesh=mesh, in_specs=in_specs, out_specs=out_specs, check_vma=False)
```
